512 devices in a mesh: row: 64 (over z_lo, y, core), col: 8 (over z_hi, x).
Axes of the slice: x: 4, y: 8, z: 8 (z_hi: 2, z_lo: 4; z = z_hi * 4 + z_lo), core: 2. Of those that a mesh axis runs over, the one named last changes fastest.
Arguments:
- query: bfloat16 [32768, 2560], P(('row', 'col')), may hold values from -6 to 6
- key: bfloat16 [32768, 2560], P(('row', 'col')), may hold values from -6 to 6
- value: bfloat16 [32768, 2560], P(('row', 'col')), may hold values from -6 to 6
- saved_out: bfloat16 [32768, 2560], P(('row', 'col')), may hold values from -6 to 6
- grad_out: bfloat16 [32768, 2560], P(('row', 'col')), may hold values from -6 to 6
- frame_ids: int32 [32768], P(('row', 'col')), may hold values from 0 to 15, never falling along the last dimension, each value on 1 to 4096 neighbouring positions
Outputs:
- grad_query: bfloat16 [32768, 2560], P(('row', 'col'))
- grad_key: bfloat16 [32768, 2560], P(('row', 'col'))
- grad_value: bfloat16 [32768, 2560], P(('row', 'col'))
The draws below stay inside these ranges and needn't reach their ends.
Inputs may be any that keep to these rules, and one draw needn't show every extreme that they name: `frame_ids`: never falls along the tokens; every frame 0 to 15 is present.
All inputs are finite; a program needn't handle non-finite values.
Results may differ from the reference program's by a relative error of at most 0.015.
Values may be sent and summed in bfloat16 or wider, within the bound.
No kernel may reach another device: no remote copies, remote signals or barrier semaphores. Data moves between devices by JAX's collectives and lax.ppermute only.
A program may use at most 64 MiB of HBM per device.

```python
import math
import jax
import jax.numpy as jnp
import numpy as np
from jax import lax

HEADS = 20
HDIM = 128
TOK_DEV = 64
WBLK = 4
FRAMES = 16
TOKENS = 32768
QBLK = 512
N_ROW = 64
N_COL = 8


def base_normal(key):
    return jnp.clip(jax.random.normal(key, (TOKENS, HEADS * HDIM), jnp.float32), -6.0, 6.0)


def draw_query(key, part):
    key = jax.random.fold_in(key, 5)
    field = base_normal(key)
    return field.astype(jnp.bfloat16)


def draw_key(key, part):
    key = jax.random.fold_in(key, 6)
    field = base_normal(key)
    return field.astype(jnp.bfloat16)


def block_scale(stream_key, shape, cuts, least, largest):
    gain = 1.0
    for position, shards_of in cuts:
        heights = jax.random.uniform(jax.random.fold_in(jax.random.fold_in(stream_key, 6), position), (shards_of,), jnp.float32, least / len(cuts), largest / len(cuts))
        gain = gain * jnp.repeat(jnp.exp(heights), shape[position] // shards_of).reshape((-1,) + (1,) * (len(shape) - 1 - position))
    return gain


def profile(count, total, limit, skew):
    weights = [(1 << 20) // math.isqrt(standing ** skew) + 1 for standing in range(2, count + 1)]
    surplus, holding = total - limit - (count - 1), [1] * (count - 1)
    while surplus > 0:
        candidates = [i for i in range(count - 1) if holding[i] < limit]
        whole, remaining = sum([weights[i] for i in candidates]), surplus
        for i in candidates:
            addition = min(limit - holding[i], max(1, remaining * weights[i] // whole), surplus)
            holding[i] = holding[i] + addition
            surplus = surplus - addition
    return np.array([limit] + holding)


def uneven_parts(key, number_of, total, limit, skew):
    if number_of == 2:
        one = jax.random.randint(key, (), max(1, total - limit), min(limit, total - 1) + 1)
        return jnp.stack([one, total - one])
    lengths = jnp.asarray(profile(number_of, total, limit, skew), jnp.int32)
    twos = (number_of - 1) // 2
    source_of, taker = lengths[1:1 + 2 * twos:2], lengths[2:2 + 2 * twos:2]
    room = jnp.minimum(source_of - 1, limit - taker)
    moved = jax.random.randint(jax.random.fold_in(key, 1), (twos,), 0, 1 << 20) % (room + 1)
    lengths = lengths.at[1:1 + 2 * twos:2].set(source_of - moved).at[2:2 + 2 * twos:2].set(taker + moved)
    return lengths[jax.random.permutation(jax.random.fold_in(key, 2), number_of)]


def normal_values(stream_key, dims, width, limit, shards=(), kind=jnp.bfloat16):
    entries = width * jax.random.normal(stream_key, dims, jnp.float32)
    if shards:
        entries = entries * block_scale(stream_key, dims, shards, -0.22, 0.18)
    return jnp.clip(entries, -limit, limit).astype(kind)


def setup_inputs(seed: int = 0) -> dict:
    seeds = jax.random.split(jax.random.key(seed), 7)
    return {
        "query": draw_query(jax.random.fold_in(seeds[6], 71), 0),
        "key": draw_key(jax.random.fold_in(seeds[6], 71), 0),
        "value": normal_values(seeds[2], (TOKENS, HEADS * HDIM), 1.0, 6.0, ((0, 512),)),
        "saved_out": normal_values(seeds[3], (TOKENS, HEADS * HDIM), 1.0, 6.0, ((0, 512),)),
        "grad_out": normal_values(seeds[4], (TOKENS, HEADS * HDIM), 1.0, 6.0, ((0, 512),)),
        "frame_ids": jnp.searchsorted(jnp.cumsum(uneven_parts(seeds[5], FRAMES, TOKENS, 2 * TOKENS // FRAMES, 1)), jnp.arange(TOKENS), side="right").astype(jnp.int32),
    }


def reference(query, key, value, saved_out, grad_out, frame_ids):
    factor = HDIM ** -0.5
    pad = (WBLK - 1) * QBLK
    span = WBLK * QBLK
    positions = jnp.arange(TOKENS + pad, dtype=jnp.int32)
    frames_pad = jnp.concatenate([jnp.zeros((pad,), jnp.int32), frame_ids.astype(jnp.int32)])
    valid_pad = positions >= pad

    def one_head(head):
        q_head = lax.dynamic_slice_in_dim(query, head * HDIM, HDIM, 1)
        k_head = lax.dynamic_slice_in_dim(key, head * HDIM, HDIM, 1)
        v_head = lax.dynamic_slice_in_dim(value, head * HDIM, HDIM, 1)
        o_head = lax.dynamic_slice_in_dim(saved_out, head * HDIM, HDIM, 1)
        g_head = lax.dynamic_slice_in_dim(grad_out, head * HDIM, HDIM, 1)
        k_pad = jnp.concatenate([jnp.zeros((pad, HDIM), jnp.bfloat16), k_head], axis=0)
        v_pad = jnp.concatenate([jnp.zeros((pad, HDIM), jnp.bfloat16), v_head], axis=0)

        def block_step(carry, block):
            key_acc, value_acc = carry
            start = (block * QBLK).astype(jnp.int32)
            q_blk = lax.dynamic_slice_in_dim(q_head, start, QBLK, 0)
            g_blk = lax.dynamic_slice_in_dim(g_head, start, QBLK, 0)
            o_blk = lax.dynamic_slice_in_dim(o_head, start, QBLK, 0)
            q_frame = lax.dynamic_slice_in_dim(frame_ids, start, QBLK, 0)
            k_win = lax.dynamic_slice_in_dim(k_pad, start, span, 0)
            v_win = lax.dynamic_slice_in_dim(v_pad, start, span, 0)
            k_frame = lax.dynamic_slice_in_dim(frames_pad, start, span, 0)
            k_valid = lax.dynamic_slice_in_dim(valid_pad, start, span, 0)
            allowed = k_valid[None, :] & (k_frame[None, :] <= q_frame[:, None])
            scores = jnp.dot(q_blk, k_win.T, preferred_element_type=jnp.float32) * factor
            row_max = jnp.max(jnp.where(allowed, scores, jnp.float32(-1e30)), axis=1)
            row_sum = jnp.sum(jnp.where(allowed, jnp.exp(scores - row_max[:, None]), 0.0), axis=1)
            log_total = row_max + jnp.log(row_sum)
            probs = jnp.where(allowed, jnp.exp(scores - log_total[:, None]), 0.0)
            dot_term = jnp.sum(g_blk.astype(jnp.float32) * o_blk.astype(jnp.float32), axis=1)
            grad_v = jnp.dot(probs.astype(jnp.bfloat16).T, g_blk, preferred_element_type=jnp.float32)
            grad_probs = jnp.dot(g_blk, v_win.T, preferred_element_type=jnp.float32)
            grad_scores = (probs * (grad_probs - dot_term[:, None]) * factor).astype(jnp.bfloat16)
            grad_k = jnp.dot(grad_scores.T, q_blk, preferred_element_type=jnp.float32)
            pieces = grad_scores.reshape(QBLK, WBLK, N_COL, TOK_DEV).astype(jnp.float32)
            key_pieces = k_win.reshape(WBLK, N_COL, TOK_DEV, HDIM).astype(jnp.float32)
            parts = jnp.einsum("qbct,bctd->cqd", pieces, key_pieces).astype(jnp.bfloat16)
            grad_q = jnp.sum(parts.astype(jnp.float32), axis=0)
            key_acc = lax.dynamic_update_slice_in_dim(key_acc, lax.dynamic_slice_in_dim(key_acc, start, span, 0) + grad_k, start, 0)
            value_acc = lax.dynamic_update_slice_in_dim(value_acc, lax.dynamic_slice_in_dim(value_acc, start, span, 0) + grad_v, start, 0)
            return (key_acc, value_acc), grad_q

        empty = jnp.zeros((TOKENS + pad, HDIM), jnp.float32)
        (key_acc, value_acc), grad_q = lax.scan(block_step, (empty, empty), jnp.arange(N_ROW, dtype=jnp.int32))
        return grad_q.reshape(TOKENS, HDIM), key_acc[pad:], value_acc[pad:]

    grad_q, grad_k, grad_v = lax.map(one_head, jnp.arange(HEADS, dtype=jnp.int32))

    def layout(stack):
        return jnp.transpose(stack, (1, 0, 2)).reshape(TOKENS, HEADS * HDIM).astype(jnp.bfloat16)

    return layout(grad_q), layout(grad_k), layout(grad_v)
```

```python
import functools
import math

import jax
import jax.numpy as jnp
from jax import lax
from jax.experimental import pallas as pl
from jax.experimental.pallas import tpu as pltpu
from jax.sharding import PartitionSpec as P

HEADS = 20
HDIM = 128
XN = 4
GROUP = HEADS // XN
NEG = -1e30
FACTOR = HDIM ** (-0.5)
SCALE2 = FACTOR * math.log2(math.e)
FRAME_LANE = 16
BF16 = jnp.bfloat16
F32 = jnp.float32
NT = (((1,), (1,)), ((), ()))
NN = (((1,), (0,)), ((), ()))


def params():
    return pltpu.CompilerParams(vmem_limit_bytes=40 * 1024 * 1024)


def cost(flops, moved, exps=0):
    return pl.CostEstimate(flops=flops, bytes_accessed=moved, transcendentals=exps)


def pack_kernel(x_ref, q_ref, k_ref, v_ref, o_ref, g_ref, f_ref, *outs):
    tok = q_ref.shape[0]
    lane = lax.broadcasted_iota(jnp.int32, (tok, HDIM), 1)
    frame = f_ref[...].astype(F32)
    for step in range(XN):
        qg, kv = outs[step], outs[XN + step]
        group = lax.rem(x_ref[0] + step, XN)
        meta = jnp.where(lane == FRAME_LANE, frame, 0.0)
        for h in range(GROUP):
            cols = pl.ds(pl.multiple_of((group * GROUP + h) * HDIM, HDIM), HDIM)
            grad = g_ref[:, cols]
            dot = jnp.sum(grad.astype(F32) * o_ref[:, cols].astype(F32), axis=1, keepdims=True)
            high = dot.astype(BF16).astype(F32)
            meta = jnp.where(lane == h, high, meta)
            meta = jnp.where(lane == 8 + h, dot - high, meta)
            at = 2 * h * HDIM
            qg[:, at : at + HDIM] = q_ref[:, cols]
            qg[:, at + HDIM : at + 2 * HDIM] = grad
            kv[:, at : at + HDIM] = k_ref[:, cols]
            kv[:, at + HDIM : at + 2 * HDIM] = v_ref[:, cols]
        qg[:, 2 * GROUP * HDIM :] = meta.astype(BF16)


def pack(x, query, key, value, saved_out, grad_out, frames):
    tok, width = query.shape
    wide = 2 * GROUP * HDIM
    vmem = pl.BlockSpec(memory_space=pltpu.VMEM)
    out_shape = [jax.ShapeDtypeStruct((tok, wide + HDIM), BF16)] * XN
    out_shape += [jax.ShapeDtypeStruct((tok, wide), BF16)] * XN
    outs = pl.pallas_call(
        pack_kernel,
        out_shape=out_shape,
        in_specs=[pl.BlockSpec(memory_space=pltpu.SMEM)] + [vmem] * 6,
        out_specs=[vmem] * (2 * XN),
        compiler_params=params(),
        cost_estimate=cost(2 * tok * width, 18 * tok * width),
        name="pack",
    )(x, query, key, value, saved_out, grad_out, frames)
    return outs[:XN], outs[XN:]


def window_scores(queries, keys):
    return lax.dot_general(keys, queries, NT, preferred_element_type=F32) * SCALE2


def meta_rows(own_meta, far_meta):
    return jnp.concatenate([own_meta[...], far_meta[...]], axis=0).astype(F32).T


def stats_kernel(bias_ref, q_own, q_far, m_own, m_far, w0, w1, w2, w3, out_ref):
    head = pl.program_id(0)
    queries = jnp.concatenate([q_own[...], q_far[...]], axis=0)
    rows = meta_rows(m_own, m_far)
    q_frame = rows[FRAME_LANE : FRAME_LANE + 1, :]
    k_frame = m_own[...].astype(F32)[:, FRAME_LANE : FRAME_LANE + 1]

    scores, peaks = [], []
    for at, ref in enumerate((w0, w1, w2, w3)):
        part = window_scores(queries, ref[...])
        if at == 0:
            part = jnp.where(k_frame <= q_frame, part, NEG)
        scores.append(part)
        peaks.append(jnp.max(part, axis=0, keepdims=True) + bias_ref[at])
    peak = functools.reduce(jnp.maximum, peaks)
    total = jnp.zeros_like(peak)
    for at, part in enumerate(scores):
        total += jnp.sum(jnp.exp2(part - (peak - bias_ref[at])), axis=0, keepdims=True)

    @pl.when(head == 0)
    def _():
        out_ref[...] = jnp.zeros_like(out_ref)

    out_ref[pl.ds(head, 1), :] = peak
    out_ref[pl.ds(8 + head, 1), :] = total


def stats(bias, own, far, window):
    half = own.shape[0]
    narrow = pl.BlockSpec((half, HDIM), lambda h: (0, 2 * h))
    meta = pl.BlockSpec((half, HDIM), lambda h: (0, 2 * GROUP))
    pairs = GROUP * 2 * half * 4 * half
    return pl.pallas_call(
        stats_kernel,
        grid=(GROUP,),
        out_shape=jax.ShapeDtypeStruct((16, 2 * half), F32),
        in_specs=[pl.BlockSpec(memory_space=pltpu.SMEM), narrow, narrow, meta, meta] + [narrow] * 4,
        out_specs=pl.BlockSpec((16, 2 * half), lambda h: (0, 0)),
        compiler_params=params(),
        cost_estimate=cost(4 * pairs * HDIM, 6 * half * GROUP * HDIM * 2, pairs),
        name="stats",
    )(bias, own, far, own, far, *window)


def grads_kernel(
    bias_ref, own_stats, far_stats, q_own, q_far, m_own, m_far, w0, w1, w2, w3,
    dq_own, dq_far, d0, d1, d2, d3,
):
    head = pl.program_id(0)
    half = q_own.shape[0]
    queries = jnp.concatenate([q_own[:, :HDIM], q_far[:, :HDIM]], axis=0)
    grads = jnp.concatenate([q_own[:, HDIM:], q_far[:, HDIM:]], axis=0)
    meta = jnp.concatenate([m_own[...], m_far[...]], axis=0).astype(F32)
    lane = lax.broadcasted_iota(jnp.int32, meta.shape, 1)
    dot_col = jnp.sum(
        jnp.where((lane == head) | (lane == head + 8), meta, 0.0), axis=1, keepdims=True
    )
    rows = jnp.where(lane == FRAME_LANE, meta, dot_col).T
    q_frame = rows[FRAME_LANE : FRAME_LANE + 1, :]
    dot = rows[0:1, :]
    k_frame = meta[:half, FRAME_LANE : FRAME_LANE + 1]

    own_peak = own_stats[pl.ds(head, 1), :]
    own_sum = own_stats[pl.ds(8 + head, 1), :]
    far_peak = far_stats[pl.ds(head, 1), :]
    far_sum = far_stats[pl.ds(8 + head, 1), :]
    far_peak = jnp.concatenate([far_peak[:, half:], far_peak[:, :half]], axis=1)
    far_sum = jnp.concatenate([far_sum[:, half:], far_sum[:, :half]], axis=1)
    peak = jnp.maximum(own_peak, far_peak)
    total = peak + jnp.log2(
        own_sum * jnp.exp2(own_peak - peak) + far_sum * jnp.exp2(far_peak - peak)
    )

    dq = jnp.zeros((HDIM, 2 * half), F32)
    for at, (ref, out) in enumerate(((w0, d0), (w1, d1), (w2, d2), (w3, d3))):
        keys, values = ref[:, :HDIM], ref[:, HDIM:]
        part = window_scores(queries, keys)
        if at == 0:
            part = jnp.where(k_frame <= q_frame, part, NEG)
        probs = jnp.exp2(part - (total - bias_ref[at]))
        dv = lax.dot_general(probs.astype(BF16), grads, NN, preferred_element_type=F32)
        dp = lax.dot_general(values, grads, NT, preferred_element_type=F32)
        ds = (probs * (dp - dot)).astype(BF16)
        dk = lax.dot_general(ds, queries, NN, preferred_element_type=F32) * FACTOR
        dq += lax.dot_general(keys.T, ds, NN, preferred_element_type=F32)
        out[:, :HDIM] = dk.astype(out.dtype)
        out[:, HDIM:] = dv.astype(out.dtype)
    dq = (dq * FACTOR).T
    dq_own[...] = dq[:half]
    dq_far[...] = dq[half:].astype(BF16)


def grads(bias, own_stats, far_stats, own, far, window):
    half = own.shape[0]
    pair = pl.BlockSpec((half, 2 * HDIM), lambda h: (0, h))
    narrow = pl.BlockSpec((half, HDIM), lambda h: (0, h))
    meta = pl.BlockSpec((half, HDIM), lambda h: (0, 2 * GROUP))
    vmem = pl.BlockSpec((16, 2 * half), lambda h: (0, 0))
    pairs = GROUP * 2 * half * 4 * half
    wide = GROUP * HDIM
    return pl.pallas_call(
        grads_kernel,
        grid=(GROUP,),
        out_shape=[
            jax.ShapeDtypeStruct((half, wide), F32),
            jax.ShapeDtypeStruct((half, wide), BF16),
            jax.ShapeDtypeStruct((half, 2 * wide), F32),
        ]
        + [jax.ShapeDtypeStruct((half, 2 * wide), BF16)] * 3,
        in_specs=[pl.BlockSpec(memory_space=pltpu.SMEM), vmem, vmem, pair, pair, meta, meta]
        + [pair] * 4,
        out_specs=[narrow, narrow] + [pair] * 4,
        compiler_params=params(),
        cost_estimate=cost(20 * pairs * HDIM, 18 * half * wide * 2, pairs),
        name="grads",
    )(bias, own_stats, far_stats, own, far, own, far, *window)


def close_kernel(even_ref, dq_own, dq_far, d0, back, side, *outs):
    even = even_ref[0].astype(F32)
    tok = outs[0].shape[0]
    for step in range(XN):
        rows = pl.ds(step * tok, tok)
        kv = d0[rows, :] + back[rows, :].astype(F32) + side[rows, :].astype(F32) * even
        wide = kv.shape[1]
        outs[step][:, :wide] = kv.astype(BF16)
        outs[step][:, wide:] = (dq_own[rows, :] + dq_far[rows, :].astype(F32)).astype(BF16)


def close(even, dq_own, dq_far, d0, back, side):
    half, wide = dq_own.shape
    tok = half // XN
    vmem = pl.BlockSpec(memory_space=pltpu.VMEM)
    return pl.pallas_call(
        close_kernel,
        out_shape=[jax.ShapeDtypeStruct((tok, 3 * wide), BF16)] * XN,
        in_specs=[pl.BlockSpec(memory_space=pltpu.SMEM)] + [vmem] * 5,
        out_specs=[vmem] * XN,
        compiler_params=params(),
        cost_estimate=cost(5 * half * wide, 28 * half * wide),
        name="close",
    )(even, dq_own, dq_far, d0, back, side)


def unpack_kernel(x_ref, *refs):
    parts, (dq, dk, dv) = refs[:XN], refs[XN:]
    base = 2 * GROUP * HDIM
    for step in range(XN):
        group = lax.rem(x_ref[0] + step, XN)
        for h in range(GROUP):
            cols = pl.ds(pl.multiple_of((group * GROUP + h) * HDIM, HDIM), HDIM)
            at = 2 * h * HDIM
            dk[:, cols] = parts[step][:, at : at + HDIM]
            dv[:, cols] = parts[step][:, at + HDIM : at + 2 * HDIM]
            dq[:, cols] = parts[step][:, base + h * HDIM : base + (h + 1) * HDIM]


def unpack(x, parts):
    tok = parts[0].shape[0]
    vmem = pl.BlockSpec(memory_space=pltpu.VMEM)
    return pl.pallas_call(
        unpack_kernel,
        out_shape=[jax.ShapeDtypeStruct((tok, HEADS * HDIM), BF16)] * 3,
        in_specs=[pl.BlockSpec(memory_space=pltpu.SMEM)] + [vmem] * XN,
        out_specs=[vmem] * 3,
        compiler_params=params(),
        cost_estimate=cost(0, 12 * tok * HEADS * HDIM),
        name="unpack",
    )(x, *parts)


def along_x(value, steps):
    count = lax.axis_size("col")
    moves = [(c, c // XN * XN + (c + steps) % XN) for c in range(count)]
    return lax.ppermute(value, "col", moves)


def across_z(value):
    count = lax.axis_size("col")
    return lax.ppermute(value, "col", [(c, (c + XN) % count) for c in range(count)])


def along_row(value, steps):
    count = lax.axis_size("row")
    first, last = max(0, -steps), min(count, count - steps)
    return lax.ppermute(value, "row", [(r, r + steps) for r in range(first, last)])


def in_chip(value):
    count = lax.axis_size("row")
    return lax.ppermute(value, "row", [(r, r ^ 1) for r in range(count)])


def per_device(query, key, value, saved_out, grad_out, frame_ids):
    row = lax.axis_index("row")
    x = (lax.axis_index("col") % XN).astype(jnp.int32).reshape(1)
    is_even = row % 2 == 0
    even = is_even.astype(jnp.int32).reshape(1)

    qg, kv = pack(x, query, key, value, saved_out, grad_out, frame_ids[:, None])
    own = jnp.concatenate([qg[0]] + [along_x(qg[s], s) for s in range(1, XN)], axis=0)
    far = across_z(own)
    w0 = jnp.concatenate([kv[0]] + [along_x(kv[s], s) for s in range(1, XN)], axis=0)
    w1 = along_row(w0, 2)
    w2 = in_chip(w1)
    w3 = along_row(jnp.where(is_even, w0, w1), 1)
    held = jnp.stack(
        [
            row >= 0,
            row >= 2,
            jnp.where(is_even, row >= 1, row >= 3),
            jnp.where(is_even, row >= 3, row >= 1),
        ]
    )
    bias = jnp.where(held, 0.0, NEG).astype(F32)
    window = (w0, w1, w2, w3)

    own_stats = stats(bias, own, far, window)
    far_stats = across_z(own_stats)
    dq_own, dq_far, d0, d1, d2, d3 = grads(bias, own_stats, far_stats, own, far, window)

    dq_back = across_z(dq_far)
    side = along_row(d3, -1)
    swapped = in_chip(d2)
    turned = jnp.where(is_even, jnp.zeros_like(side), side)
    d1 = (d1.astype(F32) + swapped.astype(F32) + turned.astype(F32)).astype(BF16)
    back = along_row(d1, -2)

    parts = close(even, dq_own, dq_back, d0, back, side)
    parts = [parts[0]] + [along_x(parts[s], -s) for s in range(1, XN)]
    return tuple(unpack(x, parts))


def solution(mesh):
    placed = P(("row", "col"), None)
    return jax.shard_map(
        per_device,
        mesh=mesh,
        in_specs=(placed,) * 5 + (P(("row", "col")),),
        out_specs=(placed,) * 3,
        check_vma=False,
    )
```

```python
import functools
import math

import jax
import jax.numpy as jnp
from jax import lax
from jax.experimental import pallas as pl
from jax.experimental.pallas import tpu as pltpu
from jax.sharding import PartitionSpec as P

HEADS = 20
HDIM = 128
XN = 4
GROUP = HEADS // XN
NEG = -1e30
FACTOR = HDIM ** (-0.5)
SCALE2 = FACTOR * math.log2(math.e)
FRAME_LANE = 16
BF16 = jnp.bfloat16
F32 = jnp.float32
NT = (((1,), (1,)), ((), ()))
NN = (((1,), (0,)), ((), ()))


def params(room=40):
    return pltpu.CompilerParams(vmem_limit_bytes=room * 1024 * 1024)


def cost(flops, moved, exps=0):
    return pl.CostEstimate(flops=flops, bytes_accessed=moved, transcendentals=exps)


def pack_kernel(q_any, k_any, v_any, o_any, g_any, f_ref, qk, gv, held, sems):
    copies = []
    for at, src in enumerate((q_any, k_any, g_any, o_any, v_any)):
        copies.append(pltpu.make_async_copy(src, held.at[at], sems.at[at]))
    for copy in copies:
        copy.start()
    for copy in copies:
        copy.wait()
    tok = held.shape[1]
    wide = GROUP * HDIM
    lane = lax.broadcasted_iota(jnp.int32, (tok, HDIM), 1)
    frame = f_ref[...].astype(F32)
    for group in range(XN):
        here = slice(group * wide, (group + 1) * wide)
        meta = jnp.where(lane == FRAME_LANE, frame, 0.0)
        for h in range(GROUP):
            cols = slice((group * GROUP + h) * HDIM, (group * GROUP + h + 1) * HDIM)
            product = held[2, :, cols].astype(F32) * held[3, :, cols].astype(F32)
            dot = jnp.sum(product, axis=1, keepdims=True)
            high = dot.astype(BF16).astype(F32)
            meta = jnp.where(lane == h, high, meta)
            meta = jnp.where(lane == 8 + h, dot - high, meta)
        qk[group, :, :wide] = held[0, :, here]
        qk[group, :, wide : wide + HDIM] = meta.astype(BF16)
        qk[group, :, wide + HDIM :] = held[1, :, here]
        gv[group, :, :wide] = held[2, :, here]
        gv[group, :, wide:] = held[4, :, here]


def pack(query, key, value, saved_out, grad_out, frames):
    tok, width = query.shape
    wide = GROUP * HDIM
    vmem = pl.BlockSpec(memory_space=pltpu.VMEM)
    return pl.pallas_call(
        pack_kernel,
        out_shape=[
            jax.ShapeDtypeStruct((XN, tok, 2 * wide + HDIM), BF16),
            jax.ShapeDtypeStruct((XN, tok, 2 * wide), BF16),
        ],
        in_specs=[pl.BlockSpec(memory_space=pl.ANY)] * 5 + [vmem],
        out_specs=[vmem] * 2,
        scratch_shapes=[pltpu.VMEM((5, tok, width), BF16), pltpu.SemaphoreType.DMA((5,))],
        compiler_params=params(60),
        cost_estimate=cost(2 * tok * width, 18 * tok * width),
        name="pack",
    )(query, key, value, saved_out, grad_out, frames)


def window_scores(queries, keys):
    return lax.dot_general(keys, queries, NT, preferred_element_type=F32) * SCALE2


def both(own, far):
    return jnp.concatenate([own[...], far[...]], axis=0)


def stats_kernel(bias_ref, q_own, q_far, m_own, m_far, w0, w1, w2, w3, out_ref):
    head = pl.program_id(0)
    queries = both(q_own, q_far)
    rows = both(m_own, m_far).astype(F32).T
    q_frame = rows[FRAME_LANE : FRAME_LANE + 1, :]
    k_frame = m_own[...].astype(F32)[:, FRAME_LANE : FRAME_LANE + 1]

    scores, peaks = [], []
    for at, ref in enumerate((w0, w1, w2, w3)):
        part = window_scores(queries, ref[...])
        if at == 0:
            part = jnp.where(k_frame <= q_frame, part, NEG)
        scores.append(part)
        peaks.append(jnp.max(part, axis=0, keepdims=True) + bias_ref[at])
    peak = functools.reduce(jnp.maximum, peaks)
    total = jnp.zeros_like(peak)
    for at, part in enumerate(scores):
        total += jnp.sum(jnp.exp2(part - (peak - bias_ref[at])), axis=0, keepdims=True)

    @pl.when(head == 0)
    def _():
        out_ref[...] = jnp.zeros_like(out_ref)

    out_ref[pl.ds(head, 1), :] = peak
    out_ref[pl.ds(8 + head, 1), :] = total


def head_block(half):
    return pl.BlockSpec((half, HDIM), lambda h: (0, h))


def meta_block(half):
    return pl.BlockSpec((half, HDIM), lambda h: (0, GROUP))


def whole(shape):
    return pl.BlockSpec(shape, lambda h: (0, 0))


def smem():
    return pl.BlockSpec(memory_space=pltpu.SMEM)


def stats(bias, q_own, q_far, keys):
    half = q_own.shape[0]
    narrow, meta = head_block(half), meta_block(half)
    pairs = GROUP * 2 * half * 4 * half
    return pl.pallas_call(
        stats_kernel,
        grid=(GROUP,),
        out_shape=jax.ShapeDtypeStruct((16, 2 * half), F32),
        in_specs=[smem(), narrow, narrow, meta, meta] + [narrow] * 4,
        out_specs=whole((16, 2 * half)),
        compiler_params=params(),
        cost_estimate=cost(4 * pairs * HDIM, 6 * half * GROUP * HDIM * 2, pairs),
        name="stats",
    )(bias, q_own, q_far, q_own, q_far, *keys)


def log_total(head, half, own_stats, far_stats):
    own_peak = own_stats[pl.ds(head, 1), :]
    own_sum = own_stats[pl.ds(8 + head, 1), :]
    far_peak = far_stats[pl.ds(head, 1), :]
    far_sum = far_stats[pl.ds(8 + head, 1), :]
    far_peak = jnp.concatenate([far_peak[:, half:], far_peak[:, :half]], axis=1)
    far_sum = jnp.concatenate([far_sum[:, half:], far_sum[:, :half]], axis=1)
    peak = jnp.maximum(own_peak, far_peak)
    own_part = own_sum * jnp.exp2(own_peak - peak)
    return peak + jnp.log2(own_part + far_sum * jnp.exp2(far_peak - peak))


def dot_and_frame(head, m_own, m_far):
    meta = both(m_own, m_far).astype(F32)
    lane = lax.broadcasted_iota(jnp.int32, meta.shape, 1)
    picked = (lane == head) | (lane == head + 8)
    dot_col = jnp.sum(jnp.where(picked, meta, 0.0), axis=1, keepdims=True)
    rows = jnp.where(lane == FRAME_LANE, meta, dot_col).T
    return rows[0:1, :], rows[FRAME_LANE : FRAME_LANE + 1, :]


def block_grads(scores, total, dot, queries, grads, keys, values):
    probs = jnp.exp2(scores - total)
    dv = lax.dot_general(probs.astype(BF16), grads, NN, preferred_element_type=F32)
    dp = lax.dot_general(values, grads, NT, preferred_element_type=F32)
    ds = (probs * (dp - dot)).astype(BF16)
    dk = lax.dot_general(ds, queries, NN, preferred_element_type=F32) * FACTOR
    dq = lax.dot_general(keys.T, ds, NN, preferred_element_type=F32)
    return dq, dk, dv


def earlier_kernel(
    bias_ref, own_stats, far_stats, q_own, q_far, g_own, g_far, m_own, m_far,
    k1, k2, k3, v1, v2, v3, dq_ref, dk1, dk2, dk3, dv1, dv2, dv3,
):
    head = pl.program_id(0)
    queries, grads = both(q_own, q_far), both(g_own, g_far)
    dot, _ = dot_and_frame(head, m_own, m_far)
    total = log_total(head, q_own.shape[0], own_stats, far_stats)
    dq_sum = jnp.zeros(dq_ref.shape, F32)
    blocks = ((k1, v1, dk1, dv1), (k2, v2, dk2, dv2), (k3, v3, dk3, dv3))
    for at, (k_ref, v_ref, dk_ref, dv_ref) in enumerate(blocks):
        keys = k_ref[...]
        scores = window_scores(queries, keys)
        bound = total - bias_ref[at + 1]
        dq, dk, dv = block_grads(scores, bound, dot, queries, grads, keys, v_ref[...])
        dq_sum += dq
        dk_ref[...] = dk.astype(BF16)
        dv_ref[...] = dv.astype(BF16)
    dq_ref[...] = dq_sum


def earlier(bias, own_stats, far_stats, q_own, q_far, g_own, g_far, keys, values):
    half = q_own.shape[0]
    wide = GROUP * HDIM
    narrow, meta = head_block(half), meta_block(half)
    stat = whole((16, 2 * half))
    pairs = GROUP * 2 * half * 3 * half
    outs = pl.pallas_call(
        earlier_kernel,
        grid=(GROUP,),
        out_shape=[jax.ShapeDtypeStruct((wide, 2 * half), F32)]
        + [jax.ShapeDtypeStruct((half, wide), BF16)] * 6,
        in_specs=[smem(), stat, stat] + [narrow] * 4 + [meta] * 2 + [narrow] * 6,
        out_specs=[pl.BlockSpec((HDIM, 2 * half), lambda h: (h, 0))] + [narrow] * 6,
        compiler_params=params(),
        cost_estimate=cost(10 * pairs * HDIM, 20 * half * wide * 2, pairs),
        name="earlier",
    )(bias, own_stats, far_stats, q_own, q_far, g_own, g_far, q_own, q_far, *keys, *values)
    return outs[0], outs[1:4], outs[4:7]


def same_kernel(
    own_stats, far_stats, q_own, q_far, g_own, g_far, m_own, m_far,
    k_ref, v_ref, dq_ref, dq_own, dq_far, dk_ref, dv_ref,
):
    head = pl.program_id(0)
    half = q_own.shape[0]
    queries, grads = both(q_own, q_far), both(g_own, g_far)
    dot, q_frame = dot_and_frame(head, m_own, m_far)
    k_frame = m_own[...].astype(F32)[:, FRAME_LANE : FRAME_LANE + 1]
    total = log_total(head, half, own_stats, far_stats)
    keys = k_ref[...]
    scores = jnp.where(k_frame <= q_frame, window_scores(queries, keys), NEG)
    dq, dk, dv = block_grads(scores, total, dot, queries, grads, keys, v_ref[...])
    dq = ((dq + dq_ref[...]) * FACTOR).T
    dq_own[...] = dq[:half]
    dq_far[...] = dq[half:].astype(BF16)
    dk_ref[...] = dk
    dv_ref[...] = dv


def same(own_stats, far_stats, q_own, q_far, g_own, g_far, keys, values, dq):
    half = q_own.shape[0]
    wide = GROUP * HDIM
    narrow, meta = head_block(half), meta_block(half)
    stat = whole((16, 2 * half))
    pairs = GROUP * 2 * half * half
    turned = pl.BlockSpec((HDIM, 2 * half), lambda h: (h, 0))
    return pl.pallas_call(
        same_kernel,
        grid=(GROUP,),
        out_shape=[
            jax.ShapeDtypeStruct((half, wide), F32),
            jax.ShapeDtypeStruct((half, wide), BF16),
            jax.ShapeDtypeStruct((half, wide), F32),
            jax.ShapeDtypeStruct((half, wide), F32),
        ],
        in_specs=[stat, stat] + [narrow] * 4 + [meta] * 2 + [narrow] * 2 + [turned],
        out_specs=[narrow] * 4,
        compiler_params=params(),
        cost_estimate=cost(10 * pairs * HDIM, 16 * half * wide * 2, pairs),
        name="same",
    )(own_stats, far_stats, q_own, q_far, g_own, g_far, q_own, q_far, keys, values, dq)


def close_kernel(even_ref, dq_own, dq_far, dk, dv, k_back, v_back, k_side, v_side, out):
    even = even_ref[0].astype(F32)
    tok = out.shape[1]
    wide = dq_own.shape[1]
    for step in range(XN):
        rows = slice(step * tok, (step + 1) * tok)
        grad_q = dq_own[rows, :] + dq_far[rows, :].astype(F32)
        grad_k = dk[rows, :] + k_back[rows, :].astype(F32) + k_side[rows, :].astype(F32) * even
        grad_v = dv[rows, :] + v_back[rows, :].astype(F32) + v_side[rows, :].astype(F32) * even
        out[step, :, :wide] = grad_q.astype(BF16)
        out[step, :, wide : 2 * wide] = grad_k.astype(BF16)
        out[step, :, 2 * wide :] = grad_v.astype(BF16)


def close(even, dq_own, dq_far, dk, dv, k_back, v_back, k_side, v_side):
    half, wide = dq_own.shape
    tok = half // XN
    vmem = pl.BlockSpec(memory_space=pltpu.VMEM)
    return pl.pallas_call(
        close_kernel,
        out_shape=jax.ShapeDtypeStruct((XN, tok, 3 * wide), BF16),
        in_specs=[smem()] + [vmem] * 8,
        out_specs=vmem,
        compiler_params=params(),
        cost_estimate=cost(5 * half * wide, 28 * half * wide),
        name="close",
    )(even, dq_own, dq_far, dk, dv, k_back, v_back, k_side, v_side)


def unpack_kernel(parts, dq, dk, dv):
    wide = GROUP * HDIM
    for group in range(XN):
        here = slice(group * wide, (group + 1) * wide)
        dq[:, here] = parts[group, :, :wide]
        dk[:, here] = parts[group, :, wide : 2 * wide]
        dv[:, here] = parts[group, :, 2 * wide :]


def unpack(parts):
    tok = parts.shape[1]
    vmem = pl.BlockSpec(memory_space=pltpu.VMEM)
    return pl.pallas_call(
        unpack_kernel,
        out_shape=[jax.ShapeDtypeStruct((tok, HEADS * HDIM), BF16)] * 3,
        in_specs=[vmem],
        out_specs=[vmem] * 3,
        compiler_params=params(),
        cost_estimate=cost(0, 12 * tok * HEADS * HDIM),
        name="unpack",
    )(parts)


def over_x(value):
    groups = [[z * XN + x for x in range(XN)] for z in range(lax.axis_size("col") // XN)]
    return lax.all_to_all(value, "col", 0, 0, axis_index_groups=groups)


def across_z(value):
    count = lax.axis_size("col")
    return lax.ppermute(value, "col", [(c, (c + XN) % count) for c in range(count)])


def along_row(value, steps):
    count = lax.axis_size("row")
    first, last = max(0, -steps), min(count, count - steps)
    return lax.ppermute(value, "row", [(r, r + steps) for r in range(first, last)])


def in_chip(value):
    count = lax.axis_size("row")
    return lax.ppermute(value, "row", [(r, r ^ 1) for r in range(count)])


def halo(own, is_even):
    second = along_row(own, 2)
    swapped = in_chip(second)
    third = along_row(jnp.where(is_even, own, second), 1)
    return own, second, swapped, third


def halo_back(second, swapped, third, is_even):
    side = along_row(third, -1)
    turned = jnp.where(is_even, jnp.zeros_like(side), side)
    held = second.astype(F32) + in_chip(swapped).astype(F32) + turned.astype(F32)
    return along_row(held.astype(BF16), -2), side


def per_device(query, key, value, saved_out, grad_out, frame_ids):
    row = lax.axis_index("row")
    is_even = row % 2 == 0
    even = is_even.astype(jnp.int32).reshape(1)
    wide = GROUP * HDIM
    half = query.shape[0] * XN

    qk, gv = pack(query, key, value, saved_out, grad_out, frame_ids[:, None])
    qk = over_x(qk)
    gv = over_x(gv)
    q_own = qk[:, :, : wide + HDIM].reshape(half, wide + HDIM)
    g_own = gv[:, :, :wide].reshape(half, wide)
    q_far = across_z(q_own)
    g_far = across_z(g_own)
    keys = halo(qk[:, :, wide + HDIM :].reshape(half, wide), is_even)
    values = halo(gv[:, :, wide:].reshape(half, wide), is_even)
    held = jnp.stack(
        [
            row >= 0,
            row >= 2,
            jnp.where(is_even, row >= 1, row >= 3),
            jnp.where(is_even, row >= 3, row >= 1),
        ]
    )
    bias = jnp.where(held, 0.0, NEG).astype(F32)

    own_stats = stats(bias, q_own, q_far, keys)
    far_stats = across_z(own_stats)
    tokens = (own_stats, far_stats, q_own, q_far, g_own, g_far)
    dq_part, dk_parts, dv_parts = earlier(bias, *tokens, keys[1:], values[1:])
    dq_own, dq_far, dk, dv = same(*tokens, keys[0], values[0], dq_part)

    k_back, k_side = halo_back(*dk_parts, is_even)
    v_back, v_side = halo_back(*dv_parts, is_even)
    dq_far = across_z(dq_far)
    parts = close(even, dq_own, dq_far, dk, dv, k_back, v_back, k_side, v_side)
    return tuple(unpack(over_x(parts)))


def solution(mesh):
    placed = P(("row", "col"), None)
    return jax.shard_map(
        per_device,
        mesh=mesh,
        in_specs=(placed,) * 5 + (P(("row", "col")),),
        out_specs=(placed,) * 3,
        check_vma=False,
    )
```

```python
import functools
import math

import jax
import jax.numpy as jnp
from jax import lax
from jax.experimental import pallas as pl
from jax.experimental.pallas import tpu as pltpu
from jax.sharding import PartitionSpec as P

HEADS = 20
HDIM = 128
XN = 4
GROUP = HEADS // XN
NEG = -1e30
FACTOR = HDIM ** (-0.5)
SCALE2 = FACTOR * math.log2(math.e)
LOW_LANE = 32
FRAME_LANE = 64
BF16 = jnp.bfloat16
F32 = jnp.float32
NT = (((1,), (1,)), ((), ()))
NN = (((1,), (0,)), ((), ()))


def params(room=40):
    return pltpu.CompilerParams(vmem_limit_bytes=room * 1024 * 1024)


def cost(flops, moved, exps=0):
    return pl.CostEstimate(flops=flops, bytes_accessed=moved, transcendentals=exps)


def pack_kernel(q_any, k_any, v_any, o_any, g_any, f_ref, kv, qg, held, sems):
    copies = []
    for at, src in enumerate((k_any, v_any, g_any, o_any, q_any)):
        copies.append(pltpu.make_async_copy(src, held.at[at], sems.at[at]))
    for copy in copies:
        copy.start()
    for copy in copies:
        copy.wait()
    tok = held.shape[1]
    wide = GROUP * HDIM
    lane = lax.broadcasted_iota(jnp.int32, (tok, HDIM), 1)
    meta = jnp.where(lane == FRAME_LANE, f_ref[...].astype(F32), 0.0)
    for head in range(HEADS):
        group, h = divmod(head, GROUP)
        cols = slice(head * HDIM, (head + 1) * HDIM)
        product = held[2, :, cols].astype(F32) * held[3, :, cols].astype(F32)
        dot = jnp.sum(product, axis=1, keepdims=True)
        high = dot.astype(BF16).astype(F32)
        meta = jnp.where(lane == head, high, meta)
        meta = jnp.where(lane == LOW_LANE + head, dot - high, meta)
        kv[group, :, 2 * h * HDIM : (2 * h + 1) * HDIM] = held[0, :, cols]
        kv[group, :, (2 * h + 1) * HDIM : (2 * h + 2) * HDIM] = held[1, :, cols]
    meta = meta.astype(BF16)
    for target in range(qg.shape[0]):
        group = target % XN
        here = slice(group * wide, (group + 1) * wide)
        qg[target, :, :wide] = held[4, :, here]
        qg[target, :, wide : 2 * wide] = held[2, :, here]
        qg[target, :, 2 * wide :] = meta


def pack(query, key, value, saved_out, grad_out, frames):
    tok, width = query.shape
    wide = GROUP * HDIM
    vmem = pl.BlockSpec(memory_space=pltpu.VMEM)
    return pl.pallas_call(
        pack_kernel,
        out_shape=[
            jax.ShapeDtypeStruct((XN, tok, 2 * wide), BF16),
            jax.ShapeDtypeStruct((lax.axis_size("col"), tok, 2 * wide + HDIM), BF16),
        ],
        in_specs=[pl.BlockSpec(memory_space=pl.ANY)] * 5 + [vmem],
        out_specs=[vmem] * 2,
        scratch_shapes=[pltpu.VMEM((5, tok, width), BF16), pltpu.SemaphoreType.DMA((5,))],
        compiler_params=params(60),
        cost_estimate=cost(2 * tok * width, 18 * tok * width),
        name="pack",
    )(query, key, value, saved_out, grad_out, frames)


def window_scores(queries, keys):
    return lax.dot_general(keys, queries, NT, preferred_element_type=F32) * SCALE2


def key_frames(place, meta):
    half = meta.shape[0] // 2
    frames = meta[:, FRAME_LANE : FRAME_LANE + 1]
    return jnp.where(place[1] == 0, frames[:half], frames[half:])


def stats_kernel(bias_ref, place, q_ref, m_ref, w0, w1, w2, w3, out_ref):
    head = pl.program_id(0)
    queries = q_ref[...]
    meta = m_ref[...].astype(F32)
    q_frame = meta.T[FRAME_LANE : FRAME_LANE + 1, :]

    scores, peaks = [], []
    for at, ref in enumerate((w0, w1, w2, w3)):
        part = window_scores(queries, ref[...])
        if at == 0:
            part = jnp.where(key_frames(place, meta) <= q_frame, part, NEG)
        scores.append(part)
        peaks.append(jnp.max(part, axis=0, keepdims=True) + bias_ref[at])
    peak = functools.reduce(jnp.maximum, peaks)
    total = jnp.zeros_like(peak)
    for at, part in enumerate(scores):
        total += jnp.sum(jnp.exp2(part - (peak - bias_ref[at])), axis=0, keepdims=True)

    @pl.when(head == 0)
    def _():
        out_ref[...] = jnp.zeros_like(out_ref)

    out_ref[pl.ds(head, 1), :] = peak
    out_ref[pl.ds(8 + head, 1), :] = total


def part_block(half, first):
    return pl.BlockSpec((half, HDIM), lambda h: (0, first + h))


def meta_block(half):
    return pl.BlockSpec((half, HDIM), lambda h: (0, 2 * GROUP))


def key_block(half):
    return pl.BlockSpec((half, HDIM), lambda h: (0, 2 * h))


def pair_block(half):
    return pl.BlockSpec((half, 2 * HDIM), lambda h: (0, h))


def whole(shape):
    return pl.BlockSpec(shape, lambda h: (0, 0))


def smem():
    return pl.BlockSpec(memory_space=pltpu.SMEM)


def stats(bias, place, qg, window):
    count, half = qg.shape[0], window[0].shape[0]
    pairs = GROUP * count * 4 * half
    return pl.pallas_call(
        stats_kernel,
        grid=(GROUP,),
        out_shape=jax.ShapeDtypeStruct((16, count), F32),
        in_specs=[smem(), smem(), part_block(count, 0), meta_block(count)] + [key_block(half)] * 4,
        out_specs=whole((16, count)),
        compiler_params=params(),
        cost_estimate=cost(4 * pairs * HDIM, 6 * half * GROUP * HDIM * 2, pairs),
        name="stats",
    )(bias, place, qg, qg, *window)


def log_total(head, own_stats, far_stats):
    own_peak = own_stats[pl.ds(head, 1), :]
    own_sum = own_stats[pl.ds(8 + head, 1), :]
    far_peak = far_stats[pl.ds(head, 1), :]
    far_sum = far_stats[pl.ds(8 + head, 1), :]
    peak = jnp.maximum(own_peak, far_peak)
    own_part = own_sum * jnp.exp2(own_peak - peak)
    return peak + jnp.log2(own_part + far_sum * jnp.exp2(far_peak - peak))


def dot_and_frame(head, meta):
    lane = lax.broadcasted_iota(jnp.int32, meta.shape, 1)
    picked = (lane == head) | (lane == head + LOW_LANE)
    dot_col = jnp.sum(jnp.where(picked, meta, 0.0), axis=1, keepdims=True)
    rows = jnp.where(lane == FRAME_LANE, meta, dot_col).T
    return rows[0:1, :], rows[FRAME_LANE : FRAME_LANE + 1, :]


def block_grads(scores, total, dot, queries, grads, keys, values):
    probs = jnp.exp2(scores - total)
    dv = lax.dot_general(probs.astype(BF16), grads, NN, preferred_element_type=F32)
    dp = lax.dot_general(values, grads, NT, preferred_element_type=F32)
    ds = (probs * (dp - dot)).astype(BF16)
    dk = lax.dot_general(ds, queries, NN, preferred_element_type=F32) * FACTOR
    dq = lax.dot_general(keys.T, ds, NN, preferred_element_type=F32)
    return dq, dk, dv


def earlier_kernel(
    bias_ref, place, own_stats, far_stats, q_ref, g_ref, m_ref, w1, w2, w3, dq_ref, d1, d2, d3
):
    head = pl.program_id(0)
    queries, grads = q_ref[...], g_ref[...]
    dot, _ = dot_and_frame(place[0] * GROUP + head, m_ref[...].astype(F32))
    total = log_total(head, own_stats, far_stats)
    dq_sum = jnp.zeros(dq_ref.shape, F32)
    for at, (ref, out) in enumerate(((w1, d1), (w2, d2), (w3, d3))):
        keys, values = ref[:, :HDIM], ref[:, HDIM:]
        scores = window_scores(queries, keys)
        bound = total - bias_ref[at + 1]
        dq, dk, dv = block_grads(scores, bound, dot, queries, grads, keys, values)
        dq_sum += dq
        out[:, :HDIM] = dk.astype(BF16)
        out[:, HDIM:] = dv.astype(BF16)
    dq_ref[...] = dq_sum


def query_specs(count):
    stat = whole((16, count))
    parts = [part_block(count, 0), part_block(count, GROUP), meta_block(count)]
    return [smem(), stat, stat] + parts


def turned_block(count):
    return pl.BlockSpec((HDIM, count), lambda h: (h, 0))


def earlier(bias, place, own_stats, far_stats, qg, window):
    count, half = qg.shape[0], window[0].shape[0]
    wide = GROUP * HDIM
    pairs = GROUP * count * 3 * half
    return pl.pallas_call(
        earlier_kernel,
        grid=(GROUP,),
        out_shape=[jax.ShapeDtypeStruct((wide, count), F32)]
        + [jax.ShapeDtypeStruct((half, 2 * wide), BF16)] * 3,
        in_specs=[smem()] + query_specs(count) + [pair_block(half)] * 3,
        out_specs=[turned_block(count)] + [pair_block(half)] * 3,
        compiler_params=params(),
        cost_estimate=cost(10 * pairs * HDIM, 20 * half * wide * 2, pairs),
        name="earlier",
    )(bias, place, own_stats, far_stats, qg, qg, qg, *window)


def same_kernel(
    place, own_stats, far_stats, q_ref, g_ref, m_ref, w0, dq_ref, dq_out, d0
):
    head = pl.program_id(0)
    queries, grads = q_ref[...], g_ref[...]
    meta = m_ref[...].astype(F32)
    dot, q_frame = dot_and_frame(place[0] * GROUP + head, meta)
    total = log_total(head, own_stats, far_stats)
    keys, values = w0[:, :HDIM], w0[:, HDIM:]
    scores = window_scores(queries, keys)
    scores = jnp.where(key_frames(place, meta) <= q_frame, scores, NEG)
    dq, dk, dv = block_grads(scores, total, dot, queries, grads, keys, values)
    dq_out[...] = ((dq + dq_ref[...]) * FACTOR).T.astype(BF16)
    d0[:, :HDIM] = dk
    d0[:, HDIM:] = dv


def same(place, own_stats, far_stats, qg, w0, dq):
    count, half = qg.shape[0], w0.shape[0]
    wide = GROUP * HDIM
    pairs = GROUP * count * half
    return pl.pallas_call(
        same_kernel,
        grid=(GROUP,),
        out_shape=[
            jax.ShapeDtypeStruct((count, wide), BF16),
            jax.ShapeDtypeStruct((half, 2 * wide), F32),
        ],
        in_specs=query_specs(count) + [pair_block(half), turned_block(count)],
        out_specs=[part_block(count, 0), pair_block(half)],
        compiler_params=params(),
        cost_estimate=cost(10 * pairs * HDIM, 16 * half * wide * 2, pairs),
        name="same",
    )(place, own_stats, far_stats, qg, qg, qg, w0, dq)


def close_kernel(even_ref, d0, back, side, out):
    even = even_ref[0].astype(F32)
    tok = out.shape[1]
    for step in range(XN):
        rows = slice(step * tok, (step + 1) * tok)
        pair = d0[rows, :] + back[rows, :].astype(F32) + side[rows, :].astype(F32) * even
        out[step] = pair.astype(BF16)


def close(even, d0, back, side):
    half, wide = d0.shape
    tok = half // XN
    vmem = pl.BlockSpec(memory_space=pltpu.VMEM)
    return pl.pallas_call(
        close_kernel,
        out_shape=jax.ShapeDtypeStruct((XN, tok, wide), BF16),
        in_specs=[smem()] + [vmem] * 3,
        out_specs=vmem,
        compiler_params=params(),
        cost_estimate=cost(3 * half * wide, 10 * half * wide),
        name="close",
    )(even, d0, back, side)


def unpack_kernel(parts, halves, dq, dk, dv):
    wide = GROUP * HDIM
    for group in range(XN):
        total = halves[group].astype(F32) + halves[XN + group].astype(F32)
        dq[:, group * wide : (group + 1) * wide] = total.astype(BF16)
        for h in range(GROUP):
            at = 2 * h * HDIM
            cols = slice((group * GROUP + h) * HDIM, (group * GROUP + h + 1) * HDIM)
            dk[:, cols] = parts[group, :, at : at + HDIM]
            dv[:, cols] = parts[group, :, at + HDIM : at + 2 * HDIM]


def unpack(parts, halves):
    tok = parts.shape[1]
    vmem = pl.BlockSpec(memory_space=pltpu.VMEM)
    return pl.pallas_call(
        unpack_kernel,
        out_shape=[jax.ShapeDtypeStruct((tok, HEADS * HDIM), BF16)] * 3,
        in_specs=[vmem] * 2,
        out_specs=[vmem] * 3,
        compiler_params=params(),
        cost_estimate=cost(0, 14 * tok * HEADS * HDIM),
        name="unpack",
    )(parts, halves)


def over_x(value):
    groups = [[z * XN + x for x in range(XN)] for z in range(lax.axis_size("col") // XN)]
    return lax.all_to_all(value, "col", 0, 0, axis_index_groups=groups)


def across_z(value):
    count = lax.axis_size("col")
    return lax.ppermute(value, "col", [(c, (c + XN) % count) for c in range(count)])


def along_row(value, steps):
    count = lax.axis_size("row")
    first, last = max(0, -steps), min(count, count - steps)
    return lax.ppermute(value, "row", [(r, r + steps) for r in range(first, last)])


def in_chip(value):
    count = lax.axis_size("row")
    return lax.ppermute(value, "row", [(r, r ^ 1) for r in range(count)])


def halo(own, is_even):
    second = along_row(own, 2)
    swapped = in_chip(second)
    third = along_row(jnp.where(is_even, own, second), 1)
    return own, second, swapped, third


def halo_back(second, swapped, third, is_even):
    side = along_row(third, -1)
    turned = jnp.where(is_even, jnp.zeros_like(side), side)
    held = second.astype(F32) + in_chip(swapped).astype(F32) + turned.astype(F32)
    return along_row(held.astype(BF16), -2), side


def per_device(query, key, value, saved_out, grad_out, frame_ids):
    row, col = lax.axis_index("row"), lax.axis_index("col")
    place = jnp.stack([col % XN, col // XN]).astype(jnp.int32)
    is_even = row % 2 == 0
    even = is_even.astype(jnp.int32).reshape(1)
    tok = query.shape[0]
    count = lax.axis_size("col") * tok

    kv, qg = pack(query, key, value, saved_out, grad_out, frame_ids[:, None])
    qg = lax.all_to_all(qg, "col", 0, 0).reshape(count, -1)
    window = halo(over_x(kv).reshape(XN * tok, -1), is_even)
    held = jnp.stack(
        [
            row >= 0,
            row >= 2,
            jnp.where(is_even, row >= 1, row >= 3),
            jnp.where(is_even, row >= 3, row >= 1),
        ]
    )
    bias = jnp.where(held, 0.0, NEG).astype(F32)

    own_stats = stats(bias, place, qg, window)
    far_stats = across_z(own_stats)
    dq_part, *earlier_grads = earlier(bias, place, own_stats, far_stats, qg, window[1:])
    dq, d0 = same(place, own_stats, far_stats, qg, window[0], dq_part)

    back, side = halo_back(*earlier_grads, is_even)
    halves = lax.all_to_all(dq.reshape(-1, tok, GROUP * HDIM), "col", 0, 0)
    return tuple(unpack(over_x(close(even, d0, back, side)), halves))


def solution(mesh):
    placed = P(("row", "col"), None)
    return jax.shard_map(
        per_device,
        mesh=mesh,
        in_specs=(placed,) * 5 + (P(("row", "col")),),
        out_specs=(placed,) * 3,
        check_vma=False,
    )
```

```python
import functools
import math

import jax
import jax.numpy as jnp
from jax import lax
from jax.experimental import pallas as pl
from jax.experimental.pallas import tpu as pltpu
from jax.sharding import PartitionSpec as P

HEADS = 20
HDIM = 128
XN = 4
GROUP = HEADS // XN
NEG = -1e30
FACTOR = HDIM ** (-0.5)
SCALE2 = FACTOR * math.log2(math.e)
LOW_LANE = 32
FRAME_LANE = 64
BF16 = jnp.bfloat16
F32 = jnp.float32
NT = (((1,), (1,)), ((), ()))
NN = (((1,), (0,)), ((), ()))


def params(room=40):
    return pltpu.CompilerParams(vmem_limit_bytes=room * 1024 * 1024)


def cost(flops, moved, exps=0):
    return pl.CostEstimate(flops=flops, bytes_accessed=moved, transcendentals=exps)


def load_all(sources, held, sems):
    copies = [
        pltpu.make_async_copy(src, held.at[at], sems.at[at]) for at, src in enumerate(sources)
    ]
    for copy in copies:
        copy.start()
    for copy in copies:
        copy.wait()


def pack_queries_kernel(q_any, o_any, g_any, f_ref, out, held, sems):
    load_all((q_any, o_any, g_any), held, sems)
    tok = held.shape[1]
    wide = GROUP * HDIM
    lane = lax.broadcasted_iota(jnp.int32, (tok, HDIM), 1)
    meta = jnp.where(lane == FRAME_LANE, f_ref[...].astype(F32), 0.0)
    for head in range(HEADS):
        cols = slice(head * HDIM, (head + 1) * HDIM)
        product = held[2, :, cols].astype(F32) * held[1, :, cols].astype(F32)
        dot = jnp.sum(product, axis=1, keepdims=True)
        high = dot.astype(BF16).astype(F32)
        meta = jnp.where(lane == head, high, meta)
        meta = jnp.where(lane == LOW_LANE + head, dot - high, meta)
    meta = meta.astype(BF16)
    for target in range(out.shape[0]):
        group = target % XN
        here = slice(group * wide, (group + 1) * wide)
        out[target, :, :wide] = held[0, :, here]
        out[target, :, wide : 2 * wide] = held[2, :, here]
        out[target, :, 2 * wide :] = meta


def pack_queries(query, saved_out, grad_out, frames):
    tok, width = query.shape
    vmem = pl.BlockSpec(memory_space=pltpu.VMEM)
    shape = (lax.axis_size("col"), tok, 2 * GROUP * HDIM + HDIM)
    return pl.pallas_call(
        pack_queries_kernel,
        out_shape=jax.ShapeDtypeStruct(shape, BF16),
        in_specs=[pl.BlockSpec(memory_space=pl.ANY)] * 3 + [vmem],
        out_specs=vmem,
        scratch_shapes=[pltpu.VMEM((3, tok, width), BF16), pltpu.SemaphoreType.DMA((3,))],
        compiler_params=params(60),
        cost_estimate=cost(2 * tok * width, 14 * tok * width),
        name="pack_queries",
    )(query, saved_out, grad_out, frames)


def head_columns(place, step, h):
    group = lax.rem(place[0] + step, XN)
    return pl.ds(pl.multiple_of((group * GROUP + h) * HDIM, HDIM), HDIM)


def pack_keys_kernel(place, k_ref, v_ref, k2_ref, v2_ref, *outs):
    for step in range(XN):
        for h in range(GROUP):
            cols = head_columns(place, step, h)
            for at, ref in enumerate((k_ref, v_ref, k2_ref, v2_ref)):
                first = (2 * (at // 2 * GROUP + h) + at % 2) * HDIM
                outs[step][:, first : first + HDIM] = ref[:, cols]


def pack_keys(place, key, value, far_key, far_value):
    tok, width = key.shape
    return pl.pallas_call(
        pack_keys_kernel,
        out_shape=[jax.ShapeDtypeStruct((tok, 4 * GROUP * HDIM), BF16)] * XN,
        in_specs=[smem()] + [pl.BlockSpec(memory_space=pltpu.VMEM)] * 4,
        out_specs=[pl.BlockSpec(memory_space=pltpu.VMEM)] * XN,
        compiler_params=params(),
        cost_estimate=cost(0, 16 * tok * width),
        name="pack_keys",
    )(place, key, value, far_key, far_value)


def window_scores(queries, keys):
    return lax.dot_general(keys, queries, NT, preferred_element_type=F32) * SCALE2


def key_frames(place, m_ref):
    tok = m_ref.shape[0] // (2 * XN)
    pieces = []
    for step in range(XN):
        piece = place[1] * XN + lax.rem(place[0] + XN - step, XN)
        rows = pl.ds(pl.multiple_of(piece * tok, tok), tok)
        pieces.append(m_ref[rows, :].astype(F32)[:, FRAME_LANE : FRAME_LANE + 1])
    return jnp.concatenate(pieces, axis=0)


def stats_kernel(bias_ref, place, q_ref, m_ref, w0, w1, w2, w3, out_ref):
    head = pl.program_id(0)
    queries = q_ref[...]
    meta = m_ref[...].astype(F32)
    q_frame = meta.T[FRAME_LANE : FRAME_LANE + 1, :]

    scores, peaks = [], []
    for at, ref in enumerate((w0, w1, w2, w3)):
        part = window_scores(queries, ref[...])
        if at == 0:
            part = jnp.where(key_frames(place, m_ref) <= q_frame, part, NEG)
        scores.append(part)
        peaks.append(jnp.max(part, axis=0, keepdims=True) + bias_ref[at])
    peak = functools.reduce(jnp.maximum, peaks)
    total = jnp.zeros_like(peak)
    for at, part in enumerate(scores):
        total += jnp.sum(jnp.exp2(part - (peak - bias_ref[at])), axis=0, keepdims=True)

    @pl.when(head == 0)
    def _():
        out_ref[...] = jnp.zeros_like(out_ref)

    out_ref[pl.ds(head, 1), :] = peak
    out_ref[pl.ds(8 + head, 1), :] = total


def part_block(half, first):
    return pl.BlockSpec((half, HDIM), lambda h: (0, first + h))


def meta_block(half):
    return pl.BlockSpec((half, HDIM), lambda h: (0, 2 * GROUP))


def key_block(half, first=0):
    return pl.BlockSpec((half, HDIM), lambda h: (0, 2 * (first + h)))


def pair_block(half, first=0):
    return pl.BlockSpec((half, 2 * HDIM), lambda h: (0, first + h))


def whole(shape):
    return pl.BlockSpec(shape, lambda h: (0, 0))


def smem():
    return pl.BlockSpec(memory_space=pltpu.SMEM)


def stats(bias, place, qg, window):
    count, half = qg.shape[0], window[0].shape[0]
    pairs = GROUP * count * 4 * half
    return pl.pallas_call(
        stats_kernel,
        grid=(GROUP,),
        out_shape=jax.ShapeDtypeStruct((16, count), F32),
        in_specs=[smem(), smem(), part_block(count, 0), meta_block(count)]
        + [key_block(half), key_block(half, GROUP), key_block(half), key_block(half)],
        out_specs=whole((16, count)),
        compiler_params=params(),
        cost_estimate=cost(4 * pairs * HDIM, 6 * half * GROUP * HDIM * 2, pairs),
        name="stats",
    )(bias, place, qg, qg, *window)


def log_total(head, own_stats, far_stats):
    own_peak = own_stats[pl.ds(head, 1), :]
    own_sum = own_stats[pl.ds(8 + head, 1), :]
    far_peak = far_stats[pl.ds(head, 1), :]
    far_sum = far_stats[pl.ds(8 + head, 1), :]
    peak = jnp.maximum(own_peak, far_peak)
    own_part = own_sum * jnp.exp2(own_peak - peak)
    return peak + jnp.log2(own_part + far_sum * jnp.exp2(far_peak - peak))


def dot_and_frame(head, meta):
    lane = lax.broadcasted_iota(jnp.int32, meta.shape, 1)
    picked = (lane == head) | (lane == head + LOW_LANE)
    dot_col = jnp.sum(jnp.where(picked, meta, 0.0), axis=1, keepdims=True)
    rows = jnp.where(lane == FRAME_LANE, meta, dot_col).T
    return rows[0:1, :], rows[FRAME_LANE : FRAME_LANE + 1, :]


def block_grads(scores, total, dot, queries, grads, keys, values):
    probs = jnp.exp2(scores - total)
    dv = lax.dot_general(probs.astype(BF16), grads, NN, preferred_element_type=F32)
    dp = lax.dot_general(values, grads, NT, preferred_element_type=F32)
    ds = (probs * (dp - dot)).astype(BF16)
    dk = lax.dot_general(ds, queries, NN, preferred_element_type=F32) * FACTOR
    dq = lax.dot_general(keys.T, ds, NN, preferred_element_type=F32)
    return dq, dk, dv


def earlier_kernel(
    bias_ref, place, own_stats, far_stats, q_ref, g_ref, m_ref, w1, w2, w3, dq_ref, d1, d2, d3
):
    head = pl.program_id(0)
    queries, grads = q_ref[...], g_ref[...]
    dot, _ = dot_and_frame(place[0] * GROUP + head, m_ref[...].astype(F32))
    total = log_total(head, own_stats, far_stats)
    dq_sum = jnp.zeros(dq_ref.shape, F32)
    for at, (ref, out) in enumerate(((w1, d1), (w2, d2), (w3, d3))):
        keys, values = ref[:, :HDIM], ref[:, HDIM:]
        scores = window_scores(queries, keys)
        bound = total - bias_ref[at + 1]
        dq, dk, dv = block_grads(scores, bound, dot, queries, grads, keys, values)
        dq_sum += dq
        out[:, :HDIM] = dk.astype(BF16)
        out[:, HDIM:] = dv.astype(BF16)
    dq_ref[...] = dq_sum


def query_specs(count):
    stat = whole((16, count))
    parts = [part_block(count, 0), part_block(count, GROUP), meta_block(count)]
    return [smem(), stat, stat] + parts


def turned_block(count):
    return pl.BlockSpec((HDIM, count), lambda h: (h, 0))


def earlier(bias, place, own_stats, far_stats, qg, window):
    count, half = qg.shape[0], window[0].shape[0]
    wide = GROUP * HDIM
    pairs = GROUP * count * 3 * half
    return pl.pallas_call(
        earlier_kernel,
        grid=(GROUP,),
        out_shape=[jax.ShapeDtypeStruct((wide, count), F32)]
        + [jax.ShapeDtypeStruct((half, 2 * wide), BF16)] * 3,
        in_specs=[smem()]
        + query_specs(count)
        + [pair_block(half, GROUP), pair_block(half), pair_block(half)],
        out_specs=[turned_block(count)] + [pair_block(half)] * 3,
        compiler_params=params(),
        cost_estimate=cost(10 * pairs * HDIM, 20 * half * wide * 2, pairs),
        name="earlier",
    )(bias, place, own_stats, far_stats, qg, qg, qg, *window)


def same_kernel(
    place, own_stats, far_stats, q_ref, g_ref, m_ref, w0, dq_ref, dq_out, d0
):
    head = pl.program_id(0)
    queries, grads = q_ref[...], g_ref[...]
    meta = m_ref[...].astype(F32)
    dot, q_frame = dot_and_frame(place[0] * GROUP + head, meta)
    total = log_total(head, own_stats, far_stats)
    keys, values = w0[:, :HDIM], w0[:, HDIM:]
    scores = window_scores(queries, keys)
    scores = jnp.where(key_frames(place, m_ref) <= q_frame, scores, NEG)
    dq, dk, dv = block_grads(scores, total, dot, queries, grads, keys, values)
    dq_out[...] = ((dq + dq_ref[...]) * FACTOR).T.astype(BF16)
    d0[:, :HDIM] = dk
    d0[:, HDIM:] = dv


def same(place, own_stats, far_stats, qg, w0, dq):
    count, half = qg.shape[0], w0.shape[0]
    wide = GROUP * HDIM
    pairs = GROUP * count * half
    return pl.pallas_call(
        same_kernel,
        grid=(GROUP,),
        out_shape=[
            jax.ShapeDtypeStruct((count, wide), BF16),
            jax.ShapeDtypeStruct((half, 2 * wide), F32),
        ],
        in_specs=query_specs(count) + [pair_block(half), turned_block(count)],
        out_specs=[part_block(count, 0), pair_block(half)],
        compiler_params=params(),
        cost_estimate=cost(10 * pairs * HDIM, 16 * half * wide * 2, pairs),
        name="same",
    )(place, own_stats, far_stats, qg, qg, qg, w0, dq)


def close_kernel(even_ref, d0, d1, swapped, side, *outs):
    even = even_ref[0].astype(F32)
    tok, wide = outs[0].shape[0], d0.shape[1]
    for step, out in enumerate(outs):
        rows = slice(step * tok, (step + 1) * tok)
        turned = side[rows, :].astype(F32)
        out[:, :wide] = (d0[rows, :] + turned * even).astype(BF16)
        held = d1[rows, :].astype(F32) + swapped[rows, :].astype(F32) + turned * (1.0 - even)
        out[:, wide:] = held.astype(BF16)


def close(even, d0, d1, swapped, side):
    half, wide = d0.shape
    tok = half // XN
    vmem = pl.BlockSpec(memory_space=pltpu.VMEM)
    return pl.pallas_call(
        close_kernel,
        out_shape=[jax.ShapeDtypeStruct((tok, 2 * wide), BF16)] * XN,
        in_specs=[smem()] + [vmem] * 4,
        out_specs=[vmem] * XN,
        compiler_params=params(),
        cost_estimate=cost(6 * half * wide, 14 * half * wide),
        name="close",
    )(even, d0, d1, swapped, side)


def turn_kernel(place, *refs):
    parts, out = refs[:XN], refs[XN]
    for step, part in enumerate(parts):
        for h in range(GROUP):
            cols = head_columns(place, step, h)
            at = 2 * (GROUP + h) * HDIM
            out[0, :, cols] = part[:, at : at + HDIM]
            out[1, :, cols] = part[:, at + HDIM : at + 2 * HDIM]


def turn(place, parts):
    tok = parts[0].shape[0]
    vmem = pl.BlockSpec(memory_space=pltpu.VMEM)
    return pl.pallas_call(
        turn_kernel,
        out_shape=jax.ShapeDtypeStruct((2, tok, HEADS * HDIM), BF16),
        in_specs=[smem()] + [vmem] * XN,
        out_specs=vmem,
        compiler_params=params(),
        cost_estimate=cost(0, 8 * tok * HEADS * HDIM),
        name="turn",
    )(place, *parts)


def unpack_kernel(place, *refs):
    parts, (back, halves, dq, dk, dv) = refs[:XN], refs[XN:]
    wide = GROUP * HDIM
    for group in range(XN):
        total = halves[group].astype(F32) + halves[XN + group].astype(F32)
        dq[:, group * wide : (group + 1) * wide] = total.astype(BF16)
    for step, part in enumerate(parts):
        for h in range(GROUP):
            cols = head_columns(place, step, h)
            at = 2 * h * HDIM
            dk_sum = part[:, at : at + HDIM].astype(F32) + back[0, :, cols].astype(F32)
            dk[:, cols] = dk_sum.astype(BF16)
            dv_sum = part[:, at + HDIM : at + 2 * HDIM].astype(F32) + back[1, :, cols].astype(F32)
            dv[:, cols] = dv_sum.astype(BF16)


def unpack(place, parts, back, halves):
    tok = parts[0].shape[0]
    vmem = pl.BlockSpec(memory_space=pltpu.VMEM)
    return pl.pallas_call(
        unpack_kernel,
        out_shape=[jax.ShapeDtypeStruct((tok, HEADS * HDIM), BF16)] * 3,
        in_specs=[smem()] + [vmem] * (XN + 2),
        out_specs=[vmem] * 3,
        compiler_params=params(),
        cost_estimate=cost(0, 22 * tok * HEADS * HDIM),
        name="unpack",
    )(place, *parts, back, halves)


def over_x(chunks, sign):
    moved = [chunks[0]]
    for step in range(1, XN):
        count = lax.axis_size("col")
        pairs = [(c, c // XN * XN + (c + sign * step) % XN) for c in range(count)]
        moved.append(lax.ppermute(chunks[step], "col", pairs))
    return moved


def across_z(value):
    count = lax.axis_size("col")
    return lax.ppermute(value, "col", [(c, (c + XN) % count) for c in range(count)])


def along_row(value, steps):
    count = lax.axis_size("row")
    first, last = max(0, -steps), min(count, count - steps)
    return lax.ppermute(value, "row", [(r, r + steps) for r in range(first, last)])


def in_chip(value):
    count = lax.axis_size("row")
    return lax.ppermute(value, "row", [(r, r ^ 1) for r in range(count)])


def per_device(query, key, value, saved_out, grad_out, frame_ids):
    row, col = lax.axis_index("row"), lax.axis_index("col")
    place = jnp.stack([col % XN, col // XN]).astype(jnp.int32)
    is_even = row % 2 == 0
    even = is_even.astype(jnp.int32).reshape(1)
    tok = query.shape[0]
    count = lax.axis_size("col") * tok
    wide = 2 * GROUP * HDIM

    far_key, far_value = along_row(key, 2), along_row(value, 2)
    qg = pack_queries(query, saved_out, grad_out, frame_ids[:, None])
    qg = lax.all_to_all(qg, "col", 0, 0).reshape(count, -1)
    near = jnp.concatenate(over_x(pack_keys(place, key, value, far_key, far_value), 1), axis=0)
    w0, w1 = near[:, :wide], near[:, wide:]
    w3 = along_row(jnp.where(is_even, w0, w1), 1)
    w2 = in_chip(w1)
    held = jnp.stack(
        [
            row >= 0,
            row >= 2,
            jnp.where(is_even, row >= 1, row >= 3),
            jnp.where(is_even, row >= 3, row >= 1),
        ]
    )
    bias = jnp.where(held, 0.0, NEG).astype(F32)

    own_stats = stats(bias, place, qg, (near, near, w2, w3))
    far_stats = across_z(own_stats)
    dq_part, d1, d2, d3 = earlier(bias, place, own_stats, far_stats, qg, (near, w2, w3))
    dq, d0 = same(place, own_stats, far_stats, qg, near, dq_part)

    side = along_row(d3, -1)
    halves = lax.all_to_all(dq.reshape(-1, tok, GROUP * HDIM), "col", 0, 0)
    parts = over_x(close(even, d0, d1, in_chip(d2), side), -1)
    back = along_row(turn(place, parts), -2)
    return tuple(unpack(place, parts, back, halves))


def solution(mesh):
    placed = P(("row", "col"), None)
    return jax.shard_map(
        per_device,
        mesh=mesh,
        in_specs=(placed,) * 5 + (P(("row", "col")),),
        out_specs=(placed,) * 3,
        check_vma=False,
    )
```

```python
import functools
import math

import jax
import jax.numpy as jnp
from jax import lax
from jax.experimental import pallas as pl
from jax.experimental.pallas import tpu as pltpu
from jax.sharding import PartitionSpec as P

HEADS = 20
HDIM = 128
XN = 4
GROUP = HEADS // XN
NEG = -1e30
FACTOR = HDIM ** (-0.5)
SCALE2 = FACTOR * math.log2(math.e)
LOW_LANE = 32
FRAME_LANE = 64
BF16 = jnp.bfloat16
F32 = jnp.float32
NT = (((1,), (1,)), ((), ()))
NN = (((1,), (0,)), ((), ()))


def params(room=20):
    return pltpu.CompilerParams(vmem_limit_bytes=room * 1024 * 1024)


def cost(flops, moved, exps=0):
    return pl.CostEstimate(flops=flops, bytes_accessed=moved, transcendentals=exps)


def load_all(sources, held, sems):
    copies = [
        pltpu.make_async_copy(src, held.at[at], sems.at[at]) for at, src in enumerate(sources)
    ]
    for copy in copies:
        copy.start()
    for copy in copies:
        copy.wait()


def pack_queries_kernel(q_any, o_any, g_any, f_ref, out, held, sems):
    load_all((q_any, o_any, g_any), held, sems)
    tok = held.shape[1]
    wide = GROUP * HDIM
    lane = lax.broadcasted_iota(jnp.int32, (tok, HDIM), 1)
    meta = jnp.where(lane == FRAME_LANE, f_ref[...].astype(F32), 0.0)
    for head in range(HEADS):
        cols = slice(head * HDIM, (head + 1) * HDIM)
        product = held[2, :, cols].astype(F32) * held[1, :, cols].astype(F32)
        dot = jnp.sum(product, axis=1, keepdims=True)
        high = dot.astype(BF16).astype(F32)
        meta = jnp.where(lane == head, high, meta)
        meta = jnp.where(lane == LOW_LANE + head, dot - high, meta)
    meta = meta.astype(BF16)
    for group in range(XN):
        here = slice(group * wide, (group + 1) * wide)
        out[group, :, :wide] = held[0, :, here]
        out[group, :, wide : wide + HDIM] = meta
        out[group, :, wide + HDIM :] = held[2, :, here]


def pack_queries(query, saved_out, grad_out, frames):
    tok, width = query.shape
    vmem = pl.BlockSpec(memory_space=pltpu.VMEM)
    shape = (XN, tok, 2 * GROUP * HDIM + HDIM)
    return pl.pallas_call(
        pack_queries_kernel,
        out_shape=jax.ShapeDtypeStruct(shape, BF16),
        in_specs=[pl.BlockSpec(memory_space=pl.ANY)] * 3 + [vmem],
        out_specs=vmem,
        scratch_shapes=[pltpu.VMEM((3, tok, width), BF16), pltpu.SemaphoreType.DMA((3,))],
        compiler_params=params(60),
        cost_estimate=cost(2 * tok * width, 14 * tok * width),
        name="pack_queries",
    )(query, saved_out, grad_out, frames)


def pack_keys_kernel(k_ref, v_ref, k2_ref, v2_ref, out):
    for head in range(HEADS):
        group, h = divmod(head, GROUP)
        cols = slice(head * HDIM, (head + 1) * HDIM)
        for at, ref in enumerate((k_ref, v_ref, k2_ref, v2_ref)):
            first = (2 * (at // 2 * GROUP + h) + at % 2) * HDIM
            out[group, :, first : first + HDIM] = ref[:, cols]


def pack_keys(key, value, far_key, far_value):
    tok, width = key.shape
    vmem = pl.BlockSpec(memory_space=pltpu.VMEM)
    return pl.pallas_call(
        pack_keys_kernel,
        out_shape=jax.ShapeDtypeStruct((XN, tok, 4 * GROUP * HDIM), BF16),
        in_specs=[vmem] * 4,
        out_specs=vmem,
        compiler_params=params(),
        cost_estimate=cost(0, 16 * tok * width),
        name="pack_keys",
    )(key, value, far_key, far_value)


def window_scores(queries, keys):
    return lax.dot_general(keys, queries, NT, preferred_element_type=F32) * SCALE2


def both(own, far):
    return jnp.concatenate([own[...], far[...]], axis=0)


def turn_meta(rows, m_own, m_far):
    @pl.when(pl.program_id(0) == 0)
    def _():
        rows[...] = both(m_own, m_far).astype(F32).T


def seen(rows, m_own):
    k_frame = m_own[...].astype(F32)[:, FRAME_LANE : FRAME_LANE + 1]
    return k_frame <= rows[FRAME_LANE : FRAME_LANE + 1, :]


def stats_kernel(bias_ref, q_own, q_far, m_own, m_far, w0, w1, w2, w3, out_ref, rows):
    head = pl.program_id(0)
    turn_meta(rows, m_own, m_far)
    queries = both(q_own, q_far)

    scores, peaks = [], []
    for at, ref in enumerate((w0, w1, w2, w3)):
        part = window_scores(queries, ref[...])
        if at == 0:
            part = jnp.where(seen(rows, m_own), part, NEG)
        scores.append(part)
        peaks.append(jnp.max(part, axis=0, keepdims=True) + bias_ref[at])
    peak = functools.reduce(jnp.maximum, peaks)
    total = jnp.zeros_like(peak)
    for at, part in enumerate(scores):
        total += jnp.sum(jnp.exp2(part - (peak - bias_ref[at])), axis=0, keepdims=True)

    @pl.when(head == 0)
    def _():
        out_ref[...] = jnp.zeros_like(out_ref)

    out_ref[pl.ds(head, 1), :] = peak
    out_ref[pl.ds(8 + head, 1), :] = total


def head_block(half):
    return pl.BlockSpec((half, HDIM), lambda h: (0, h))


def meta_block(half):
    return pl.BlockSpec((half, HDIM), lambda h: (0, GROUP))


def key_block(half, first=0):
    return pl.BlockSpec((half, HDIM), lambda h: (0, 2 * (first + h)))


def pair_block(half, first=0):
    return pl.BlockSpec((half, 2 * HDIM), lambda h: (0, first + h))


def turned_block(half):
    return pl.BlockSpec((HDIM, 2 * half), lambda h: (h, 0))


def whole(shape):
    return pl.BlockSpec(shape, lambda h: (0, 0))


def smem():
    return pl.BlockSpec(memory_space=pltpu.SMEM)


def meta_rows(half):
    return [pltpu.VMEM((HDIM, 2 * half), F32)]


def stats(bias, q_own, q_far, near, w2, w3):
    half = q_own.shape[0]
    pairs = GROUP * 2 * half * 4 * half
    return pl.pallas_call(
        stats_kernel,
        grid=(GROUP,),
        out_shape=jax.ShapeDtypeStruct((16, 2 * half), F32),
        in_specs=[smem(), head_block(half), head_block(half), meta_block(half), meta_block(half)]
        + [key_block(half), key_block(half, GROUP), key_block(half), key_block(half)],
        out_specs=whole((16, 2 * half)),
        scratch_shapes=meta_rows(half),
        compiler_params=params(),
        cost_estimate=cost(4 * pairs * HDIM, 6 * half * GROUP * HDIM * 2, pairs),
        name="stats",
    )(bias, q_own, q_far, q_own, q_far, near, near, w2, w3)


def log_total(head, half, own_stats, far_stats):
    own_peak = own_stats[pl.ds(head, 1), :]
    own_sum = own_stats[pl.ds(8 + head, 1), :]
    far_peak = far_stats[pl.ds(head, 1), :]
    far_sum = far_stats[pl.ds(8 + head, 1), :]
    far_peak = jnp.concatenate([far_peak[:, half:], far_peak[:, :half]], axis=1)
    far_sum = jnp.concatenate([far_sum[:, half:], far_sum[:, :half]], axis=1)
    peak = jnp.maximum(own_peak, far_peak)
    own_part = own_sum * jnp.exp2(own_peak - peak)
    return peak + jnp.log2(own_part + far_sum * jnp.exp2(far_peak - peak))


def block_grads(scores, total, dot, queries, grads, keys, values):
    probs = jnp.exp2(scores - total)
    dv = lax.dot_general(probs.astype(BF16), grads, NN, preferred_element_type=F32)
    dp = lax.dot_general(values, grads, NT, preferred_element_type=F32)
    ds = (probs * (dp - dot)).astype(BF16)
    dk = lax.dot_general(ds, queries, NN, preferred_element_type=F32) * FACTOR
    dq = lax.dot_general(keys.T, ds, NN, preferred_element_type=F32)
    return dq, dk, dv


def grads_kernel(
    roles, bias_ref, place, own_stats, far_stats, q_own, q_far, g_own, g_far, m_own, m_far, *rest
):
    *rest, rows = rest
    blocks, rest = rest[: len(roles)], rest[len(roles) :]
    head = pl.program_id(0)
    half = q_own.shape[0]
    turn_meta(rows, m_own, m_far)
    queries, grads = both(q_own, q_far), both(g_own, g_far)
    first = place[0] * GROUP + head
    dot = rows[pl.ds(first, 1), :] + rows[pl.ds(LOW_LANE + first, 1), :]
    total = log_total(head, half, own_stats, far_stats)
    if 0 in roles:
        dq_part, dq_own, dq_far, *outs = rest
        dq_sum = dq_part[...]
    else:
        dq_part, *outs = rest
        dq_sum = jnp.zeros(dq_part.shape, F32)
    for role, ref, out in zip(roles, blocks, outs):
        keys, values = ref[:, :HDIM], ref[:, HDIM:]
        scores = window_scores(queries, keys)
        if role == 0:
            scores = jnp.where(seen(rows, m_own), scores, NEG)
        bound = total - bias_ref[role]
        dq, dk, dv = block_grads(scores, bound, dot, queries, grads, keys, values)
        dq_sum += dq
        out[:, :HDIM] = dk.astype(out.dtype)
        out[:, HDIM:] = dv.astype(out.dtype)
    if 0 in roles:
        turned = (dq_sum * FACTOR).T
        dq_own[...] = turned[:half]
        dq_far[...] = turned[half:].astype(BF16)
    else:
        dq_part[...] = dq_sum


def grads(bias, place, own_stats, far_stats, q, g, roles, blocks, dq_part=None):
    half = q[0].shape[0]
    wide = GROUP * HDIM
    head, meta = head_block(half), meta_block(half)
    stat = whole((16, 2 * half))
    pairs = GROUP * 2 * half * len(roles) * half
    specs = [pair_block(half, GROUP if role == 1 else 0) for role in roles]
    turned = jax.ShapeDtypeStruct((wide, 2 * half), F32)
    outs = [
        jax.ShapeDtypeStruct((half, 2 * wide), F32 if role == 0 else BF16) for role in roles
    ]
    if 0 in roles:
        extra, extra_specs = [dq_part], [turned_block(half)]
        dq_outs = [
            jax.ShapeDtypeStruct((half, wide), F32),
            jax.ShapeDtypeStruct((half, wide), BF16),
        ]
        dq_specs = [head, head]
    else:
        extra, extra_specs = [], []
        dq_outs, dq_specs = [turned], [turned_block(half)]
    return pl.pallas_call(
        functools.partial(grads_kernel, roles),
        grid=(GROUP,),
        out_shape=dq_outs + outs,
        in_specs=[smem(), smem(), stat, stat, head, head, head, head, meta, meta]
        + specs
        + extra_specs,
        out_specs=dq_specs + [pair_block(half)] * len(roles),
        scratch_shapes=meta_rows(half),
        compiler_params=params(),
        cost_estimate=cost(10 * pairs * HDIM, 18 * half * wide * 2, pairs),
        name="grads" + "".join(str(role) for role in roles),
    )(bias, place, own_stats, far_stats, *q, *g, *q, *blocks, *extra)


def fold_kernel(even_ref, d1, swapped, side, out):
    odd = 1.0 - even_ref[0].astype(F32)
    total = d1[...].astype(F32) + swapped[...].astype(F32) + side[...].astype(F32) * odd
    out[...] = total.astype(BF16)


def fold(even, d1, swapped, side):
    vmem = pl.BlockSpec(memory_space=pltpu.VMEM)
    return pl.pallas_call(
        fold_kernel,
        out_shape=jax.ShapeDtypeStruct(d1.shape, BF16),
        in_specs=[smem()] + [vmem] * 3,
        out_specs=vmem,
        compiler_params=params(),
        cost_estimate=cost(3 * d1.size, 8 * d1.size),
        name="fold",
    )(even, d1, swapped, side)


def close_kernel(even_ref, dq_own, dq_far, d0, back, side, out):
    even = even_ref[0].astype(F32)
    tok = out.shape[1]
    wide = dq_own.shape[1]
    for step in range(XN):
        rows = slice(step * tok, (step + 1) * tok)
        grad_q = dq_own[rows, :] + dq_far[rows, :].astype(F32)
        pair = d0[rows, :] + back[rows, :].astype(F32) + side[rows, :].astype(F32) * even
        out[step, :, :wide] = grad_q.astype(BF16)
        out[step, :, wide:] = pair.astype(BF16)


def close(even, dq_own, dq_far, d0, back, side):
    half, wide = dq_own.shape
    tok = half // XN
    vmem = pl.BlockSpec(memory_space=pltpu.VMEM)
    return pl.pallas_call(
        close_kernel,
        out_shape=jax.ShapeDtypeStruct((XN, tok, 3 * wide), BF16),
        in_specs=[smem()] + [vmem] * 5,
        out_specs=vmem,
        compiler_params=params(),
        cost_estimate=cost(5 * half * wide, 28 * half * wide),
        name="close",
    )(even, dq_own, dq_far, d0, back, side)


def unpack_kernel(parts, dq, dk, dv):
    wide = GROUP * HDIM
    for group in range(XN):
        dq[:, group * wide : (group + 1) * wide] = parts[group, :, :wide]
        for h in range(GROUP):
            at = wide + 2 * h * HDIM
            cols = slice((group * GROUP + h) * HDIM, (group * GROUP + h + 1) * HDIM)
            dk[:, cols] = parts[group, :, at : at + HDIM]
            dv[:, cols] = parts[group, :, at + HDIM : at + 2 * HDIM]


def unpack(parts):
    tok = parts.shape[1]
    vmem = pl.BlockSpec(memory_space=pltpu.VMEM)
    return pl.pallas_call(
        unpack_kernel,
        out_shape=[jax.ShapeDtypeStruct((tok, HEADS * HDIM), BF16)] * 3,
        in_specs=[vmem],
        out_specs=[vmem] * 3,
        compiler_params=params(),
        cost_estimate=cost(0, 12 * tok * HEADS * HDIM),
        name="unpack",
    )(parts)


def over_x(value):
    groups = [[z * XN + x for x in range(XN)] for z in range(lax.axis_size("col") // XN)]
    return lax.all_to_all(value, "col", 0, 0, axis_index_groups=groups)


def across_z(value):
    count = lax.axis_size("col")
    return lax.ppermute(value, "col", [(c, (c + XN) % count) for c in range(count)])


def along_row(value, steps):
    count = lax.axis_size("row")
    first, last = max(0, -steps), min(count, count - steps)
    return lax.ppermute(value, "row", [(r, r + steps) for r in range(first, last)])


def in_chip(value):
    count = lax.axis_size("row")
    return lax.ppermute(value, "row", [(r, r ^ 1) for r in range(count)])


def per_device(query, key, value, saved_out, grad_out, frame_ids):
    row, col = lax.axis_index("row"), lax.axis_index("col")
    place = (col % XN).astype(jnp.int32).reshape(1)
    is_even = row % 2 == 0
    even = is_even.astype(jnp.int32).reshape(1)
    half = query.shape[0] * XN
    wide = GROUP * HDIM

    far_key, far_value = along_row(key, 2), along_row(value, 2)
    qg = over_x(pack_queries(query, saved_out, grad_out, frame_ids[:, None]))
    q_own = qg[:, :, : wide + HDIM].reshape(half, wide + HDIM)
    g_own = qg[:, :, wide + HDIM :].reshape(half, wide)
    q_far = across_z(q_own)
    near = over_x(pack_keys(key, value, far_key, far_value)).reshape(half, -1)
    near, q_far, g_own = lax.optimization_barrier((near, q_far, g_own))
    w0, w1 = near[:, : 2 * wide], near[:, 2 * wide :]
    w3 = along_row(jnp.where(is_even, w0, w1), 1)
    w2 = in_chip(w1)
    g_far = across_z(g_own)
    held = jnp.stack(
        [
            row >= 0,
            row >= 2,
            jnp.where(is_even, row >= 1, row >= 3),
            jnp.where(is_even, row >= 3, row >= 1),
        ]
    )
    bias = jnp.where(held, 0.0, NEG).astype(F32)

    own_stats = stats(bias, q_own, q_far, near, w2, w3)
    far_stats = across_z(own_stats)
    common = (bias, place, own_stats, far_stats, (q_own, q_far), (g_own, g_far))
    dq_part, d2, d3 = grads(*common, (2, 3), (w2, w3))
    dq_own, dq_far, d0, d1 = grads(*common, (0, 1), (near, near), dq_part)

    side = along_row(d3, -1)
    back = along_row(fold(even, d1, in_chip(d2), side), -2)
    dq_far = across_z(dq_far)
    return tuple(unpack(over_x(close(even, dq_own, dq_far, d0, back, side))))


def solution(mesh):
    placed = P(("row", "col"), None)
    return jax.shard_map(
        per_device,
        mesh=mesh,
        in_specs=(placed,) * 5 + (P(("row", "col")),),
        out_specs=(placed,) * 3,
        check_vma=False,
    )
```

```python
import functools
import math

import jax
import jax.numpy as jnp
from jax import lax
from jax.experimental import pallas as pl
from jax.experimental.pallas import tpu as pltpu
from jax.sharding import PartitionSpec as P

HEADS = 20
HDIM = 128
XN = 4
GROUP = HEADS // XN
NEG = -1e30
FACTOR = HDIM ** (-0.5)
SCALE2 = FACTOR * math.log2(math.e)
LOW_LANE = 32
FRAME_LANE = 64
BF16 = jnp.bfloat16
F32 = jnp.float32
NT = (((1,), (1,)), ((), ()))
NN = (((1,), (0,)), ((), ()))


def params(room=20):
    return pltpu.CompilerParams(vmem_limit_bytes=room * 1024 * 1024)


def cost(flops, moved, exps=0):
    return pl.CostEstimate(flops=flops, bytes_accessed=moved, transcendentals=exps)


def load_all(sources, held, sems):
    copies = [
        pltpu.make_async_copy(src, held.at[at], sems.at[at]) for at, src in enumerate(sources)
    ]
    for copy in copies:
        copy.start()
    for copy in copies:
        copy.wait()


def pack_queries_kernel(q_any, o_any, g_any, f_ref, out, held, sems):
    load_all((q_any, o_any, g_any), held, sems)
    tok = held.shape[1]
    wide = GROUP * HDIM
    lane = lax.broadcasted_iota(jnp.int32, (tok, HDIM), 1)
    meta = jnp.where(lane == FRAME_LANE, f_ref[...].astype(F32), 0.0)
    for head in range(HEADS):
        cols = slice(head * HDIM, (head + 1) * HDIM)
        product = held[2, :, cols].astype(F32) * held[1, :, cols].astype(F32)
        dot = jnp.sum(product, axis=1, keepdims=True)
        high = dot.astype(BF16).astype(F32)
        meta = jnp.where(lane == head, high, meta)
        meta = jnp.where(lane == LOW_LANE + head, dot - high, meta)
    meta = meta.astype(BF16)
    for group in range(XN):
        here = slice(group * wide, (group + 1) * wide)
        out[group, :, :wide] = held[0, :, here]
        out[group, :, wide : 2 * wide] = held[2, :, here]
        out[group, :, 2 * wide :] = meta


def pack_queries(query, saved_out, grad_out, frames):
    tok, width = query.shape
    vmem = pl.BlockSpec(memory_space=pltpu.VMEM)
    shape = (XN, tok, 2 * GROUP * HDIM + HDIM)
    return pl.pallas_call(
        pack_queries_kernel,
        out_shape=jax.ShapeDtypeStruct(shape, BF16),
        in_specs=[pl.BlockSpec(memory_space=pl.ANY)] * 3 + [vmem],
        out_specs=vmem,
        scratch_shapes=[pltpu.VMEM((3, tok, width), BF16), pltpu.SemaphoreType.DMA((3,))],
        compiler_params=params(60),
        cost_estimate=cost(2 * tok * width, 14 * tok * width),
        name="pack_queries",
    )(query, saved_out, grad_out, frames)


def pack_keys_kernel(near, far, out):
    for head in range(HEADS):
        group, h = divmod(head, GROUP)
        cols = slice(head * HDIM, (head + 1) * HDIM)
        for block, ref in enumerate((near, far)):
            for at in range(2):
                first = (2 * (block * GROUP + h) + at) * HDIM
                out[group, :, first : first + HDIM] = ref[at, :, cols]


def pack_keys(near, far):
    _, tok, width = near.shape
    vmem = pl.BlockSpec(memory_space=pltpu.VMEM)
    return pl.pallas_call(
        pack_keys_kernel,
        out_shape=jax.ShapeDtypeStruct((XN, tok, 4 * GROUP * HDIM), BF16),
        in_specs=[vmem] * 2,
        out_specs=vmem,
        compiler_params=params(),
        cost_estimate=cost(0, 16 * tok * width),
        name="pack_keys",
    )(near, far)


def window_scores(queries, keys):
    return lax.dot_general(keys, queries, NT, preferred_element_type=F32) * SCALE2


def both(own, far):
    return jnp.concatenate([own[...], far[...]], axis=0)


def turn_meta(rows, m_own, m_far):
    @pl.when(pl.program_id(0) == 0)
    def _():
        rows[...] = both(m_own, m_far).astype(F32).T


def seen(rows, m_own):
    k_frame = m_own[...].astype(F32)[:, FRAME_LANE : FRAME_LANE + 1]
    return k_frame <= rows[FRAME_LANE : FRAME_LANE + 1, :]


def stats_kernel(bias_ref, q_own, q_far, m_own, m_far, w0, w1, w2, w3, out_ref, rows):
    head = pl.program_id(0)
    turn_meta(rows, m_own, m_far)
    queries = both(q_own, q_far)

    scores, peaks = [], []
    for at, ref in enumerate((w0, w1, w2, w3)):
        part = window_scores(queries, ref[...])
        if at == 0:
            part = jnp.where(seen(rows, m_own), part, NEG)
        scores.append(part)
        peaks.append(jnp.max(part, axis=0, keepdims=True) + bias_ref[at])
    peak = functools.reduce(jnp.maximum, peaks)
    total = jnp.zeros_like(peak)
    for at, part in enumerate(scores):
        total += jnp.sum(jnp.exp2(part - (peak - bias_ref[at])), axis=0, keepdims=True)

    @pl.when(head == 0)
    def _():
        out_ref[...] = jnp.zeros_like(out_ref)

    out_ref[pl.ds(head, 1), :] = peak
    out_ref[pl.ds(8 + head, 1), :] = total


def head_block(half, first=0):
    return pl.BlockSpec((half, HDIM), lambda h: (0, first + h))


def meta_block(half):
    return pl.BlockSpec((half, HDIM), lambda h: (0, 2 * GROUP))


def key_block(half, first=0):
    return pl.BlockSpec((half, HDIM), lambda h: (0, 2 * (first + h)))


def pair_block(half, first=0):
    return pl.BlockSpec((half, 2 * HDIM), lambda h: (0, first + h))


def turned_block(half):
    return pl.BlockSpec((HDIM, 2 * half), lambda h: (h, 0))


def whole(shape):
    return pl.BlockSpec(shape, lambda h: (0, 0))


def smem():
    return pl.BlockSpec(memory_space=pltpu.SMEM)


def meta_rows(half):
    return [pltpu.VMEM((HDIM, 2 * half), F32)]


def stats(bias, own, far, near, w2, w3):
    half = own.shape[0]
    pairs = GROUP * 2 * half * 4 * half
    return pl.pallas_call(
        stats_kernel,
        grid=(GROUP,),
        out_shape=jax.ShapeDtypeStruct((16, 2 * half), F32),
        in_specs=[smem(), head_block(half), head_block(half), meta_block(half), meta_block(half)]
        + [key_block(half), key_block(half, GROUP), key_block(half), key_block(half)],
        out_specs=whole((16, 2 * half)),
        scratch_shapes=meta_rows(half),
        compiler_params=params(),
        cost_estimate=cost(4 * pairs * HDIM, 6 * half * GROUP * HDIM * 2, pairs),
        name="stats",
    )(bias, own, far, own, far, near, near, w2, w3)


def log_total(head, half, own_stats, far_stats):
    own_peak = own_stats[pl.ds(head, 1), :]
    own_sum = own_stats[pl.ds(8 + head, 1), :]
    far_peak = far_stats[pl.ds(head, 1), :]
    far_sum = far_stats[pl.ds(8 + head, 1), :]
    far_peak = jnp.concatenate([far_peak[:, half:], far_peak[:, :half]], axis=1)
    far_sum = jnp.concatenate([far_sum[:, half:], far_sum[:, :half]], axis=1)
    peak = jnp.maximum(own_peak, far_peak)
    own_part = own_sum * jnp.exp2(own_peak - peak)
    return peak + jnp.log2(own_part + far_sum * jnp.exp2(far_peak - peak))


def block_grads(scores, total, dot, queries, grads, keys, values):
    probs = jnp.exp2(scores - total)
    dv = lax.dot_general(probs.astype(BF16), grads, NN, preferred_element_type=F32)
    dp = lax.dot_general(values, grads, NT, preferred_element_type=F32)
    ds = (probs * (dp - dot)).astype(BF16)
    dk = lax.dot_general(ds, queries, NN, preferred_element_type=F32) * FACTOR
    dq = lax.dot_general(keys.T, ds, NN, preferred_element_type=F32)
    return dq, dk, dv


def grads_kernel(
    roles, bias_ref, place, own_stats, far_stats, q_own, q_far, g_own, g_far, m_own, m_far, *rest
):
    *rest, rows = rest
    blocks, rest = rest[: len(roles)], rest[len(roles) :]
    head = pl.program_id(0)
    half = q_own.shape[0]
    turn_meta(rows, m_own, m_far)
    queries, grads = both(q_own, q_far), both(g_own, g_far)
    first = place[0] * GROUP + head
    dot = rows[pl.ds(first, 1), :] + rows[pl.ds(LOW_LANE + first, 1), :]
    total = log_total(head, half, own_stats, far_stats)
    if 3 in roles:
        dq_out, *outs = rest
        dq_sum = jnp.zeros(dq_out.shape, F32)
    else:
        dq_part, dq_out, *outs = rest
        dq_sum = dq_part[...]
    for role, ref, out in zip(roles, blocks, outs):
        keys, values = ref[:, :HDIM], ref[:, HDIM:]
        scores = window_scores(queries, keys)
        if role == 0:
            scores = jnp.where(seen(rows, m_own), scores, NEG)
        bound = total - bias_ref[role]
        dq, dk, dv = block_grads(scores, bound, dot, queries, grads, keys, values)
        dq_sum += dq
        out[:, :HDIM] = dk.astype(out.dtype)
        out[:, HDIM:] = dv.astype(out.dtype)
    if 0 in roles:
        turned = (dq_sum * FACTOR).T.astype(BF16)
        near_rows = pl.multiple_of(place[1] * half, half)
        far_rows = pl.multiple_of((1 - place[1]) * half, half)
        dq_out[pl.ds(near_rows, half), :] = turned[:half]
        dq_out[pl.ds(far_rows, half), :] = turned[half:]
    else:
        dq_out[...] = dq_sum


def grads(bias, place, own_stats, far_stats, own, far, roles, blocks, dq_part=None):
    half = own.shape[0]
    wide = GROUP * HDIM
    query, cotangent, meta = head_block(half), head_block(half, GROUP), meta_block(half)
    stat = whole((16, 2 * half))
    pairs = GROUP * 2 * half * len(roles) * half
    specs = [pair_block(half, GROUP if role == 1 else 0) for role in roles]
    outs = [
        jax.ShapeDtypeStruct((half, 2 * wide), F32 if role == 0 else BF16) for role in roles
    ]
    extra = [] if dq_part is None else [dq_part]
    if 0 in roles:
        dq_out = jax.ShapeDtypeStruct((2 * half, wide), BF16)
        dq_spec = head_block(2 * half)
    else:
        dq_out, dq_spec = jax.ShapeDtypeStruct((wide, 2 * half), F32), turned_block(half)
    return pl.pallas_call(
        functools.partial(grads_kernel, roles),
        grid=(GROUP,),
        out_shape=[dq_out] + outs,
        in_specs=[smem(), smem(), stat, stat, query, query, cotangent, cotangent, meta, meta]
        + specs
        + [turned_block(half)] * len(extra),
        out_specs=[dq_spec] + [pair_block(half)] * len(roles),
        scratch_shapes=meta_rows(half),
        compiler_params=params(),
        cost_estimate=cost(10 * pairs * HDIM, 18 * half * wide * 2, pairs),
        name="grads" + "".join(str(role) for role in roles),
    )(bias, place, own_stats, far_stats, own, far, own, far, own, far, *blocks, *extra)


def fold_kernel(even_ref, d1, swapped, side, out):
    odd = 1.0 - even_ref[0].astype(F32)
    total = d1[...].astype(F32) + swapped[...].astype(F32) + side[...].astype(F32) * odd
    out[...] = total.astype(BF16)


def fold(even, d1, swapped, side):
    vmem = pl.BlockSpec(memory_space=pltpu.VMEM)
    return pl.pallas_call(
        fold_kernel,
        out_shape=jax.ShapeDtypeStruct(d1.shape, BF16),
        in_specs=[smem()] + [vmem] * 3,
        out_specs=vmem,
        compiler_params=params(),
        cost_estimate=cost(3 * d1.size, 8 * d1.size),
        name="fold",
    )(even, d1, swapped, side)


def close_kernel(even_ref, d0, back, side, out):
    even = even_ref[0].astype(F32)
    tok = out.shape[1]
    for step in range(XN):
        rows = slice(step * tok, (step + 1) * tok)
        pair = d0[rows, :] + back[rows, :].astype(F32) + side[rows, :].astype(F32) * even
        out[step] = pair.astype(BF16)


def close(even, d0, back, side):
    half, wide = d0.shape
    tok = half // XN
    vmem = pl.BlockSpec(memory_space=pltpu.VMEM)
    return pl.pallas_call(
        close_kernel,
        out_shape=jax.ShapeDtypeStruct((XN, tok, wide), BF16),
        in_specs=[smem()] + [vmem] * 3,
        out_specs=vmem,
        compiler_params=params(),
        cost_estimate=cost(3 * half * wide, 10 * half * wide),
        name="close",
    )(even, d0, back, side)


def unpack_kernel(parts, halves, dq, dk, dv):
    wide = GROUP * HDIM
    for group in range(XN):
        total = halves[group].astype(F32) + halves[XN + group].astype(F32)
        dq[:, group * wide : (group + 1) * wide] = total.astype(BF16)
        for h in range(GROUP):
            at = 2 * h * HDIM
            cols = slice((group * GROUP + h) * HDIM, (group * GROUP + h + 1) * HDIM)
            dk[:, cols] = parts[group, :, at : at + HDIM]
            dv[:, cols] = parts[group, :, at + HDIM : at + 2 * HDIM]


def unpack(parts, halves):
    tok = parts.shape[1]
    vmem = pl.BlockSpec(memory_space=pltpu.VMEM)
    return pl.pallas_call(
        unpack_kernel,
        out_shape=[jax.ShapeDtypeStruct((tok, HEADS * HDIM), BF16)] * 3,
        in_specs=[vmem] * 2,
        out_specs=[vmem] * 3,
        compiler_params=params(),
        cost_estimate=cost(0, 14 * tok * HEADS * HDIM),
        name="unpack",
    )(parts, halves)


def over_x(value):
    groups = [[z * XN + x for x in range(XN)] for z in range(lax.axis_size("col") // XN)]
    return lax.all_to_all(value, "col", 0, 0, axis_index_groups=groups)


def across_z(value):
    count = lax.axis_size("col")
    return lax.ppermute(value, "col", [(c, (c + XN) % count) for c in range(count)])


def along_row(value, steps):
    count = lax.axis_size("row")
    first, last = max(0, -steps), min(count, count - steps)
    return lax.ppermute(value, "row", [(r, r + steps) for r in range(first, last)])


def in_chip(value):
    count = lax.axis_size("row")
    return lax.ppermute(value, "row", [(r, r ^ 1) for r in range(count)])


def per_device(query, key, value, saved_out, grad_out, frame_ids):
    row, col = lax.axis_index("row"), lax.axis_index("col")
    place = jnp.stack([col % XN, col // XN]).astype(jnp.int32)
    is_even = row % 2 == 0
    even = is_even.astype(jnp.int32).reshape(1)
    tok = query.shape[0]
    half = XN * tok
    wide = 2 * GROUP * HDIM

    kv = jnp.stack([key, value])
    kv_far = along_row(kv, 2)
    own = over_x(pack_queries(query, saved_out, grad_out, frame_ids[:, None])).reshape(half, -1)
    far = across_z(own)
    near = over_x(pack_keys(kv, kv_far)).reshape(half, -1)
    w0, w1 = near[:, :wide], near[:, wide:]
    w3 = along_row(jnp.where(is_even, w0, w1), 1)
    w2 = in_chip(w1)
    held = jnp.stack(
        [
            row >= 0,
            row >= 2,
            jnp.where(is_even, row >= 1, row >= 3),
            jnp.where(is_even, row >= 3, row >= 1),
        ]
    )
    bias = jnp.where(held, 0.0, NEG).astype(F32)

    own_stats = stats(bias, own, far, near, w2, w3)
    common = (bias, place, own_stats, across_z(own_stats), own, far)
    dq_part, d2, d3 = grads(*common, (2, 3), (w2, w3))
    side, swapped = along_row(d3, -1), in_chip(d2)
    dq_part, d1 = grads(*common, (1,), (near,), dq_part)
    held = fold(even, d1, swapped, side)
    back = along_row(held, -2)
    dq_part, held = lax.optimization_barrier((dq_part, held))
    dq, d0 = grads(*common, (0,), (near,), dq_part)
    halves = lax.all_to_all(dq.reshape(-1, tok, GROUP * HDIM), "col", 0, 0)
    return tuple(unpack(over_x(close(even, d0, back, side)), halves))


def solution(mesh):
    placed = P(("row", "col"), None)
    return jax.shard_map(
        per_device,
        mesh=mesh,
        in_specs=(placed,) * 5 + (P(("row", "col")),),
        out_specs=(placed,) * 3,
        check_vma=False,
    )
```

```python
import functools
import math

import jax
import jax.numpy as jnp
from jax import lax
from jax.experimental import pallas as pl
from jax.experimental.pallas import tpu as pltpu
from jax.sharding import PartitionSpec as P

HEADS = 20
HDIM = 128
XN = 4
GROUP = HEADS // XN
NEG = -1e30
FACTOR = HDIM ** (-0.5)
SCALE2 = FACTOR * math.log2(math.e)
LOW_LANE = 32
FRAME_LANE = 64
BF16 = jnp.bfloat16
F32 = jnp.float32


def params(room=20):
    return pltpu.CompilerParams(vmem_limit_bytes=room * 1024 * 1024)


def cost(flops, moved, exps=0):
    return pl.CostEstimate(flops=flops, bytes_accessed=moved, transcendentals=exps)


def load_all(sources, held, sems):
    copies = [
        pltpu.make_async_copy(src, held.at[at], sems.at[at]) for at, src in enumerate(sources)
    ]
    for copy in copies:
        copy.start()
    for copy in copies:
        copy.wait()


def pack_queries_kernel(q_any, o_any, g_any, f_ref, out, held, sems):
    load_all((q_any, o_any, g_any), held, sems)
    tok = held.shape[1]
    wide = GROUP * HDIM
    lane = lax.broadcasted_iota(jnp.int32, (tok, HDIM), 1)
    meta = jnp.where(lane == FRAME_LANE, f_ref[...].astype(F32), 0.0)
    for head in range(HEADS):
        cols = slice(head * HDIM, (head + 1) * HDIM)
        product = held[2, :, cols].astype(F32) * held[1, :, cols].astype(F32)
        dot = jnp.sum(product, axis=1, keepdims=True)
        high = dot.astype(BF16).astype(F32)
        meta = jnp.where(lane == head, high, meta)
        meta = jnp.where(lane == LOW_LANE + head, dot - high, meta)
    meta = meta.astype(BF16)
    for group in range(XN):
        here = slice(group * wide, (group + 1) * wide)
        out[group, :, :wide] = held[0, :, here]
        out[group, :, wide : 2 * wide] = held[2, :, here]
        out[group, :, 2 * wide :] = meta


def pack_queries(query, saved_out, grad_out, frames):
    tok, width = query.shape
    shape = (XN, tok, 2 * GROUP * HDIM + HDIM)
    return pl.pallas_call(
        pack_queries_kernel,
        out_shape=jax.ShapeDtypeStruct(shape, BF16),
        in_specs=[pl.BlockSpec(memory_space=pl.ANY)] * 3 + [vmem()],
        out_specs=vmem(),
        scratch_shapes=[pltpu.VMEM((3, tok, width), BF16), pltpu.SemaphoreType.DMA((3,))],
        compiler_params=params(60),
        cost_estimate=cost(2 * tok * width, 14 * tok * width),
        name="pack_queries",
    )(query, saved_out, grad_out, frames)


def pack_keys_kernel(near, far, out):
    for head in range(HEADS):
        group, h = divmod(head, GROUP)
        cols = slice(head * HDIM, (head + 1) * HDIM)
        for block, ref in enumerate((near, far)):
            for at in range(2):
                first = (2 * (block * GROUP + h) + at) * HDIM
                out[group, :, first : first + HDIM] = ref[at, :, cols]


def pack_keys(near, far):
    _, tok, width = near.shape
    return pl.pallas_call(
        pack_keys_kernel,
        out_shape=jax.ShapeDtypeStruct((XN, tok, 4 * GROUP * HDIM), BF16),
        in_specs=[vmem()] * 2,
        out_specs=vmem(),
        compiler_params=params(),
        cost_estimate=cost(0, 16 * tok * width),
        name="pack_keys",
    )(near, far)


def both(own, far, cols):
    return jnp.concatenate([own[:, cols], far[:, cols]], axis=0)


META = slice(2 * GROUP * HDIM, (2 * GROUP + 1) * HDIM)


def head_slice(at):
    return slice(at * HDIM, (at + 1) * HDIM)


def seen(rows, own):
    k_frame = own[:, META].astype(F32)[:, FRAME_LANE : FRAME_LANE + 1]
    return k_frame <= rows[FRAME_LANE : FRAME_LANE + 1, :]


def stats_kernel(bias_ref, own, far, near, w2, w3, out_ref):
    half = own.shape[0]
    rows = both(own, far, META).astype(F32).T
    mask = seen(rows, own)
    out_ref[...] = jnp.zeros_like(out_ref)
    for head in range(GROUP):
        queries = both(own, far, head_slice(head)).T
        at = head_slice(2 * head)
        keys = [near[:, at], near[:, head_slice(2 * (GROUP + head))], w2[:, at], w3[:, at]]
        scores = jnp.dot(
            jnp.concatenate(keys, axis=0), queries, preferred_element_type=F32
        ) * SCALE2
        parts = [scores[role * half : (role + 1) * half] for role in range(4)]
        parts[0] = jnp.where(mask, parts[0], NEG)
        peaks = [
            jnp.max(part, axis=0, keepdims=True) + bias_ref[role]
            for role, part in enumerate(parts)
        ]
        peak = functools.reduce(jnp.maximum, peaks)
        total = jnp.zeros_like(peak)
        for role, part in enumerate(parts):
            total += jnp.sum(jnp.exp2(part - (peak - bias_ref[role])), axis=0, keepdims=True)
        out_ref[head : head + 1, :] = peak
        out_ref[8 + head : 9 + head, :] = total


def smem():
    return pl.BlockSpec(memory_space=pltpu.SMEM)


def vmem():
    return pl.BlockSpec(memory_space=pltpu.VMEM)


def stats(bias, own, far, near, w2, w3):
    half = own.shape[0]
    pairs = GROUP * 2 * half * 4 * half
    return pl.pallas_call(
        stats_kernel,
        out_shape=jax.ShapeDtypeStruct((16, 2 * half), F32),
        in_specs=[smem()] + [vmem()] * 5,
        out_specs=vmem(),
        compiler_params=params(),
        cost_estimate=cost(4 * pairs * HDIM, 6 * half * GROUP * HDIM * 2, pairs),
        name="stats",
    )(bias, own, far, near, w2, w3)


def log_total(own_stats, far_stats):
    half = own_stats.shape[1] // 2
    turned = jnp.concatenate([far_stats[:, half:], far_stats[:, :half]], axis=1)
    own_peak, own_sum = own_stats[:8, :], own_stats[8:, :]
    far_peak, far_sum = turned[:8], turned[8:]
    peak = jnp.maximum(own_peak, far_peak)
    own_part = own_sum * jnp.exp2(own_peak - peak)
    return peak + jnp.log2(own_part + far_sum * jnp.exp2(far_peak - peak))


def grads_kernel(roles, bias_ref, place, own_stats, far_stats, own, far, *rest):
    *rest, rows = rest
    blocks, rest = rest[: len(roles)], rest[len(roles) :]
    if 3 in roles:
        dq_out, *outs = rest
    else:
        dq_part, dq_out, *outs = rest
    half = own.shape[0]
    rows[...] = both(own, far, META).astype(F32).T
    totals = log_total(own_stats, far_stats)
    for head in range(GROUP):
        q_cols, g_cols = head_slice(head), head_slice(GROUP + head)
        queries, grads = both(own, far, q_cols), both(own, far, g_cols)
        first = place[0] * GROUP + head
        dot = rows[pl.ds(first, 1), :] + rows[pl.ds(LOW_LANE + first, 1), :]
        total = totals[head : head + 1]
        at = [2 * (GROUP + head) if role == 1 else 2 * head for role in roles]
        keys = jnp.concatenate([ref[:, head_slice(a)] for ref, a in zip(blocks, at)], axis=0)
        values = jnp.concatenate([ref[:, head_slice(a + 1)] for ref, a in zip(blocks, at)], axis=0)
        scores = jnp.dot(keys, queries.T, preferred_element_type=F32) * SCALE2
        if 0 in roles:
            scores = jnp.where(seen(rows, own), scores, NEG)
        bounds = [total - bias_ref[role] for role in roles]
        parts = [
            jnp.exp2(scores[i * half : (i + 1) * half] - bound) for i, bound in enumerate(bounds)
        ]
        probs = jnp.concatenate(parts, axis=0)
        dv = jnp.dot(probs.astype(BF16), grads, preferred_element_type=F32)
        dp = jnp.dot(values, grads.T, preferred_element_type=F32)
        ds = (probs * (dp - dot)).astype(BF16)
        dk = jnp.dot(ds, queries, preferred_element_type=F32) * FACTOR
        dq = jnp.dot(keys.T, ds, preferred_element_type=F32)
        for i, out in enumerate(outs):
            out[:, head_slice(2 * head)] = dk[i * half : (i + 1) * half].astype(out.dtype)
            out[:, head_slice(2 * head + 1)] = dv[i * half : (i + 1) * half].astype(out.dtype)
        if 3 not in roles:
            dq += dq_part[q_cols, :]
        if 0 in roles:
            turned = (dq * FACTOR).T.astype(BF16)
            near_rows = pl.multiple_of(place[1] * half, half)
            far_rows = pl.multiple_of((1 - place[1]) * half, half)
            dq_out[pl.ds(near_rows, half), q_cols] = turned[:half]
            dq_out[pl.ds(far_rows, half), q_cols] = turned[half:]
        else:
            dq_out[q_cols, :] = dq


def grads(bias, place, own_stats, far_stats, own, far, roles, blocks, dq_part=None):
    half = own.shape[0]
    wide = GROUP * HDIM
    pairs = GROUP * 2 * half * len(roles) * half
    outs = [
        jax.ShapeDtypeStruct((half, 2 * wide), F32 if role == 0 else BF16) for role in roles
    ]
    extra = [] if dq_part is None else [dq_part]
    if 0 in roles:
        dq_out = jax.ShapeDtypeStruct((2 * half, wide), BF16)
    else:
        dq_out = jax.ShapeDtypeStruct((wide, 2 * half), F32)
    return pl.pallas_call(
        functools.partial(grads_kernel, roles),
        out_shape=[dq_out] + outs,
        in_specs=[smem(), smem()] + [vmem()] * (4 + len(blocks) + len(extra)),
        out_specs=[vmem()] * (1 + len(outs)),
        scratch_shapes=[pltpu.VMEM((HDIM, 2 * half), F32)],
        compiler_params=params(),
        cost_estimate=cost(10 * pairs * HDIM, 18 * half * wide * 2, pairs),
        name="grads" + "".join(str(role) for role in roles),
    )(bias, place, own_stats, far_stats, own, far, *blocks, *extra)


def fold_kernel(even_ref, d1, swapped, side, out):
    odd = 1.0 - even_ref[0].astype(F32)
    total = d1[...].astype(F32) + swapped[...].astype(F32) + side[...].astype(F32) * odd
    out[...] = total.astype(BF16)


def fold(even, d1, swapped, side):
    return pl.pallas_call(
        fold_kernel,
        out_shape=jax.ShapeDtypeStruct(d1.shape, BF16),
        in_specs=[smem()] + [vmem()] * 3,
        out_specs=vmem(),
        compiler_params=params(),
        cost_estimate=cost(3 * d1.size, 8 * d1.size),
        name="fold",
    )(even, d1, swapped, side)


def close_kernel(even_ref, d0, back, side, out):
    even = even_ref[0].astype(F32)
    tok = out.shape[1]
    for step in range(XN):
        rows = slice(step * tok, (step + 1) * tok)
        pair = d0[rows, :] + back[rows, :].astype(F32) + side[rows, :].astype(F32) * even
        out[step] = pair.astype(BF16)


def close(even, d0, back, side):
    half, wide = d0.shape
    tok = half // XN
    return pl.pallas_call(
        close_kernel,
        out_shape=jax.ShapeDtypeStruct((XN, tok, wide), BF16),
        in_specs=[smem()] + [vmem()] * 3,
        out_specs=vmem(),
        compiler_params=params(),
        cost_estimate=cost(3 * half * wide, 10 * half * wide),
        name="close",
    )(even, d0, back, side)


def unpack_kernel(parts, halves, dq, dk, dv):
    wide = GROUP * HDIM
    for group in range(XN):
        total = halves[group].astype(F32) + halves[XN + group].astype(F32)
        dq[:, group * wide : (group + 1) * wide] = total.astype(BF16)
        for h in range(GROUP):
            at = 2 * h * HDIM
            cols = slice((group * GROUP + h) * HDIM, (group * GROUP + h + 1) * HDIM)
            dk[:, cols] = parts[group, :, at : at + HDIM]
            dv[:, cols] = parts[group, :, at + HDIM : at + 2 * HDIM]


def unpack(parts, halves):
    tok = parts.shape[1]
    return pl.pallas_call(
        unpack_kernel,
        out_shape=[jax.ShapeDtypeStruct((tok, HEADS * HDIM), BF16)] * 3,
        in_specs=[vmem()] * 2,
        out_specs=[vmem()] * 3,
        compiler_params=params(),
        cost_estimate=cost(0, 14 * tok * HEADS * HDIM),
        name="unpack",
    )(parts, halves)


def over_x(value):
    groups = [[z * XN + x for x in range(XN)] for z in range(lax.axis_size("col") // XN)]
    return lax.all_to_all(value, "col", 0, 0, axis_index_groups=groups)


def across_z(value):
    count = lax.axis_size("col")
    return lax.ppermute(value, "col", [(c, (c + XN) % count) for c in range(count)])


def along_row(value, steps):
    count = lax.axis_size("row")
    first, last = max(0, -steps), min(count, count - steps)
    return lax.ppermute(value, "row", [(r, r + steps) for r in range(first, last)])


def in_chip(value):
    count = lax.axis_size("row")
    return lax.ppermute(value, "row", [(r, r ^ 1) for r in range(count)])


def per_device(query, key, value, saved_out, grad_out, frame_ids):
    row, col = lax.axis_index("row"), lax.axis_index("col")
    place = jnp.stack([col % XN, col // XN]).astype(jnp.int32)
    is_even = row % 2 == 0
    even = is_even.astype(jnp.int32).reshape(1)
    tok = query.shape[0]
    half = XN * tok
    wide = 2 * GROUP * HDIM

    kv = jnp.stack([key, value])
    kv_far = along_row(kv, 2)
    own = over_x(pack_queries(query, saved_out, grad_out, frame_ids[:, None])).reshape(half, -1)
    far = across_z(own)
    near = over_x(pack_keys(kv, kv_far)).reshape(half, -1)
    w0, w1 = near[:, :wide], near[:, wide:]
    w3 = along_row(jnp.where(is_even, w0, w1), 1)
    w2 = in_chip(w1)
    held = jnp.stack(
        [
            row >= 0,
            row >= 2,
            jnp.where(is_even, row >= 1, row >= 3),
            jnp.where(is_even, row >= 3, row >= 1),
        ]
    )
    bias = jnp.where(held, 0.0, NEG).astype(F32)

    own_stats = stats(bias, own, far, near, w2, w3)
    common = (bias, place, own_stats, across_z(own_stats), own, far)
    dq_part, d2, d3 = grads(*common, (2, 3), (w2, w3))
    side, swapped = along_row(d3, -1), in_chip(d2)
    dq_part, d1 = grads(*common, (1,), (near,), dq_part)
    held = fold(even, d1, swapped, side)
    back = along_row(held, -2)
    dq_part, held = lax.optimization_barrier((dq_part, held))
    dq, d0 = grads(*common, (0,), (near,), dq_part)
    halves = lax.all_to_all(dq.reshape(-1, tok, GROUP * HDIM), "col", 0, 0)
    back, halves = lax.optimization_barrier((back, halves))
    return tuple(unpack(over_x(close(even, d0, back, side)), halves))


def solution(mesh):
    placed = P(("row", "col"), None)
    return jax.shard_map(
        per_device,
        mesh=mesh,
        in_specs=(placed,) * 5 + (P(("row", "col")),),
        out_specs=(placed,) * 3,
        check_vma=False,
    )
```

```python
import functools
import math

import jax
import jax.numpy as jnp
from jax import lax
from jax.experimental import pallas as pl
from jax.experimental.pallas import tpu as pltpu
from jax.sharding import PartitionSpec as P

HEADS = 20
HDIM = 128
XN = 4
GROUP = HEADS // XN
NEG = -1e30
FACTOR = HDIM ** (-0.5)
SCALE2 = FACTOR * math.log2(math.e)
LOW_LANE = 32
FRAME_LANE = 64
BF16 = jnp.bfloat16
F32 = jnp.float32


def params(room=20):
    return pltpu.CompilerParams(vmem_limit_bytes=room * 1024 * 1024)


def cost(flops, moved, exps=0):
    return pl.CostEstimate(flops=flops, bytes_accessed=moved, transcendentals=exps)


def load_all(sources, held, sems):
    copies = [
        pltpu.make_async_copy(src, held.at[at], sems.at[at]) for at, src in enumerate(sources)
    ]
    for copy in copies:
        copy.start()
    for copy in copies:
        copy.wait()


def pack_queries_kernel(q_any, o_any, g_any, f_ref, out, held, sems):
    load_all((q_any, o_any, g_any), held, sems)
    tok = held.shape[1]
    wide = GROUP * HDIM
    lane = lax.broadcasted_iota(jnp.int32, (tok, HDIM), 1)
    meta = jnp.where(lane == FRAME_LANE, f_ref[...].astype(F32), 0.0)
    for head in range(HEADS):
        cols = slice(head * HDIM, (head + 1) * HDIM)
        product = held[2, :, cols].astype(F32) * held[1, :, cols].astype(F32)
        dot = jnp.sum(product, axis=1, keepdims=True)
        high = dot.astype(BF16).astype(F32)
        meta = jnp.where(lane == head, high, meta)
        meta = jnp.where(lane == LOW_LANE + head, dot - high, meta)
    meta = meta.astype(BF16)
    for group in range(XN):
        here = slice(group * wide, (group + 1) * wide)
        out[group, :, :wide] = held[0, :, here]
        out[group, :, wide : 2 * wide] = held[2, :, here]
        out[group, :, 2 * wide :] = meta


def pack_queries(query, saved_out, grad_out, frames):
    tok, width = query.shape
    shape = (XN, tok, 2 * GROUP * HDIM + HDIM)
    return pl.pallas_call(
        pack_queries_kernel,
        out_shape=jax.ShapeDtypeStruct(shape, BF16),
        in_specs=[pl.BlockSpec(memory_space=pl.ANY)] * 3 + [vmem()],
        out_specs=vmem(),
        scratch_shapes=[pltpu.VMEM((3, tok, width), BF16), pltpu.SemaphoreType.DMA((3,))],
        compiler_params=params(60),
        cost_estimate=cost(2 * tok * width, 14 * tok * width),
        name="pack_queries",
    )(query, saved_out, grad_out, frames)


def pack_keys_kernel(near, far, out):
    for head in range(HEADS):
        group, h = divmod(head, GROUP)
        cols = slice(head * HDIM, (head + 1) * HDIM)
        for block, ref in enumerate((near, far)):
            for at in range(2):
                first = (2 * (block * GROUP + h) + at) * HDIM
                out[group, :, first : first + HDIM] = ref[at, :, cols]


def pack_keys(near, far):
    _, tok, width = near.shape
    return pl.pallas_call(
        pack_keys_kernel,
        out_shape=jax.ShapeDtypeStruct((XN, tok, 4 * GROUP * HDIM), BF16),
        in_specs=[vmem()] * 2,
        out_specs=vmem(),
        compiler_params=params(),
        cost_estimate=cost(0, 16 * tok * width),
        name="pack_keys",
    )(near, far)


META = slice(2 * GROUP * HDIM, (2 * GROUP + 1) * HDIM)


def head_slice(at):
    return slice(at * HDIM, (at + 1) * HDIM)


def seen(rows, own):
    k_frame = own[:, META].astype(F32)[:, FRAME_LANE : FRAME_LANE + 1]
    return k_frame <= rows[FRAME_LANE : FRAME_LANE + 1, :]


def stats_kernel(bias_ref, tokens, own, near, w2, w3, out_ref):
    half = own.shape[0]
    mask = seen(tokens[:, META].astype(F32).T, own)
    out_ref[...] = jnp.zeros_like(out_ref)
    for head in range(GROUP):
        queries = tokens[:, head_slice(head)].T
        at = head_slice(2 * head)
        keys = [near[:, at], near[:, head_slice(2 * (GROUP + head))], w2[:, at], w3[:, at]]
        scores = jnp.dot(
            jnp.concatenate(keys, axis=0), queries, preferred_element_type=F32
        ) * SCALE2
        parts = [scores[role * half : (role + 1) * half] for role in range(4)]
        parts[0] = jnp.where(mask, parts[0], NEG)
        peaks = [
            jnp.max(part, axis=0, keepdims=True) + bias_ref[role]
            for role, part in enumerate(parts)
        ]
        peak = functools.reduce(jnp.maximum, peaks)
        total = jnp.zeros_like(peak)
        for role, part in enumerate(parts):
            total += jnp.sum(jnp.exp2(part - (peak - bias_ref[role])), axis=0, keepdims=True)
        out_ref[head : head + 1, :] = peak
        out_ref[8 + head : 9 + head, :] = total


def smem():
    return pl.BlockSpec(memory_space=pltpu.SMEM)


def vmem():
    return pl.BlockSpec(memory_space=pltpu.VMEM)


def stats(name, bias, tokens, own, near, w2, w3):
    half = own.shape[0]
    pairs = GROUP * half * 4 * half
    return pl.pallas_call(
        stats_kernel,
        out_shape=jax.ShapeDtypeStruct((16, half), F32),
        in_specs=[smem()] + [vmem()] * 5,
        out_specs=vmem(),
        compiler_params=params(),
        cost_estimate=cost(4 * pairs * HDIM, 5 * half * GROUP * HDIM * 2, pairs),
        name=name,
    )(bias, tokens, own, near, w2, w3)


def log_total(one, other):
    one_peak, one_sum = one[:8, :], one[8:, :]
    other_peak, other_sum = other[:8, :], other[8:, :]
    peak = jnp.maximum(one_peak, other_peak)
    one_part = one_sum * jnp.exp2(one_peak - peak)
    return peak + jnp.log2(one_part + other_sum * jnp.exp2(other_peak - peak))


def grads_kernel(roles, parts_in, dq_in, last, bias_ref, place, one, other, tokens, own, *rest):
    *rest, rows = rest
    blocks, rest = rest[: len(roles)], rest[len(roles) :]
    if parts_in:
        parts, rest = rest[: len(roles)], rest[len(roles) :]
    if dq_in:
        dq_part, *rest = rest
    dq_out, *outs = rest
    half = own.shape[0]
    rows[...] = tokens[:, META].astype(F32).T
    totals = log_total(one, other)
    for head in range(GROUP):
        q_cols = head_slice(head)
        queries, grads = tokens[:, q_cols], tokens[:, head_slice(GROUP + head)]
        first = place[0] * GROUP + head
        dot = rows[pl.ds(first, 1), :] + rows[pl.ds(LOW_LANE + first, 1), :]
        at = [2 * (GROUP + head) if role == 1 else 2 * head for role in roles]
        keys = jnp.concatenate([ref[:, head_slice(a)] for ref, a in zip(blocks, at)], axis=0)
        values = jnp.concatenate([ref[:, head_slice(a + 1)] for ref, a in zip(blocks, at)], axis=0)
        scores = jnp.dot(keys, queries.T, preferred_element_type=F32) * SCALE2
        pieces = []
        for i, role in enumerate(roles):
            piece = scores[i * half : (i + 1) * half]
            if role == 0:
                piece = jnp.where(seen(rows, own), piece, NEG)
            pieces.append(jnp.exp2(piece - (totals[head : head + 1] - bias_ref[role])))
        probs = jnp.concatenate(pieces, axis=0)
        dv = jnp.dot(probs.astype(BF16), grads, preferred_element_type=F32)
        dp = jnp.dot(values, grads.T, preferred_element_type=F32)
        ds = (probs * (dp - dot)).astype(BF16)
        dk = jnp.dot(ds, queries, preferred_element_type=F32) * FACTOR
        dq = jnp.dot(keys.T, ds, preferred_element_type=F32)
        for i, out in enumerate(outs):
            rows_of = slice(i * half, (i + 1) * half)
            for cols, value in ((2 * head, dk[rows_of]), (2 * head + 1, dv[rows_of])):
                if parts_in:
                    value += parts[i][:, head_slice(cols)].astype(F32)
                out[:, head_slice(cols)] = value.astype(out.dtype)
        if dq_in:
            dq += dq_part[q_cols, :]
        if last:
            dq_out[:, q_cols] = (dq * FACTOR).T.astype(dq_out.dtype)
        else:
            dq_out[q_cols, :] = dq


def grads(name, common, tokens, own, blocks, kinds, parts=(), dq_part=None, dq_kind=None):
    roles = tuple(blocks)
    half = own.shape[0]
    wide = GROUP * HDIM
    pairs = GROUP * half * len(roles) * half
    extra = list(parts) + ([] if dq_part is None else [dq_part])
    if dq_kind is None:
        dq_out = jax.ShapeDtypeStruct((wide, half), F32)
    else:
        dq_out = jax.ShapeDtypeStruct((half, wide), dq_kind)
    return pl.pallas_call(
        functools.partial(
            grads_kernel, roles, bool(parts), dq_part is not None, dq_kind is not None
        ),
        out_shape=[dq_out] + [jax.ShapeDtypeStruct((half, 2 * wide), kind) for kind in kinds],
        in_specs=[smem(), smem()] + [vmem()] * (4 + len(roles) + len(extra)),
        out_specs=[vmem()] * (1 + len(kinds)),
        scratch_shapes=[pltpu.VMEM((HDIM, half), F32)],
        compiler_params=params(),
        cost_estimate=cost(10 * pairs * HDIM, 12 * half * wide * 2, pairs),
        name=name,
    )(*common, tokens, own, *blocks.values(), *extra)


def fold_kernel(even_ref, d1, swapped, side, dq_own, dq_back, out, dq_out):
    odd = 1.0 - even_ref[0].astype(F32)
    total = d1[...].astype(F32) + swapped[...].astype(F32) + side[...].astype(F32) * odd
    out[...] = total.astype(BF16)
    dq_out[...] = (dq_own[...] + dq_back[...].astype(F32)).astype(BF16)


def fold(even, d1, swapped, side, dq_own, dq_back):
    return pl.pallas_call(
        fold_kernel,
        out_shape=[
            jax.ShapeDtypeStruct(d1.shape, BF16),
            jax.ShapeDtypeStruct(dq_own.shape, BF16),
        ],
        in_specs=[smem()] + [vmem()] * 5,
        out_specs=[vmem()] * 2,
        compiler_params=params(),
        cost_estimate=cost(3 * d1.size, 8 * d1.size),
        name="fold",
    )(even, d1, swapped, side, dq_own, dq_back)


def close_kernel(even_ref, dq, d0, back, side, out):
    even = even_ref[0].astype(F32)
    tok = out.shape[1]
    wide = dq.shape[1]
    for step in range(XN):
        rows = slice(step * tok, (step + 1) * tok)
        pair = d0[rows, :] + back[rows, :].astype(F32) + side[rows, :].astype(F32) * even
        out[step, :, :wide] = dq[rows, :]
        out[step, :, wide:] = pair.astype(BF16)


def close(even, dq, d0, back, side):
    half, wide = dq.shape
    tok = half // XN
    return pl.pallas_call(
        close_kernel,
        out_shape=jax.ShapeDtypeStruct((XN, tok, 3 * wide), BF16),
        in_specs=[smem()] + [vmem()] * 4,
        out_specs=vmem(),
        compiler_params=params(),
        cost_estimate=cost(6 * half * wide, 24 * half * wide),
        name="close",
    )(even, dq, d0, back, side)


def unpack_kernel(parts, dq, dk, dv):
    wide = GROUP * HDIM
    for group in range(XN):
        dq[:, group * wide : (group + 1) * wide] = parts[group, :, :wide]
        for h in range(GROUP):
            at = wide + 2 * h * HDIM
            cols = slice((group * GROUP + h) * HDIM, (group * GROUP + h + 1) * HDIM)
            dk[:, cols] = parts[group, :, at : at + HDIM]
            dv[:, cols] = parts[group, :, at + HDIM : at + 2 * HDIM]


def unpack(parts):
    tok = parts.shape[1]
    return pl.pallas_call(
        unpack_kernel,
        out_shape=[jax.ShapeDtypeStruct((tok, HEADS * HDIM), BF16)] * 3,
        in_specs=[vmem()],
        out_specs=[vmem()] * 3,
        compiler_params=params(),
        cost_estimate=cost(0, 12 * tok * HEADS * HDIM),
        name="unpack",
    )(parts)


def over_x(value):
    groups = [[z * XN + x for x in range(XN)] for z in range(lax.axis_size("col") // XN)]
    return lax.all_to_all(value, "col", 0, 0, axis_index_groups=groups)


def across_z(value):
    count = lax.axis_size("col")
    return lax.ppermute(value, "col", [(c, (c + XN) % count) for c in range(count)])


def along_row(value, steps):
    count = lax.axis_size("row")
    first, last = max(0, -steps), min(count, count - steps)
    return lax.ppermute(value, "row", [(r, r + steps) for r in range(first, last)])


def in_chip(value):
    count = lax.axis_size("row")
    return lax.ppermute(value, "row", [(r, r ^ 1) for r in range(count)])


def per_device(query, key, value, saved_out, grad_out, frame_ids):
    row, col = lax.axis_index("row"), lax.axis_index("col")
    place = jnp.stack([col % XN, col // XN]).astype(jnp.int32)
    is_even = row % 2 == 0
    even = is_even.astype(jnp.int32).reshape(1)
    tok = query.shape[0]
    half = XN * tok
    wide = 2 * GROUP * HDIM

    kv = jnp.stack([key, value])
    kv_far = along_row(kv, 2)
    own = over_x(pack_queries(query, saved_out, grad_out, frame_ids[:, None])).reshape(half, -1)
    far = across_z(own)
    near = over_x(pack_keys(kv, kv_far)).reshape(half, -1)
    w0, w1 = near[:, :wide], near[:, wide:]
    w3 = along_row(jnp.where(is_even, w0, w1), 1)
    w2 = in_chip(w1)
    held = jnp.stack(
        [
            row >= 0,
            row >= 2,
            jnp.where(is_even, row >= 1, row >= 3),
            jnp.where(is_even, row >= 3, row >= 1),
        ]
    )
    bias = jnp.where(held, 0.0, NEG).astype(F32)

    window = (near, w2, w3)
    own_near = stats("stats_own", bias, own, own, *window)
    far_other = across_z(own_near)
    far_near = stats("stats_far", bias, far, own, *window)
    own_other = across_z(far_near)

    common = (bias, place, far_near, far_other)
    blocks = {0: near, 1: near, 2: w2, 3: w3}
    dq_far, *parts = grads("grads_far", common, far, own, blocks, [BF16] * 4, dq_kind=BF16)
    dq_back = across_z(dq_far)
    common = (bias, place, own_near, own_other)
    dq_part, d2, d3 = grads(
        "grads_own23", common, own, own, {2: w2, 3: w3}, [BF16] * 2, parts[2:]
    )
    side, swapped = along_row(d3, -1), in_chip(d2)
    dq_own, d0, d1 = grads(
        "grads_own01", common, own, own, {0: near, 1: near}, [F32, BF16], parts[:2], dq_part, F32
    )
    held, dq = fold(even, d1, swapped, side, dq_own, dq_back)
    back = along_row(held, -2)
    return tuple(unpack(over_x(close(even, dq, d0, back, side))))


def solution(mesh):
    placed = P(("row", "col"), None)
    return jax.shard_map(
        per_device,
        mesh=mesh,
        in_specs=(placed,) * 5 + (P(("row", "col")),),
        out_specs=(placed,) * 3,
        check_vma=False,
    )
```

```python
import functools
import math

import jax
import jax.numpy as jnp
from jax import lax
from jax.experimental import pallas as pl
from jax.experimental.pallas import tpu as pltpu
from jax.sharding import PartitionSpec as P

HEADS = 20
HDIM = 128
XN = 4
GROUP = HEADS // XN
NEG = -1e30
FACTOR = HDIM ** (-0.5)
SCALE2 = FACTOR * math.log2(math.e)
LOW_LANE = 32
FRAME_LANE = 64
BF16 = jnp.bfloat16
F32 = jnp.float32


def params(room=20):
    return pltpu.CompilerParams(vmem_limit_bytes=room * 1024 * 1024)


def cost(flops, moved, exps=0):
    return pl.CostEstimate(flops=flops, bytes_accessed=moved, transcendentals=exps)


def load_all(sources, held, sems):
    copies = [
        pltpu.make_async_copy(src, held.at[at], sems.at[at]) for at, src in enumerate(sources)
    ]
    for copy in copies:
        copy.start()
    for copy in copies:
        copy.wait()


def pack_queries_kernel(q_any, o_any, g_any, f_ref, out, held, sems):
    load_all((q_any, o_any, g_any), held, sems)
    tok = held.shape[1]
    wide = GROUP * HDIM
    lane = lax.broadcasted_iota(jnp.int32, (tok, HDIM), 1)
    meta = jnp.where(lane == FRAME_LANE, f_ref[...].astype(F32), 0.0)
    for head in range(HEADS):
        cols = slice(head * HDIM, (head + 1) * HDIM)
        product = held[2, :, cols].astype(F32) * held[1, :, cols].astype(F32)
        dot = jnp.sum(product, axis=1, keepdims=True)
        high = dot.astype(BF16).astype(F32)
        meta = jnp.where(lane == head, high, meta)
        meta = jnp.where(lane == LOW_LANE + head, dot - high, meta)
    meta = meta.astype(BF16)
    for group in range(XN):
        here = slice(group * wide, (group + 1) * wide)
        out[group, :, :wide] = held[0, :, here]
        out[group, :, wide : 2 * wide] = held[2, :, here]
        out[group, :, 2 * wide :] = meta


def pack_queries(query, saved_out, grad_out, frames):
    tok, width = query.shape
    shape = (XN, tok, 2 * GROUP * HDIM + HDIM)
    return pl.pallas_call(
        pack_queries_kernel,
        out_shape=jax.ShapeDtypeStruct(shape, BF16),
        in_specs=[pl.BlockSpec(memory_space=pl.ANY)] * 3 + [vmem()],
        out_specs=vmem(),
        scratch_shapes=[pltpu.VMEM((3, tok, width), BF16), pltpu.SemaphoreType.DMA((3,))],
        compiler_params=params(60),
        cost_estimate=cost(2 * tok * width, 14 * tok * width),
        name="pack_queries",
    )(query, saved_out, grad_out, frames)


def pack_keys_kernel(k_any, v_any, out, held, sems):
    load_all((k_any, v_any), held, sems)
    for head in range(HEADS):
        group, h = divmod(head, GROUP)
        cols = slice(head * HDIM, (head + 1) * HDIM)
        for at in range(2):
            out[group, :, (2 * h + at) * HDIM : (2 * h + at + 1) * HDIM] = held[at, :, cols]


def pack_keys(key, value):
    tok, width = key.shape
    return pl.pallas_call(
        pack_keys_kernel,
        out_shape=jax.ShapeDtypeStruct((XN, tok, 2 * GROUP * HDIM), BF16),
        in_specs=[pl.BlockSpec(memory_space=pl.ANY)] * 2,
        out_specs=vmem(),
        scratch_shapes=[pltpu.VMEM((2, tok, width), BF16), pltpu.SemaphoreType.DMA((2,))],
        compiler_params=params(60),
        cost_estimate=cost(0, 8 * tok * width),
        name="pack_keys",
    )(key, value)


META = slice(2 * GROUP * HDIM, (2 * GROUP + 1) * HDIM)


def head_slice(at):
    return slice(at * HDIM, (at + 1) * HDIM)


def seen(rows, own):
    k_frame = own[:, META].astype(F32)[:, FRAME_LANE : FRAME_LANE + 1]
    return k_frame <= rows[FRAME_LANE : FRAME_LANE + 1, :]


def stats_kernel(bias_ref, tokens, own, w0, w1, w2, w3, out_ref):
    half = own.shape[0]
    mask = seen(tokens[:, META].astype(F32).T, own)
    out_ref[...] = jnp.zeros_like(out_ref)
    for head in range(GROUP):
        queries = tokens[:, head_slice(head)].T
        keys = [ref[:, head_slice(2 * head)] for ref in (w0, w1, w2, w3)]
        scores = jnp.dot(
            jnp.concatenate(keys, axis=0), queries, preferred_element_type=F32
        ) * SCALE2
        parts = [scores[role * half : (role + 1) * half] for role in range(4)]
        parts[0] = jnp.where(mask, parts[0], NEG)
        peaks = [
            jnp.max(part, axis=0, keepdims=True) + bias_ref[role]
            for role, part in enumerate(parts)
        ]
        peak = functools.reduce(jnp.maximum, peaks)
        total = jnp.zeros_like(peak)
        for role, part in enumerate(parts):
            total += jnp.sum(jnp.exp2(part - (peak - bias_ref[role])), axis=0, keepdims=True)
        out_ref[head : head + 1, :] = peak
        out_ref[8 + head : 9 + head, :] = total


def smem():
    return pl.BlockSpec(memory_space=pltpu.SMEM)


def vmem():
    return pl.BlockSpec(memory_space=pltpu.VMEM)


def stats(name, bias, tokens, own, window):
    half = own.shape[0]
    pairs = GROUP * half * 4 * half
    return pl.pallas_call(
        stats_kernel,
        out_shape=jax.ShapeDtypeStruct((16, half), F32),
        in_specs=[smem()] + [vmem()] * 6,
        out_specs=vmem(),
        compiler_params=params(),
        cost_estimate=cost(4 * pairs * HDIM, 5 * half * GROUP * HDIM * 2, pairs),
        name=name,
    )(bias, tokens, own, *window)


def shape_of(shape, kind, kept):
    return pltpu.VMEM(shape, kind) if kept else jax.ShapeDtypeStruct(shape, kind)


def log_total(one, other):
    one_peak, one_sum = one[:8, :], one[8:, :]
    other_peak, other_sum = other[:8, :], other[8:, :]
    peak = jnp.maximum(one_peak, other_peak)
    one_part = one_sum * jnp.exp2(one_peak - peak)
    return peak + jnp.log2(one_part + other_sum * jnp.exp2(other_peak - peak))


def grads_kernel(roles, parts_in, dq_in, last, bias_ref, place, one, other, tokens, own, *rest):
    *rest, rows = rest
    blocks, rest = rest[: len(roles)], rest[len(roles) :]
    if parts_in:
        parts, rest = rest[: len(roles)], rest[len(roles) :]
    if dq_in:
        dq_part, *rest = rest
    dq_out, *outs = rest
    half = own.shape[0]
    rows[...] = tokens[:, META].astype(F32).T
    totals = log_total(one, other)
    for head in range(GROUP):
        q_cols = head_slice(head)
        queries, grads = tokens[:, q_cols], tokens[:, head_slice(GROUP + head)]
        first = place[0] * GROUP + head
        dot = rows[pl.ds(first, 1), :] + rows[pl.ds(LOW_LANE + first, 1), :]
        keys = jnp.concatenate([ref[:, head_slice(2 * head)] for ref in blocks], axis=0)
        values = jnp.concatenate([ref[:, head_slice(2 * head + 1)] for ref in blocks], axis=0)
        scores = jnp.dot(keys, queries.T, preferred_element_type=F32) * SCALE2
        pieces = []
        for i, role in enumerate(roles):
            piece = scores[i * half : (i + 1) * half]
            if role == 0:
                piece = jnp.where(seen(rows, own), piece, NEG)
            pieces.append(jnp.exp2(piece - (totals[head : head + 1] - bias_ref[role])))
        probs = jnp.concatenate(pieces, axis=0)
        dv = jnp.dot(probs.astype(BF16), grads, preferred_element_type=F32)
        dp = jnp.dot(values, grads.T, preferred_element_type=F32)
        ds = (probs * (dp - dot)).astype(BF16)
        dk = jnp.dot(ds, queries, preferred_element_type=F32) * FACTOR
        dq = jnp.dot(keys.T, ds, preferred_element_type=F32)
        for i, out in enumerate(outs):
            rows_of = slice(i * half, (i + 1) * half)
            for cols, value in ((2 * head, dk[rows_of]), (2 * head + 1, dv[rows_of])):
                if parts_in:
                    value += parts[i][:, head_slice(cols)].astype(F32)
                out[:, head_slice(cols)] = value.astype(out.dtype)
        if dq_in:
            dq += dq_part[q_cols, :]
        if last:
            dq_out[:, q_cols] = (dq * FACTOR).T.astype(dq_out.dtype)
        else:
            dq_out[q_cols, :] = dq


def grads(name, common, tokens, own, window, roles, outs, parts=(), dq_part=None, dq_out=None):
    half = own.shape[0]
    wide = GROUP * HDIM
    pairs = GROUP * half * len(roles) * half
    extra = list(parts) + ([] if dq_part is None else [dq_part])
    last = dq_out is not None
    if last:
        dq_shape = shape_of((half, wide), *dq_out)
    else:
        dq_shape = shape_of((wide, half), F32, True)
    return pl.pallas_call(
        functools.partial(grads_kernel, roles, bool(parts), dq_part is not None, last),
        out_shape=[dq_shape] + [shape_of((half, 2 * wide), *out) for out in outs],
        in_specs=[smem(), smem()] + [vmem()] * (4 + len(roles) + len(extra)),
        out_specs=[vmem()] * (1 + len(outs)),
        scratch_shapes=[pltpu.VMEM((HDIM, half), F32)],
        compiler_params=params(),
        cost_estimate=cost(10 * pairs * HDIM, 12 * half * wide * 2, pairs),
        name=name,
    )(*common, tokens, own, *[window[role] for role in roles], *extra)


def fold_kernel(even_ref, d1, swapped, side, out):
    odd = 1.0 - even_ref[0].astype(F32)
    total = d1[...].astype(F32) + swapped[...].astype(F32) + side[...].astype(F32) * odd
    out[...] = total.astype(BF16)


def fold(even, d1, swapped, side):
    return pl.pallas_call(
        fold_kernel,
        out_shape=jax.ShapeDtypeStruct(d1.shape, BF16),
        in_specs=[smem()] + [vmem()] * 3,
        out_specs=vmem(),
        compiler_params=params(),
        cost_estimate=cost(3 * d1.size, 8 * d1.size),
        name="fold",
    )(even, d1, swapped, side)


def close_kernel(even_ref, dq_own, dq_back, d0, back, side, out):
    even = even_ref[0].astype(F32)
    tok = out.shape[1]
    wide = dq_own.shape[1]
    for step in range(XN):
        rows = slice(step * tok, (step + 1) * tok)
        pair = d0[rows, :] + back[rows, :].astype(F32) + side[rows, :].astype(F32) * even
        out[step, :, :wide] = (dq_own[rows, :] + dq_back[rows, :].astype(F32)).astype(BF16)
        out[step, :, wide:] = pair.astype(BF16)


def close(even, dq_own, dq_back, d0, back, side):
    half, wide = dq_own.shape
    tok = half // XN
    return pl.pallas_call(
        close_kernel,
        out_shape=jax.ShapeDtypeStruct((XN, tok, 3 * wide), BF16),
        in_specs=[smem()] + [vmem()] * 5,
        out_specs=vmem(),
        compiler_params=params(),
        cost_estimate=cost(6 * half * wide, 24 * half * wide),
        name="close",
    )(even, dq_own, dq_back, d0, back, side)


def unpack_kernel(parts, dq, dk, dv):
    wide = GROUP * HDIM
    for group in range(XN):
        dq[:, group * wide : (group + 1) * wide] = parts[group, :, :wide]
        for h in range(GROUP):
            at = wide + 2 * h * HDIM
            cols = slice((group * GROUP + h) * HDIM, (group * GROUP + h + 1) * HDIM)
            dk[:, cols] = parts[group, :, at : at + HDIM]
            dv[:, cols] = parts[group, :, at + HDIM : at + 2 * HDIM]


def unpack(parts):
    tok = parts.shape[1]
    return pl.pallas_call(
        unpack_kernel,
        out_shape=[jax.ShapeDtypeStruct((tok, HEADS * HDIM), BF16)] * 3,
        in_specs=[vmem()],
        out_specs=[vmem()] * 3,
        compiler_params=params(),
        cost_estimate=cost(0, 12 * tok * HEADS * HDIM),
        name="unpack",
    )(parts)


def over_x(value):
    groups = [[z * XN + x for x in range(XN)] for z in range(lax.axis_size("col") // XN)]
    return lax.all_to_all(value, "col", 0, 0, axis_index_groups=groups)


def across_z(value):
    count = lax.axis_size("col")
    return lax.ppermute(value, "col", [(c, (c + XN) % count) for c in range(count)])


def along_row(value, steps):
    count = lax.axis_size("row")
    first, last = max(0, -steps), min(count, count - steps)
    return lax.ppermute(value, "row", [(r, r + steps) for r in range(first, last)])


def in_chip(value):
    count = lax.axis_size("row")
    return lax.ppermute(value, "row", [(r, r ^ 1) for r in range(count)])


def per_device(query, key, value, saved_out, grad_out, frame_ids):
    row, col = lax.axis_index("row"), lax.axis_index("col")
    place = jnp.stack([col % XN, col // XN]).astype(jnp.int32)
    is_even = row % 2 == 0
    even = is_even.astype(jnp.int32).reshape(1)
    tok = query.shape[0]
    half = XN * tok

    qg = pack_queries(query, saved_out, grad_out, frame_ids[:, None])
    w0 = over_x(pack_keys(key, value))
    qg, w0 = lax.optimization_barrier((qg, w0))
    w0 = w0.reshape(half, -1)
    own = over_x(qg).reshape(half, -1)
    far = across_z(own)
    w1 = along_row(w0, 2)
    w3 = along_row(jnp.where(is_even, w0, w1), 1)
    w2 = in_chip(w1)
    held = jnp.stack(
        [
            row >= 0,
            row >= 2,
            jnp.where(is_even, row >= 1, row >= 3),
            jnp.where(is_even, row >= 3, row >= 1),
        ]
    )
    bias = jnp.where(held, 0.0, NEG).astype(F32)

    window = (w0, w1, w2, w3)
    own_near = stats("stats_own", bias, own, own, window)
    far_other = across_z(own_near)
    far_near = stats("stats_far", bias, far, own, window)
    own_other = across_z(far_near)

    common = (bias, place, far_near, far_other)
    kept, sent, summed = (BF16, True), (BF16, False), (F32, True)
    dq_far, *parts = grads(
        "grads_far", common, far, own, window, (0, 1, 2, 3), [kept] * 4, dq_out=sent
    )
    dq_back = across_z(dq_far)
    common = (bias, place, own_near, own_other)
    dq_part, d2, d3 = grads(
        "grads_own23", common, own, own, window, (2, 3), [sent] * 2, parts[2:]
    )
    side, swapped = along_row(d3, -1), in_chip(d2)
    dq_own, d0, d1 = grads(
        "grads_own01", common, own, own, window, (0, 1), [summed, kept], parts[:2], dq_part, summed
    )
    back = along_row(fold(even, d1, swapped, side), -2)
    return tuple(unpack(over_x(close(even, dq_own, dq_back, d0, back, side))))


def solution(mesh):
    placed = P(("row", "col"), None)
    return jax.shard_map(
        per_device,
        mesh=mesh,
        in_specs=(placed,) * 5 + (P(("row", "col")),),
        out_specs=(placed,) * 3,
        check_vma=False,
    )
```

```python
import functools
import math

import jax
import jax.numpy as jnp
from jax import lax
from jax.experimental import pallas as pl
from jax.experimental.pallas import tpu as pltpu
from jax.sharding import PartitionSpec as P

HEADS = 20
HDIM = 128
XN = 4
GROUP = HEADS // XN
NEG = -1e30
FACTOR = HDIM ** (-0.5)
SCALE2 = FACTOR * math.log2(math.e)
LOW_LANE = 32
FRAME_LANE = 64
BF16 = jnp.bfloat16
F32 = jnp.float32


def params(room=20):
    return pltpu.CompilerParams(vmem_limit_bytes=room * 1024 * 1024)


def cost(flops, moved, exps=0):
    return pl.CostEstimate(flops=flops, bytes_accessed=moved, transcendentals=exps)


def load_all(sources, held, sems):
    copies = [
        pltpu.make_async_copy(src, held.at[at], sems.at[at]) for at, src in enumerate(sources)
    ]
    for copy in copies:
        copy.start()
    for copy in copies:
        copy.wait()


def pack_queries_kernel(q_any, o_any, g_any, f_ref, out, held, sems):
    load_all((q_any, o_any, g_any), held, sems)
    tok = held.shape[1]
    wide = GROUP * HDIM
    lane = lax.broadcasted_iota(jnp.int32, (tok, HDIM), 1)
    meta = jnp.where(lane == FRAME_LANE, f_ref[...].astype(F32), 0.0)
    for head in range(HEADS):
        cols = slice(head * HDIM, (head + 1) * HDIM)
        product = held[2, :, cols].astype(F32) * held[1, :, cols].astype(F32)
        dot = jnp.sum(product, axis=1, keepdims=True)
        high = dot.astype(BF16).astype(F32)
        meta = jnp.where(lane == head, high, meta)
        meta = jnp.where(lane == LOW_LANE + head, dot - high, meta)
    meta = meta.astype(BF16)
    for group in range(XN):
        here = slice(group * wide, (group + 1) * wide)
        out[group, :, :wide] = held[0, :, here]
        out[group, :, wide : 2 * wide] = held[2, :, here]
        out[group, :, 2 * wide :] = meta


def pack_queries(query, saved_out, grad_out, frames):
    tok, width = query.shape
    shape = (XN, tok, 2 * GROUP * HDIM + HDIM)
    return pl.pallas_call(
        pack_queries_kernel,
        out_shape=jax.ShapeDtypeStruct(shape, BF16),
        in_specs=[pl.BlockSpec(memory_space=pl.ANY)] * 3 + [vmem()],
        out_specs=vmem(),
        scratch_shapes=[pltpu.VMEM((3, tok, width), BF16), pltpu.SemaphoreType.DMA((3,))],
        compiler_params=params(60),
        cost_estimate=cost(2 * tok * width, 14 * tok * width),
        name="pack_queries",
    )(query, saved_out, grad_out, frames)


def pack_keys_kernel(k_any, v_any, out, held, sems):
    load_all((k_any, v_any), held, sems)
    for head in range(HEADS):
        group, h = divmod(head, GROUP)
        cols = slice(head * HDIM, (head + 1) * HDIM)
        for at in range(2):
            out[group, :, (2 * h + at) * HDIM : (2 * h + at + 1) * HDIM] = held[at, :, cols]


def pack_keys(key, value):
    tok, width = key.shape
    return pl.pallas_call(
        pack_keys_kernel,
        out_shape=jax.ShapeDtypeStruct((XN, tok, 2 * GROUP * HDIM), BF16),
        in_specs=[pl.BlockSpec(memory_space=pl.ANY)] * 2,
        out_specs=vmem(),
        scratch_shapes=[pltpu.VMEM((2, tok, width), BF16), pltpu.SemaphoreType.DMA((2,))],
        compiler_params=params(60),
        cost_estimate=cost(0, 8 * tok * width),
        name="pack_keys",
    )(key, value)


META = slice(2 * GROUP * HDIM, (2 * GROUP + 1) * HDIM)


def head_slice(at):
    return slice(at * HDIM, (at + 1) * HDIM)


def seen(rows, own):
    k_frame = own[:, META].astype(F32)[:, FRAME_LANE : FRAME_LANE + 1]
    return k_frame <= rows[FRAME_LANE : FRAME_LANE + 1, :]


def stats_kernel(bias_ref, tokens, own, w0, w1, w2, w3, out_ref):
    half = own.shape[0]
    mask = seen(tokens[:, META].astype(F32).T, own)
    out_ref[...] = jnp.zeros_like(out_ref)
    for head in range(GROUP):
        queries = tokens[:, head_slice(head)].T
        keys = [ref[:, head_slice(2 * head)] for ref in (w0, w1, w2, w3)]
        scores = jnp.dot(
            jnp.concatenate(keys, axis=0), queries, preferred_element_type=F32
        ) * SCALE2
        parts = [scores[role * half : (role + 1) * half] for role in range(4)]
        parts[0] = jnp.where(mask, parts[0], NEG)
        peaks = [
            jnp.max(part, axis=0, keepdims=True) + bias_ref[role]
            for role, part in enumerate(parts)
        ]
        peak = functools.reduce(jnp.maximum, peaks)
        total = jnp.zeros_like(peak)
        for role, part in enumerate(parts):
            total += jnp.sum(jnp.exp2(part - (peak - bias_ref[role])), axis=0, keepdims=True)
        out_ref[head : head + 1, :] = peak
        out_ref[8 + head : 9 + head, :] = total


def smem():
    return pl.BlockSpec(memory_space=pltpu.SMEM)


def vmem():
    return pl.BlockSpec(memory_space=pltpu.VMEM)


def stats(name, bias, tokens, own, window):
    half = own.shape[0]
    pairs = GROUP * half * 4 * half
    return pl.pallas_call(
        stats_kernel,
        out_shape=jax.ShapeDtypeStruct((16, half), F32),
        in_specs=[smem()] + [vmem()] * 6,
        out_specs=vmem(),
        compiler_params=params(),
        cost_estimate=cost(4 * pairs * HDIM, 5 * half * GROUP * HDIM * 2, pairs),
        name=name,
    )(bias, tokens, own, *window)


def shape_of(shape, kind, kept):
    return pltpu.VMEM(shape, kind) if kept else jax.ShapeDtypeStruct(shape, kind)


def log_total(one, other):
    one_peak, one_sum = one[:8, :], one[8:, :]
    other_peak, other_sum = other[:8, :], other[8:, :]
    peak = jnp.maximum(one_peak, other_peak)
    one_part = one_sum * jnp.exp2(one_peak - peak)
    return peak + jnp.log2(one_part + other_sum * jnp.exp2(other_peak - peak))


def grads_kernel(roles, parts_in, bias_ref, place, one, other, tokens, own, *rest):
    *rest, rows = rest
    blocks, rest = rest[: len(roles)], rest[len(roles) :]
    if parts_in:
        parts, rest = rest[: len(roles)], rest[len(roles) :]
    dq_out, *outs = rest
    half = own.shape[0]
    rows[...] = tokens[:, META].astype(F32).T
    totals = log_total(one, other)
    for head in range(GROUP):
        q_cols = head_slice(head)
        queries, grads = tokens[:, q_cols], tokens[:, head_slice(GROUP + head)]
        first = place[0] * GROUP + head
        dot = rows[pl.ds(first, 1), :] + rows[pl.ds(LOW_LANE + first, 1), :]
        keys = jnp.concatenate([ref[:, head_slice(2 * head)] for ref in blocks], axis=0)
        values = jnp.concatenate([ref[:, head_slice(2 * head + 1)] for ref in blocks], axis=0)
        scores = jnp.dot(keys, queries.T, preferred_element_type=F32) * SCALE2
        pieces = []
        for i, role in enumerate(roles):
            piece = scores[i * half : (i + 1) * half]
            if role == 0:
                piece = jnp.where(seen(rows, own), piece, NEG)
            pieces.append(jnp.exp2(piece - (totals[head : head + 1] - bias_ref[role])))
        probs = jnp.concatenate(pieces, axis=0)
        dv = jnp.dot(probs.astype(BF16), grads, preferred_element_type=F32)
        dp = jnp.dot(values, grads.T, preferred_element_type=F32)
        ds = (probs * (dp - dot)).astype(BF16)
        dk = jnp.dot(ds, queries, preferred_element_type=F32) * FACTOR
        dq = jnp.dot(keys.T, ds, preferred_element_type=F32)
        for i, out in enumerate(outs):
            rows_of = slice(i * half, (i + 1) * half)
            for cols, value in ((2 * head, dk[rows_of]), (2 * head + 1, dv[rows_of])):
                if parts_in:
                    value += parts[i][:, head_slice(cols)].astype(F32)
                out[:, head_slice(cols)] = value.astype(out.dtype)
        turned = (dq * FACTOR).T.astype(dq_out.dtype)
        if parts_in:
            dq_out[:, q_cols] = turned
        else:
            dq_out[0, :, q_cols] = turned
            dq_out[1, :, q_cols] = turned


def grads(name, common, tokens, own, window, roles, outs, parts=(), dq_out=None):
    half = own.shape[0]
    wide = GROUP * HDIM
    pairs = GROUP * half * len(roles) * half
    dq_shape = shape_of((half, wide) if parts else (2, half, wide), *dq_out)
    return pl.pallas_call(
        functools.partial(grads_kernel, roles, bool(parts)),
        out_shape=[dq_shape] + [shape_of((half, 2 * wide), *out) for out in outs],
        in_specs=[smem(), smem()] + [vmem()] * (4 + len(roles) + len(parts)),
        out_specs=[vmem()] * (1 + len(outs)),
        scratch_shapes=[pltpu.VMEM((HDIM, half), F32)],
        compiler_params=params(),
        cost_estimate=cost(10 * pairs * HDIM, 12 * half * wide * 2, pairs),
        name=name,
    )(*common, tokens, own, *[window[role] for role in roles], *parts)


def fold_kernel(even_ref, d1, swapped, side, out):
    odd = 1.0 - even_ref[0].astype(F32)
    total = d1[...].astype(F32) + swapped[...].astype(F32) + side[...].astype(F32) * odd
    out[...] = total.astype(BF16)


def fold(even, d1, swapped, side):
    return pl.pallas_call(
        fold_kernel,
        out_shape=jax.ShapeDtypeStruct(d1.shape, BF16),
        in_specs=[smem()] + [vmem()] * 3,
        out_specs=vmem(),
        compiler_params=params(),
        cost_estimate=cost(3 * d1.size, 8 * d1.size),
        name="fold",
    )(even, d1, swapped, side)


def close_kernel(even_ref, place, dq_own, dq_back, d0, back, side, out):
    even = even_ref[0].astype(F32)
    tok = out.shape[1]
    wide = dq_own.shape[1]
    for step in range(XN):
        rows = slice(step * tok, (step + 1) * tok)
        pair = d0[rows, :] + back[rows, :].astype(F32) + side[rows, :].astype(F32) * even
        out[step, :, :wide] = (dq_own[rows, :] + dq_back[1 - place[1], rows, :].astype(F32)).astype(BF16)
        out[step, :, wide:] = pair.astype(BF16)


def close(even, place, dq_own, dq_back, d0, back, side):
    half, wide = dq_own.shape
    tok = half // XN
    return pl.pallas_call(
        close_kernel,
        out_shape=jax.ShapeDtypeStruct((XN, tok, 3 * wide), BF16),
        in_specs=[smem(), smem()] + [vmem()] * 5,
        out_specs=vmem(),
        compiler_params=params(),
        cost_estimate=cost(6 * half * wide, 24 * half * wide),
        name="close",
    )(even, place, dq_own, dq_back, d0, back, side)


def unpack_kernel(parts, dq, dk, dv):
    wide = GROUP * HDIM
    for group in range(XN):
        dq[:, group * wide : (group + 1) * wide] = parts[group, :, :wide]
        for h in range(GROUP):
            at = wide + 2 * h * HDIM
            cols = slice((group * GROUP + h) * HDIM, (group * GROUP + h + 1) * HDIM)
            dk[:, cols] = parts[group, :, at : at + HDIM]
            dv[:, cols] = parts[group, :, at + HDIM : at + 2 * HDIM]


def unpack(parts):
    tok = parts.shape[1]
    return pl.pallas_call(
        unpack_kernel,
        out_shape=[jax.ShapeDtypeStruct((tok, HEADS * HDIM), BF16)] * 3,
        in_specs=[vmem()],
        out_specs=[vmem()] * 3,
        compiler_params=params(),
        cost_estimate=cost(0, 12 * tok * HEADS * HDIM),
        name="unpack",
    )(parts)


def over_x(value):
    groups = [[z * XN + x for x in range(XN)] for z in range(lax.axis_size("col") // XN)]
    return lax.all_to_all(value, "col", 0, 0, axis_index_groups=groups)


def across_z(value):
    count = lax.axis_size("col")
    return lax.ppermute(value, "col", [(c, (c + XN) % count) for c in range(count)])


def pair_swap(value):
    half = lax.axis_size("col") // 2
    groups = [[c, c + half] for c in range(half)]
    return lax.all_to_all(value, "col", 0, 0, axis_index_groups=groups)


def along_row(value, steps):
    count = lax.axis_size("row")
    first, last = max(0, -steps), min(count, count - steps)
    return lax.ppermute(value, "row", [(r, r + steps) for r in range(first, last)])


def in_chip(value):
    count = lax.axis_size("row")
    return lax.ppermute(value, "row", [(r, r ^ 1) for r in range(count)])


def per_device(query, key, value, saved_out, grad_out, frame_ids):
    row, col = lax.axis_index("row"), lax.axis_index("col")
    place = jnp.stack([col % XN, col // XN]).astype(jnp.int32)
    is_even = row % 2 == 0
    even = is_even.astype(jnp.int32).reshape(1)
    tok = query.shape[0]
    half = XN * tok

    qg = pack_queries(query, saved_out, grad_out, frame_ids[:, None])
    w0 = over_x(pack_keys(key, value))
    qg, w0 = lax.optimization_barrier((qg, w0))
    w0 = w0.reshape(half, -1)
    own = over_x(qg).reshape(half, -1)
    far = across_z(own)
    w1 = along_row(w0, 2)
    w3 = along_row(jnp.where(is_even, w0, w1), 1)
    w2 = in_chip(w1)
    held = jnp.stack(
        [
            row >= 0,
            row >= 2,
            jnp.where(is_even, row >= 1, row >= 3),
            jnp.where(is_even, row >= 3, row >= 1),
        ]
    )
    bias = jnp.where(held, 0.0, NEG).astype(F32)

    window = (w0, w1, w2, w3)
    own_near = stats("stats_own", bias, own, own, window)
    far_other = across_z(own_near)
    far_near = stats("stats_far", bias, far, own, window)
    own_other = across_z(far_near)

    common = (bias, place, far_near, far_other)
    kept, sent, summed = (BF16, True), (BF16, False), (F32, True)
    roles = (0, 1, 2, 3)
    dq_far, *parts = grads("grads_far", common, far, own, window, roles, [kept] * 4, dq_out=sent)
    dq_back = pair_swap(dq_far)
    common = (bias, place, own_near, own_other)
    outs = [summed, kept, sent, sent]
    dq_own, d0, d1, d2, d3 = grads(
        "grads_own", common, own, own, window, roles, outs, parts, dq_out=summed
    )
    side, swapped = along_row(d3, -1), in_chip(d2)
    back = along_row(fold(even, d1, swapped, side), -2)
    return tuple(unpack(over_x(close(even, place, dq_own, dq_back, d0, back, side))))


def solution(mesh):
    placed = P(("row", "col"), None)
    return jax.shard_map(
        per_device,
        mesh=mesh,
        in_specs=(placed,) * 5 + (P(("row", "col")),),
        out_specs=(placed,) * 3,
        check_vma=False,
    )
```

```python
import functools
import math

import jax
import jax.numpy as jnp
from jax import lax
from jax.experimental import pallas as pl
from jax.experimental.pallas import tpu as pltpu
from jax.sharding import PartitionSpec as P

HEADS = 20
HDIM = 128
WBLK = 4
XN = 4
GROUP = HEADS // XN
NEG = -1e30
FACTOR = HDIM ** (-0.5)
SCALE2 = FACTOR * math.log2(math.e)
LOW_LANE = 32
FRAME_LANE = 64
BF16 = jnp.bfloat16
F32 = jnp.float32


def params(room=20):
    return pltpu.CompilerParams(vmem_limit_bytes=room * 1024 * 1024)


def cost(flops, moved, exps=0):
    return pl.CostEstimate(flops=flops, bytes_accessed=moved, transcendentals=exps)


def load_all(sources, held, sems):
    copies = [
        pltpu.make_async_copy(src, held.at[at], sems.at[at]) for at, src in enumerate(sources)
    ]
    for copy in copies:
        copy.start()
    for copy in copies:
        copy.wait()


def pack_queries_kernel(q_any, o_any, g_any, f_ref, out, held, sems):
    load_all((q_any, o_any, g_any), held, sems)
    tok = held.shape[1]
    wide = GROUP * HDIM
    lane = lax.broadcasted_iota(jnp.int32, (tok, HDIM), 1)
    meta = jnp.where(lane == FRAME_LANE, f_ref[...].astype(F32), 0.0)
    for head in range(HEADS):
        cols = slice(head * HDIM, (head + 1) * HDIM)
        product = held[2, :, cols].astype(F32) * held[1, :, cols].astype(F32)
        dot = jnp.sum(product, axis=1, keepdims=True)
        high = dot.astype(BF16).astype(F32)
        meta = jnp.where(lane == head, high, meta)
        meta = jnp.where(lane == LOW_LANE + head, dot - high, meta)
    meta = meta.astype(BF16)
    for group in range(XN):
        here = slice(group * wide, (group + 1) * wide)
        out[group, :, :wide] = held[0, :, here]
        out[group, :, wide : 2 * wide] = held[2, :, here]
        out[group, :, 2 * wide :] = meta


def pack_queries(query, saved_out, grad_out, frames):
    tok, width = query.shape
    shape = (XN, tok, 2 * GROUP * HDIM + HDIM)
    return pl.pallas_call(
        pack_queries_kernel,
        out_shape=jax.ShapeDtypeStruct(shape, BF16),
        in_specs=[pl.BlockSpec(memory_space=pl.ANY)] * 3 + [vmem()],
        out_specs=vmem(),
        scratch_shapes=[pltpu.VMEM((3, tok, width), BF16), pltpu.SemaphoreType.DMA((3,))],
        compiler_params=params(60),
        cost_estimate=cost(2 * tok * width, 14 * tok * width),
        name="pack_queries",
    )(query, saved_out, grad_out, frames)


def pack_keys_kernel(k_any, v_any, out, held, sems):
    load_all((k_any, v_any), held, sems)
    for head in range(HEADS):
        group, h = divmod(head, GROUP)
        cols = slice(head * HDIM, (head + 1) * HDIM)
        for at in range(2):
            out[group, :, (2 * h + at) * HDIM : (2 * h + at + 1) * HDIM] = held[at, :, cols]


def pack_keys(key, value):
    tok, width = key.shape
    return pl.pallas_call(
        pack_keys_kernel,
        out_shape=jax.ShapeDtypeStruct((XN, tok, 2 * GROUP * HDIM), BF16),
        in_specs=[pl.BlockSpec(memory_space=pl.ANY)] * 2,
        out_specs=vmem(),
        scratch_shapes=[pltpu.VMEM((2, tok, width), BF16), pltpu.SemaphoreType.DMA((2,))],
        compiler_params=params(60),
        cost_estimate=cost(0, 8 * tok * width),
        name="pack_keys",
    )(key, value)


META = slice(2 * GROUP * HDIM, (2 * GROUP + 1) * HDIM)


def head_slice(at):
    return slice(at * HDIM, (at + 1) * HDIM)


def seen(rows, own):
    k_frame = own[:, META].astype(F32)[:, FRAME_LANE : FRAME_LANE + 1]
    return k_frame <= rows[FRAME_LANE : FRAME_LANE + 1, :]


def stats_kernel(bias_ref, tokens, own, w0, w1, w2, w3, out_ref):
    half = own.shape[0]
    mask = seen(tokens[:, META].astype(F32).T, own)
    out_ref[...] = jnp.zeros_like(out_ref)
    for head in range(GROUP):
        queries = tokens[:, head_slice(head)].T
        keys = [ref[:, head_slice(2 * head)] for ref in (w0, w1, w2, w3)]
        scores = jnp.dot(
            jnp.concatenate(keys, axis=0), queries, preferred_element_type=F32
        ) * SCALE2
        parts = [scores[role * half : (role + 1) * half] for role in range(4)]
        parts[0] = jnp.where(mask, parts[0], NEG)
        peaks = [
            jnp.max(part, axis=0, keepdims=True) + bias_ref[role]
            for role, part in enumerate(parts)
        ]
        peak = functools.reduce(jnp.maximum, peaks)
        total = jnp.zeros_like(peak)
        for role, part in enumerate(parts):
            total += jnp.sum(jnp.exp2(part - (peak - bias_ref[role])), axis=0, keepdims=True)
        out_ref[head : head + 1, :] = peak
        out_ref[8 + head : 9 + head, :] = total


def smem():
    return pl.BlockSpec(memory_space=pltpu.SMEM)


def vmem():
    return pl.BlockSpec(memory_space=pltpu.VMEM)


def stats(name, bias, tokens, own, window):
    half = own.shape[0]
    pairs = GROUP * half * 4 * half
    return pl.pallas_call(
        stats_kernel,
        out_shape=jax.ShapeDtypeStruct((16, half), F32),
        in_specs=[smem()] + [vmem()] * 6,
        out_specs=vmem(),
        compiler_params=params(),
        cost_estimate=cost(4 * pairs * HDIM, 5 * half * GROUP * HDIM * 2, pairs),
        name=name,
    )(bias, tokens, own, *window)


def log_total(one, other):
    one_peak, one_sum = one[:8, :], one[8:, :]
    other_peak, other_sum = other[:8, :], other[8:, :]
    peak = jnp.maximum(one_peak, other_peak)
    one_part = one_sum * jnp.exp2(one_peak - peak)
    return peak + jnp.log2(one_part + other_sum * jnp.exp2(other_peak - peak))


def grads_kernel(parts_in, bias_ref, place, one, other, tokens, own, w0, w1, w2, w3, *rest):
    if parts_in:
        parts, rest = rest[:WBLK], rest[WBLK:]
    dq_out, *outs = rest[: 1 + WBLK]
    rows, acc, dq_acc, sems, *rest = rest[1 + WBLK :]
    loads, stores = [], []
    if parts_in:
        held, load_sems = rest
        for role, part in enumerate(parts):
            loads.append(pltpu.make_async_copy(part, held.at[role], load_sems.at[role]))
            loads[-1].start()
    half = own.shape[0]
    rows[...] = tokens[:, META].astype(F32).T
    totals = log_total(one, other)
    window = (w0, w1, w2, w3)
    for head in range(GROUP):
        q_cols = head_slice(head)
        pair = slice(2 * head * HDIM, 2 * (head + 1) * HDIM)
        queries, grads = tokens[:, q_cols], tokens[:, head_slice(GROUP + head)]
        first = place[0] * GROUP + head
        dot = rows[pl.ds(first, 1), :] + rows[pl.ds(LOW_LANE + first, 1), :]
        keys = jnp.concatenate([ref[:, head_slice(2 * head)] for ref in window], axis=0)
        values = jnp.concatenate([ref[:, head_slice(2 * head + 1)] for ref in window], axis=0)
        scores = jnp.dot(keys, queries.T, preferred_element_type=F32) * SCALE2
        pieces = []
        for role in range(WBLK):
            piece = scores[role * half : (role + 1) * half]
            if role == 0:
                piece = jnp.where(seen(rows, own), piece, NEG)
            pieces.append(jnp.exp2(piece - (totals[head : head + 1] - bias_ref[role])))
        probs = jnp.concatenate(pieces, axis=0)
        dv = jnp.dot(probs.astype(BF16), grads, preferred_element_type=F32)
        dp = jnp.dot(values, grads.T, preferred_element_type=F32)
        ds = (probs * (dp - dot)).astype(BF16)
        dk = jnp.dot(ds, queries, preferred_element_type=F32) * FACTOR
        dq = jnp.dot(keys.T, ds, preferred_element_type=F32)
        if parts_in and head == 0:
            for load in loads:
                load.wait()
        for role in range(WBLK):
            of = slice(role * half, (role + 1) * half)
            for cols, value in ((2 * head, dk[of]), (2 * head + 1, dv[of])):
                if parts_in:
                    value += held[role, :, head_slice(cols)].astype(F32)
                acc[role, :, head_slice(cols)] = value.astype(BF16)
            stores.append(
                pltpu.make_async_copy(
                    acc.at[role, :, pair], outs[role].at[:, pair], sems.at[role, head]
                )
            )
            stores[-1].start()
        dq_acc[:, q_cols] = (dq * FACTOR).T.astype(dq_acc.dtype)
        stores.append(
            pltpu.make_async_copy(
                dq_acc.at[:, q_cols], dq_out.at[:, q_cols], sems.at[WBLK, head]
            )
        )
        stores[-1].start()
    for store in stores:
        store.wait()


def grads(name, common, tokens, own, window, dq_kind, parts=()):
    half = own.shape[0]
    wide = GROUP * HDIM
    pairs = GROUP * half * WBLK * half
    hbm = pl.BlockSpec(memory_space=pl.ANY)
    scratch = [
        pltpu.VMEM((HDIM, half), F32),
        pltpu.VMEM((WBLK, half, 2 * wide), BF16),
        pltpu.VMEM((half, wide), dq_kind),
        pltpu.SemaphoreType.DMA((WBLK + 1, GROUP)),
    ]
    if parts:
        scratch += [pltpu.VMEM((WBLK, half, 2 * wide), BF16), pltpu.SemaphoreType.DMA((WBLK,))]
    return pl.pallas_call(
        functools.partial(grads_kernel, bool(parts)),
        out_shape=[jax.ShapeDtypeStruct((half, wide), dq_kind)]
        + [jax.ShapeDtypeStruct((half, 2 * wide), BF16)] * WBLK,
        in_specs=[smem(), smem()] + [vmem()] * (4 + WBLK) + [hbm] * len(parts),
        out_specs=[hbm] * (1 + WBLK),
        scratch_shapes=scratch,
        compiler_params=params(),
        cost_estimate=cost(10 * pairs * HDIM, 12 * half * wide * 2, pairs),
        name=name,
    )(*common, tokens, own, *window, *parts)


def row_block(shape):
    return pl.BlockSpec(shape, lambda step: (step, 0))


def fold_kernel(even_ref, d1, swapped, side, out):
    odd = 1.0 - even_ref[0].astype(F32)
    total = d1[...].astype(F32) + swapped[...].astype(F32) + side[...].astype(F32) * odd
    out[...] = total.astype(BF16)


def fold(even, d1, swapped, side):
    block = row_block((d1.shape[0] // 2, d1.shape[1]))
    return pl.pallas_call(
        fold_kernel,
        grid=(2,),
        out_shape=jax.ShapeDtypeStruct(d1.shape, BF16),
        in_specs=[smem()] + [block] * 3,
        out_specs=block,
        compiler_params=params(),
        cost_estimate=cost(3 * d1.size, 8 * d1.size),
        name="fold",
    )(even, d1, swapped, side)


def close_kernel(even_ref, dq_own, dq_back, d0, back, side, out):
    even = even_ref[0].astype(F32)
    wide = dq_own.shape[1]
    pair = d0[...].astype(F32) + back[...].astype(F32) + side[...].astype(F32) * even
    out[0, :, :wide] = (dq_own[...] + dq_back[...].astype(F32)).astype(BF16)
    out[0, :, wide:] = pair.astype(BF16)


def close(even, dq_own, dq_back, d0, back, side):
    half, wide = dq_own.shape
    tok = half // XN
    pair = row_block((tok, 2 * wide))
    return pl.pallas_call(
        close_kernel,
        grid=(XN,),
        out_shape=jax.ShapeDtypeStruct((XN, tok, 3 * wide), BF16),
        in_specs=[smem(), row_block((tok, wide)), row_block((tok, wide)), pair, pair, pair],
        out_specs=pl.BlockSpec((1, tok, 3 * wide), lambda step: (step, 0, 0)),
        compiler_params=params(),
        cost_estimate=cost(6 * half * wide, 24 * half * wide),
        name="close",
    )(even, dq_own, dq_back, d0, back, side)


def unpack_kernel(parts, dq, dk, dv):
    wide = GROUP * HDIM
    for group in range(XN):
        dq[:, group * wide : (group + 1) * wide] = parts[group, :, :wide]
        for h in range(GROUP):
            at = wide + 2 * h * HDIM
            cols = slice((group * GROUP + h) * HDIM, (group * GROUP + h + 1) * HDIM)
            dk[:, cols] = parts[group, :, at : at + HDIM]
            dv[:, cols] = parts[group, :, at + HDIM : at + 2 * HDIM]


def unpack(parts):
    tok = parts.shape[1]
    return pl.pallas_call(
        unpack_kernel,
        out_shape=[jax.ShapeDtypeStruct((tok, HEADS * HDIM), BF16)] * 3,
        in_specs=[vmem()],
        out_specs=[vmem()] * 3,
        compiler_params=params(),
        cost_estimate=cost(0, 12 * tok * HEADS * HDIM),
        name="unpack",
    )(parts)


def over_x(value):
    groups = [[z * XN + x for x in range(XN)] for z in range(lax.axis_size("col") // XN)]
    return lax.all_to_all(value, "col", 0, 0, axis_index_groups=groups)


def across_z(value):
    count = lax.axis_size("col")
    return lax.ppermute(value, "col", [(c, (c + XN) % count) for c in range(count)])


def along_row(value, steps):
    count = lax.axis_size("row")
    first, last = max(0, -steps), min(count, count - steps)
    return lax.ppermute(value, "row", [(r, r + steps) for r in range(first, last)])


def in_chip(value):
    count = lax.axis_size("row")
    return lax.ppermute(value, "row", [(r, r ^ 1) for r in range(count)])


def own_grads(operands):
    common, own, window, parts, even = operands
    dq_own, d0, d1, d2, d3 = grads("grads_own", common, own, own, window, F32, parts)
    side, swapped = along_row(d3, -1), in_chip(d2)
    return dq_own, d0, along_row(fold(even, d1, swapped, side), -2), side


def no_grads(operands):
    own, window = operands[1:3]
    empty = jnp.zeros_like(window[0])
    return jnp.zeros((own.shape[0], GROUP * HDIM), F32), empty, empty, empty


def per_device(query, key, value, saved_out, grad_out, frame_ids):
    row, col = lax.axis_index("row"), lax.axis_index("col")
    place = jnp.stack([col % XN, col // XN]).astype(jnp.int32)
    is_even = row % 2 == 0
    even = is_even.astype(jnp.int32).reshape(1)
    tok = query.shape[0]
    half = XN * tok

    qg = pack_queries(query, saved_out, grad_out, frame_ids[:, None])
    w0 = over_x(pack_keys(key, value))
    qg, w0 = lax.optimization_barrier((qg, w0))
    w0 = w0.reshape(half, -1)
    own = over_x(qg).reshape(half, -1)
    far = across_z(own)
    w1 = along_row(w0, 2)
    w3 = along_row(jnp.where(is_even, w0, w1), 1)
    w2 = in_chip(w1)
    held = jnp.stack(
        [
            row >= 0,
            row >= 2,
            jnp.where(is_even, row >= 1, row >= 3),
            jnp.where(is_even, row >= 3, row >= 1),
        ]
    )
    bias = jnp.where(held, 0.0, NEG).astype(F32)

    window = (w0, w1, w2, w3)
    own_near = stats("stats_own", bias, own, own, window)
    far_other = across_z(own_near)
    far_near = stats("stats_far", bias, far, own, window)
    own_other = across_z(far_near)

    common = (bias, place, far_near, far_other)
    dq_far, *parts = grads("grads_far", common, far, own, window, BF16)
    dq_far, own_other = lax.optimization_barrier((dq_far, own_other))
    dq_back = across_z(dq_far)
    common = (bias, place, own_near, own_other)
    dq_own, d0, back, side = lax.cond(
        row < lax.axis_size("row"), own_grads, no_grads, (common, own, window, parts, even)
    )
    return tuple(unpack(over_x(close(even, dq_own, dq_back, d0, back, side))))


def solution(mesh):
    placed = P(("row", "col"), None)
    return jax.shard_map(
        per_device,
        mesh=mesh,
        in_specs=(placed,) * 5 + (P(("row", "col")),),
        out_specs=(placed,) * 3,
        check_vma=False,
    )
```

```python
import functools
import math

import jax
import jax.numpy as jnp
from jax import lax
from jax.experimental import pallas as pl
from jax.experimental.pallas import tpu as pltpu
from jax.sharding import PartitionSpec as P

HEADS = 20
HDIM = 128
WBLK = 4
XN = 4
GROUP = HEADS // XN
NEG = -1e30
FACTOR = HDIM ** (-0.5)
SCALE2 = FACTOR * math.log2(math.e)
LOW_LANE = 32
FRAME_LANE = 64
BF16 = jnp.bfloat16
F32 = jnp.float32


def params(room=20):
    return pltpu.CompilerParams(vmem_limit_bytes=room * 1024 * 1024)


def cost(flops, moved, exps=0):
    return pl.CostEstimate(flops=flops, bytes_accessed=moved, transcendentals=exps)


def load_all(sources, held, sems):
    copies = [
        pltpu.make_async_copy(src, held.at[at], sems.at[at]) for at, src in enumerate(sources)
    ]
    for copy in copies:
        copy.start()
    for copy in copies:
        copy.wait()


def head_columns(place, step, h):
    group = lax.rem(place[0] + step, XN)
    return pl.ds(pl.multiple_of((group * GROUP + h) * HDIM, HDIM), HDIM)


def group_columns(place, step):
    group = lax.rem(place[0] + step, XN)
    return pl.ds(pl.multiple_of(group * GROUP * HDIM, GROUP * HDIM), GROUP * HDIM)


def pack_queries_kernel(place, q_any, o_any, g_any, f_ref, *rest):
    outs, (held, sems) = rest[:XN], rest[XN:]
    load_all((q_any, o_any, g_any), held, sems)
    tok = held.shape[1]
    wide = GROUP * HDIM
    lane = lax.broadcasted_iota(jnp.int32, (tok, HDIM), 1)
    meta = jnp.where(lane == FRAME_LANE, f_ref[...].astype(F32), 0.0)
    for head in range(HEADS):
        cols = slice(head * HDIM, (head + 1) * HDIM)
        product = held[2, :, cols].astype(F32) * held[1, :, cols].astype(F32)
        dot = jnp.sum(product, axis=1, keepdims=True)
        high = dot.astype(BF16).astype(F32)
        meta = jnp.where(lane == head, high, meta)
        meta = jnp.where(lane == LOW_LANE + head, dot - high, meta)
    meta = meta.astype(BF16)
    for step, out in enumerate(outs):
        here = group_columns(place, step)
        out[:, :wide] = held[0, :, here]
        out[:, wide : 2 * wide] = held[2, :, here]
        out[:, 2 * wide :] = meta


def pack_queries(place, query, saved_out, grad_out, frames):
    tok, width = query.shape
    return pl.pallas_call(
        pack_queries_kernel,
        out_shape=[jax.ShapeDtypeStruct((tok, 2 * GROUP * HDIM + HDIM), BF16)] * XN,
        in_specs=[smem()] + [pl.BlockSpec(memory_space=pl.ANY)] * 3 + [vmem()],
        out_specs=[vmem()] * XN,
        scratch_shapes=[pltpu.VMEM((3, tok, width), BF16), pltpu.SemaphoreType.DMA((3,))],
        compiler_params=params(60),
        cost_estimate=cost(2 * tok * width, 14 * tok * width),
        name="pack_queries",
    )(place, query, saved_out, grad_out, frames)


def pack_keys_kernel(place, k_any, v_any, *rest):
    outs, (held, sems) = rest[:XN], rest[XN:]
    load_all((k_any, v_any), held, sems)
    for step, out in enumerate(outs):
        for h in range(GROUP):
            cols = head_columns(place, step, h)
            for at in range(2):
                out[:, (2 * h + at) * HDIM : (2 * h + at + 1) * HDIM] = held[at, :, cols]


def pack_keys(place, key, value):
    tok, width = key.shape
    return pl.pallas_call(
        pack_keys_kernel,
        out_shape=[jax.ShapeDtypeStruct((tok, 2 * GROUP * HDIM), BF16)] * XN,
        in_specs=[smem()] + [pl.BlockSpec(memory_space=pl.ANY)] * 2,
        out_specs=[vmem()] * XN,
        scratch_shapes=[pltpu.VMEM((2, tok, width), BF16), pltpu.SemaphoreType.DMA((2,))],
        compiler_params=params(60),
        cost_estimate=cost(0, 8 * tok * width),
        name="pack_keys",
    )(place, key, value)


META = slice(2 * GROUP * HDIM, (2 * GROUP + 1) * HDIM)


def head_slice(at):
    return slice(at * HDIM, (at + 1) * HDIM)


def seen(rows, own):
    k_frame = own[:, META].astype(F32)[:, FRAME_LANE : FRAME_LANE + 1]
    return k_frame <= rows[FRAME_LANE : FRAME_LANE + 1, :]


def stats_kernel(bias_ref, tokens, own, w0, w1, w2, w3, out_ref):
    half = own.shape[0]
    mask = seen(tokens[:, META].astype(F32).T, own)
    out_ref[...] = jnp.zeros_like(out_ref)
    for head in range(GROUP):
        queries = tokens[:, head_slice(head)].T
        keys = [ref[:, head_slice(2 * head)] for ref in (w0, w1, w2, w3)]
        scores = jnp.dot(
            jnp.concatenate(keys, axis=0), queries, preferred_element_type=F32
        ) * SCALE2
        parts = [scores[role * half : (role + 1) * half] for role in range(4)]
        parts[0] = jnp.where(mask, parts[0], NEG)
        peaks = [
            jnp.max(part, axis=0, keepdims=True) + bias_ref[role]
            for role, part in enumerate(parts)
        ]
        peak = functools.reduce(jnp.maximum, peaks)
        total = jnp.zeros_like(peak)
        for role, part in enumerate(parts):
            total += jnp.sum(jnp.exp2(part - (peak - bias_ref[role])), axis=0, keepdims=True)
        out_ref[head : head + 1, :] = peak
        out_ref[8 + head : 9 + head, :] = total


def smem():
    return pl.BlockSpec(memory_space=pltpu.SMEM)


def vmem():
    return pl.BlockSpec(memory_space=pltpu.VMEM)


def stats(name, bias, tokens, own, window):
    half = own.shape[0]
    pairs = GROUP * half * 4 * half
    return pl.pallas_call(
        stats_kernel,
        out_shape=jax.ShapeDtypeStruct((16, half), F32),
        in_specs=[smem()] + [vmem()] * 6,
        out_specs=vmem(),
        compiler_params=params(),
        cost_estimate=cost(4 * pairs * HDIM, 5 * half * GROUP * HDIM * 2, pairs),
        name=name,
    )(bias, tokens, own, *window)


def log_total(one, other):
    one_peak, one_sum = one[:8, :], one[8:, :]
    other_peak, other_sum = other[:8, :], other[8:, :]
    peak = jnp.maximum(one_peak, other_peak)
    one_part = one_sum * jnp.exp2(one_peak - peak)
    return peak + jnp.log2(one_part + other_sum * jnp.exp2(other_peak - peak))


def grads_kernel(parts_in, bias_ref, place, one, other, tokens, own, w0, w1, w2, w3, *rest):
    if parts_in:
        parts, rest = rest[:WBLK], rest[WBLK:]
    dq_out, *outs = rest[: 1 + WBLK]
    rows, dq_acc, sems, *rest = rest[1 + WBLK :]
    sums = [rest[0].at[role] for role in range(WBLK)] if parts_in else outs
    stores = []
    half = own.shape[0]
    rows[...] = tokens[:, META].astype(F32).T
    totals = log_total(one, other)
    window = (w0, w1, w2, w3)
    for head in range(GROUP):
        q_cols = head_slice(head)
        pair = slice(2 * head * HDIM, 2 * (head + 1) * HDIM)
        queries, grads = tokens[:, q_cols], tokens[:, head_slice(GROUP + head)]
        first = place[0] * GROUP + head
        dot = rows[pl.ds(first, 1), :] + rows[pl.ds(LOW_LANE + first, 1), :]
        keys = jnp.concatenate([ref[:, head_slice(2 * head)] for ref in window], axis=0)
        values = jnp.concatenate([ref[:, head_slice(2 * head + 1)] for ref in window], axis=0)
        scores = jnp.dot(keys, queries.T, preferred_element_type=F32) * SCALE2
        pieces = []
        for role in range(WBLK):
            piece = scores[role * half : (role + 1) * half]
            if role == 0:
                piece = jnp.where(seen(rows, own), piece, NEG)
            pieces.append(jnp.exp2(piece - (totals[head : head + 1] - bias_ref[role])))
        probs = jnp.concatenate(pieces, axis=0)
        dv = jnp.dot(probs.astype(BF16), grads, preferred_element_type=F32)
        dp = jnp.dot(values, grads.T, preferred_element_type=F32)
        ds = (probs * (dp - dot)).astype(BF16)
        dk = jnp.dot(ds, queries, preferred_element_type=F32) * FACTOR
        dq = jnp.dot(keys.T, ds, preferred_element_type=F32)
        for role in range(WBLK):
            of = slice(role * half, (role + 1) * half)
            for cols, value in ((2 * head, dk[of]), (2 * head + 1, dv[of])):
                if parts_in:
                    value += parts[role][:, head_slice(cols)].astype(F32)
                sums[role][:, head_slice(cols)] = value.astype(BF16)
            if parts_in:
                stores.append(
                    pltpu.make_async_copy(
                        sums[role].at[:, pair], outs[role].at[:, pair], sems.at[role, head]
                    )
                )
                stores[-1].start()
        dq_acc[:, q_cols] = (dq * FACTOR).T.astype(dq_acc.dtype)
        stores.append(
            pltpu.make_async_copy(
                dq_acc.at[:, q_cols], dq_out.at[:, q_cols], sems.at[WBLK, head]
            )
        )
        stores[-1].start()
    for store in stores:
        store.wait()


def grads(name, common, tokens, own, window, dq_kind, parts=()):
    half = own.shape[0]
    wide = GROUP * HDIM
    pairs = GROUP * half * WBLK * half
    hbm = pl.BlockSpec(memory_space=pl.ANY)
    scratch = [
        pltpu.VMEM((HDIM, half), F32),
        pltpu.VMEM((half, wide), dq_kind),
        pltpu.SemaphoreType.DMA((WBLK + 1, GROUP)),
    ]
    if parts:
        scratch.append(pltpu.VMEM((WBLK, half, 2 * wide), BF16))
    return pl.pallas_call(
        functools.partial(grads_kernel, bool(parts)),
        out_shape=[jax.ShapeDtypeStruct((half, wide), dq_kind)]
        + [jax.ShapeDtypeStruct((half, 2 * wide), BF16)] * WBLK,
        in_specs=[smem(), smem()] + [vmem()] * (4 + WBLK + len(parts)),
        out_specs=[hbm] + [hbm if parts else vmem()] * WBLK,
        scratch_shapes=scratch,
        compiler_params=params(),
        cost_estimate=cost(10 * pairs * HDIM, 12 * half * wide * 2, pairs),
        name=name,
    )(*common, tokens, own, *window, *parts)


def row_block(shape):
    return pl.BlockSpec(shape, lambda step: (step, 0))


def fold_kernel(even_ref, d1, swapped, side, out):
    odd = 1.0 - even_ref[0].astype(F32)
    total = d1[...].astype(F32) + swapped[...].astype(F32) + side[...].astype(F32) * odd
    out[...] = total.astype(BF16)


def fold(even, d1, swapped, side):
    block = row_block((d1.shape[0] // 2, d1.shape[1]))
    return pl.pallas_call(
        fold_kernel,
        grid=(2,),
        out_shape=jax.ShapeDtypeStruct(d1.shape, BF16),
        in_specs=[smem()] + [block] * 3,
        out_specs=block,
        compiler_params=params(),
        cost_estimate=cost(3 * d1.size, 8 * d1.size),
        name="fold",
    )(even, d1, swapped, side)


def close_kernel(even_ref, place, dq_own, dq_back, d0, back, side, out):
    even = even_ref[0].astype(F32)
    wide = dq_own.shape[1]
    owner = pl.ds(lax.rem(place[0] + XN - pl.program_id(0), XN), 1)
    pair = d0[...].astype(F32) + back[...].astype(F32) + side[...].astype(F32) * even
    out[owner, :, :wide] = (dq_own[...] + dq_back[...].astype(F32)).astype(BF16)[None]
    out[owner, :, wide:] = pair.astype(BF16)[None]


def close(even, place, dq_own, dq_back, d0, back, side):
    half, wide = dq_own.shape
    tok = half // XN
    pair = row_block((tok, 2 * wide))
    return pl.pallas_call(
        close_kernel,
        grid=(XN,),
        out_shape=jax.ShapeDtypeStruct((XN, tok, 3 * wide), BF16),
        in_specs=[smem(), smem(), row_block((tok, wide)), row_block((tok, wide)), pair, pair, pair],
        out_specs=pl.BlockSpec((XN, tok, 3 * wide), lambda step: (0, 0, 0)),
        compiler_params=params(),
        cost_estimate=cost(6 * half * wide, 24 * half * wide),
        name="close",
    )(even, place, dq_own, dq_back, d0, back, side)


def unpack_kernel(parts, dq, dk, dv):
    wide = GROUP * HDIM
    for group in range(XN):
        dq[:, group * wide : (group + 1) * wide] = parts[group, :, :wide]
        for h in range(GROUP):
            at = wide + 2 * h * HDIM
            cols = slice((group * GROUP + h) * HDIM, (group * GROUP + h + 1) * HDIM)
            dk[:, cols] = parts[group, :, at : at + HDIM]
            dv[:, cols] = parts[group, :, at + HDIM : at + 2 * HDIM]


def unpack(parts):
    tok = parts.shape[1]
    return pl.pallas_call(
        unpack_kernel,
        out_shape=[jax.ShapeDtypeStruct((tok, HEADS * HDIM), BF16)] * 3,
        in_specs=[vmem()],
        out_specs=[vmem()] * 3,
        compiler_params=params(),
        cost_estimate=cost(0, 12 * tok * HEADS * HDIM),
        name="unpack",
    )(parts)


def over_x(value):
    groups = [[z * XN + x for x in range(XN)] for z in range(lax.axis_size("col") // XN)]
    return lax.all_to_all(value, "col", 0, 0, axis_index_groups=groups)


def gathered_over_x(chunks):
    count = lax.axis_size("col")
    moved = [chunks[0]]
    for step in range(1, XN):
        pairs = [(c, c // XN * XN + (c + step) % XN) for c in range(count)]
        moved.append(lax.ppermute(chunks[step], "col", pairs))
    return jnp.concatenate(moved, axis=0)


def across_z(value):
    count = lax.axis_size("col")
    return lax.ppermute(value, "col", [(c, (c + XN) % count) for c in range(count)])


def along_row(value, steps):
    count = lax.axis_size("row")
    first, last = max(0, -steps), min(count, count - steps)
    return lax.ppermute(value, "row", [(r, r + steps) for r in range(first, last)])


def in_chip(value):
    count = lax.axis_size("row")
    return lax.ppermute(value, "row", [(r, r ^ 1) for r in range(count)])


def own_grads(operands):
    common, own, window, parts, even = operands
    dq_own, d0, d1, d2, d3 = grads("grads_own", common, own, own, window, F32, parts)
    side, swapped = along_row(d3, -1), in_chip(d2)
    return dq_own, d0, along_row(fold(even, d1, swapped, side), -2), side


def no_grads(operands):
    own, window = operands[1:3]
    empty = jnp.zeros_like(window[0])
    return jnp.zeros((own.shape[0], GROUP * HDIM), F32), empty, empty, empty


def per_device(query, key, value, saved_out, grad_out, frame_ids):
    row, col = lax.axis_index("row"), lax.axis_index("col")
    place = jnp.stack([col % XN, col // XN]).astype(jnp.int32)
    is_even = row % 2 == 0
    even = is_even.astype(jnp.int32).reshape(1)

    own = gathered_over_x(pack_queries(place, query, saved_out, grad_out, frame_ids[:, None]))
    w0 = gathered_over_x(pack_keys(place, key, value))
    far = across_z(own)
    w1 = along_row(w0, 2)
    w3 = along_row(jnp.where(is_even, w0, w1), 1)
    w2 = in_chip(w1)
    held = jnp.stack(
        [
            row >= 0,
            row >= 2,
            jnp.where(is_even, row >= 1, row >= 3),
            jnp.where(is_even, row >= 3, row >= 1),
        ]
    )
    bias = jnp.where(held, 0.0, NEG).astype(F32)

    window = (w0, w1, w2, w3)
    own_near = stats("stats_own", bias, own, own, window)
    far_other = across_z(own_near)
    far_near = stats("stats_far", bias, far, own, window)
    own_other = across_z(far_near)

    common = (bias, place, far_near, far_other)
    dq_far, *parts = grads("grads_far", common, far, own, window, BF16)
    dq_far, own_other = lax.optimization_barrier((dq_far, own_other))
    dq_back = across_z(dq_far)
    common = (bias, place, own_near, own_other)
    dq_own, d0, back, side = lax.cond(
        row < lax.axis_size("row"), own_grads, no_grads, (common, own, window, parts, even)
    )
    return tuple(unpack(over_x(close(even, place, dq_own, dq_back, d0, back, side))))


def solution(mesh):
    placed = P(("row", "col"), None)
    return jax.shard_map(
        per_device,
        mesh=mesh,
        in_specs=(placed,) * 5 + (P(("row", "col")),),
        out_specs=(placed,) * 3,
        check_vma=False,
    )
```

```python
import functools
import math

import jax
import jax.numpy as jnp
from jax import lax
from jax.experimental import pallas as pl
from jax.experimental.pallas import tpu as pltpu
from jax.sharding import PartitionSpec as P

HEADS = 20
HDIM = 128
WBLK = 4
XN = 4
GROUP = HEADS // XN
NEG = -1e30
FACTOR = HDIM ** (-0.5)
SCALE2 = FACTOR * math.log2(math.e)
LOW_LANE = 32
FRAME_LANE = 64
BF16 = jnp.bfloat16
F32 = jnp.float32


def params(room=20):
    return pltpu.CompilerParams(vmem_limit_bytes=room * 1024 * 1024)


def cost(flops, moved, exps=0):
    return pl.CostEstimate(flops=flops, bytes_accessed=moved, transcendentals=exps)


def load_all(sources, held, sems):
    copies = [
        pltpu.make_async_copy(src, held.at[at], sems.at[at]) for at, src in enumerate(sources)
    ]
    for copy in copies:
        copy.start()
    for copy in copies:
        copy.wait()


def pack_queries_kernel(q_any, o_any, g_any, f_ref, out, held, sems):
    load_all((q_any, o_any, g_any), held, sems)
    tok = held.shape[1]
    wide = GROUP * HDIM
    lane = lax.broadcasted_iota(jnp.int32, (tok, HDIM), 1)
    meta = jnp.where(lane == FRAME_LANE, f_ref[...].astype(F32), 0.0)
    for head in range(HEADS):
        cols = slice(head * HDIM, (head + 1) * HDIM)
        product = held[2, :, cols].astype(F32) * held[1, :, cols].astype(F32)
        dot = jnp.sum(product, axis=1, keepdims=True)
        high = dot.astype(BF16).astype(F32)
        meta = jnp.where(lane == head, high, meta)
        meta = jnp.where(lane == LOW_LANE + head, dot - high, meta)
    meta = meta.astype(BF16)
    for group in range(XN):
        here = slice(group * wide, (group + 1) * wide)
        out[group, :, :wide] = held[0, :, here]
        out[group, :, wide : 2 * wide] = held[2, :, here]
        out[group, :, 2 * wide :] = meta


def pack_queries(query, saved_out, grad_out, frames):
    tok, width = query.shape
    shape = (XN, tok, 2 * GROUP * HDIM + HDIM)
    return pl.pallas_call(
        pack_queries_kernel,
        out_shape=jax.ShapeDtypeStruct(shape, BF16),
        in_specs=[pl.BlockSpec(memory_space=pl.ANY)] * 3 + [vmem()],
        out_specs=vmem(),
        scratch_shapes=[pltpu.VMEM((3, tok, width), BF16), pltpu.SemaphoreType.DMA((3,))],
        compiler_params=params(60),
        cost_estimate=cost(2 * tok * width, 14 * tok * width),
        name="pack_queries",
    )(query, saved_out, grad_out, frames)


def pack_keys_kernel(near, far, out):
    for head in range(HEADS):
        group, h = divmod(head, GROUP)
        cols = slice(head * HDIM, (head + 1) * HDIM)
        for block, ref in enumerate((near, far)):
            for at in range(2):
                first = (2 * (block * GROUP + h) + at) * HDIM
                out[group, :, first : first + HDIM] = ref[at, :, cols]


def pack_keys(near, far):
    _, tok, width = near.shape
    return pl.pallas_call(
        pack_keys_kernel,
        out_shape=jax.ShapeDtypeStruct((XN, tok, 4 * GROUP * HDIM), BF16),
        in_specs=[vmem()] * 2,
        out_specs=vmem(),
        compiler_params=params(),
        cost_estimate=cost(0, 16 * tok * width),
        name="pack_keys",
    )(near, far)


META = slice(2 * GROUP * HDIM, (2 * GROUP + 1) * HDIM)


def head_slice(at):
    return slice(at * HDIM, (at + 1) * HDIM)


def seen(rows, own_meta):
    k_frame = own_meta.astype(F32)[:, FRAME_LANE : FRAME_LANE + 1]
    return k_frame <= rows[FRAME_LANE : FRAME_LANE + 1, :]


def stats_kernel(bias_ref, tokens, own, near, w2, w3, out_ref):
    half = own.shape[0]
    mask = seen(tokens[:, META].astype(F32).T, own[:, META])
    out_ref[...] = jnp.zeros_like(out_ref)
    for head in range(GROUP):
        queries = tokens[:, head_slice(head)].T
        at = head_slice(2 * head)
        keys = [near[:, at], near[:, head_slice(2 * (GROUP + head))], w2[:, at], w3[:, at]]
        scores = jnp.dot(
            jnp.concatenate(keys, axis=0), queries, preferred_element_type=F32
        ) * SCALE2
        parts = [scores[role * half : (role + 1) * half] for role in range(4)]
        parts[0] = jnp.where(mask, parts[0], NEG)
        peaks = [
            jnp.max(part, axis=0, keepdims=True) + bias_ref[role]
            for role, part in enumerate(parts)
        ]
        peak = functools.reduce(jnp.maximum, peaks)
        total = jnp.zeros_like(peak)
        for role, part in enumerate(parts):
            total += jnp.sum(jnp.exp2(part - (peak - bias_ref[role])), axis=0, keepdims=True)
        out_ref[head : head + 1, :] = peak
        out_ref[8 + head : 9 + head, :] = total


def smem():
    return pl.BlockSpec(memory_space=pltpu.SMEM)


def vmem():
    return pl.BlockSpec(memory_space=pltpu.VMEM)


def stats(name, bias, tokens, own, window):
    half = own.shape[0]
    pairs = GROUP * half * 4 * half
    return pl.pallas_call(
        stats_kernel,
        out_shape=jax.ShapeDtypeStruct((16, half), F32),
        in_specs=[smem()] + [vmem()] * 5,
        out_specs=vmem(),
        compiler_params=params(),
        cost_estimate=cost(4 * pairs * HDIM, 5 * half * GROUP * HDIM * 2, pairs),
        name=name,
    )(bias, tokens, own, *window)


def log_total(one, other):
    one_peak, one_sum = one[:8, :], one[8:, :]
    other_peak, other_sum = other[:8, :], other[8:, :]
    peak = jnp.maximum(one_peak, other_peak)
    one_part = one_sum * jnp.exp2(one_peak - peak)
    return peak + jnp.log2(one_part + other_sum * jnp.exp2(other_peak - peak))


def pair_slice(head):
    return slice(2 * head * HDIM, 2 * (head + 1) * HDIM)


def grads_kernel(parts_in, bias_ref, place, one, other, tokens, own, near, w2, w3, *rest):
    if parts_in:
        parts, rest = rest[:WBLK], rest[WBLK:]
    dq_out, *outs = rest[: 1 + WBLK]
    rest = rest[1 + WBLK :]
    rows, dq_acc, sums, window, held, k_meta, load_sems, sems, *rest = rest
    half = rows.shape[1]

    metas = [
        pltpu.make_async_copy(tokens.at[:, META], held.at[:, META], load_sems.at[GROUP, 0]),
        pltpu.make_async_copy(own.at[:, META], k_meta, load_sems.at[GROUP, 1]),
    ]
    loads = []
    for head in range(GROUP):
        at = pair_slice(head)
        moves = [
            (near.at[:, at], window.at[0, :, at]),
            (near.at[:, pair_slice(GROUP + head)], window.at[1, :, at]),
            (w2.at[:, at], window.at[2, :, at]),
            (w3.at[:, at], window.at[3, :, at]),
        ]
        for cols in (head_slice(head), head_slice(GROUP + head)):
            moves.append((tokens.at[:, cols], held.at[:, cols]))
        if parts_in:
            moves += [(part.at[:, at], rest[0].at[role, :, at]) for role, part in enumerate(parts)]
        loads.append(
            [
                pltpu.make_async_copy(src, dst, load_sems.at[head, i])
                for i, (src, dst) in enumerate(moves)
            ]
        )
    for copy in metas + sum(loads, []):
        copy.start()
    for copy in metas:
        copy.wait()

    rows[...] = held[:, META].astype(F32).T
    mask = seen(rows, k_meta[...])
    totals = log_total(one, other)
    stores = []
    for head in range(GROUP):
        for copy in loads[head]:
            copy.wait()
        q_cols = head_slice(head)
        queries, grads = held[:, q_cols], held[:, head_slice(GROUP + head)]
        first = place[0] * GROUP + head
        dot = rows[pl.ds(first, 1), :] + rows[pl.ds(LOW_LANE + first, 1), :]
        keys = window[:, :, head_slice(2 * head)].reshape(WBLK * half, HDIM)
        values = window[:, :, head_slice(2 * head + 1)].reshape(WBLK * half, HDIM)
        scores = jnp.dot(keys, queries.T, preferred_element_type=F32) * SCALE2
        pieces = []
        for role in range(WBLK):
            piece = scores[role * half : (role + 1) * half]
            if role == 0:
                piece = jnp.where(mask, piece, NEG)
            pieces.append(jnp.exp2(piece - (totals[head : head + 1] - bias_ref[role])))
        probs = jnp.concatenate(pieces, axis=0)
        dv = jnp.dot(probs.astype(BF16), grads, preferred_element_type=F32)
        dp = jnp.dot(values, grads.T, preferred_element_type=F32)
        ds = (probs * (dp - dot)).astype(BF16)
        dk = jnp.dot(ds, queries, preferred_element_type=F32) * FACTOR
        dq = jnp.dot(keys.T, ds, preferred_element_type=F32)
        for role in range(WBLK):
            of = slice(role * half, (role + 1) * half)
            for cols, value in ((2 * head, dk[of]), (2 * head + 1, dv[of])):
                if parts_in:
                    value += rest[0][role, :, head_slice(cols)].astype(F32)
                sums[role, :, head_slice(cols)] = value.astype(BF16)
            at = pair_slice(head)
            stores.append(
                pltpu.make_async_copy(
                    sums.at[role, :, at], outs[role].at[:, at], sems.at[head, role]
                )
            )
            stores[-1].start()
        dq_acc[:, q_cols] = (dq * FACTOR).T.astype(dq_acc.dtype)
        stores.append(
            pltpu.make_async_copy(
                dq_acc.at[:, q_cols], dq_out.at[:, q_cols], sems.at[head, WBLK]
            )
        )
        stores[-1].start()
    for store in stores:
        store.wait()


def grads(name, common, tokens, own, window, dq_kind, parts=()):
    half = own.shape[0]
    wide = GROUP * HDIM
    pairs = GROUP * half * WBLK * half
    hbm = pl.BlockSpec(memory_space=pl.ANY)
    blocks = pltpu.VMEM((WBLK, half, 2 * wide), BF16)
    scratch = [
        pltpu.VMEM((HDIM, half), F32),
        pltpu.VMEM((half, wide), dq_kind),
        blocks,
        blocks,
        pltpu.VMEM(tokens.shape, BF16),
        pltpu.VMEM((half, HDIM), BF16),
        pltpu.SemaphoreType.DMA((GROUP + 1, 2 * WBLK + 2)),
        pltpu.SemaphoreType.DMA((GROUP, WBLK + 1)),
    ]
    return pl.pallas_call(
        functools.partial(grads_kernel, bool(parts)),
        out_shape=[jax.ShapeDtypeStruct((half, wide), dq_kind)]
        + [jax.ShapeDtypeStruct((half, 2 * wide), BF16)] * WBLK,
        in_specs=[smem(), smem(), vmem(), vmem()] + [hbm] * (5 + len(parts)),
        out_specs=[hbm] * (1 + WBLK),
        scratch_shapes=scratch + [blocks] * bool(parts),
        compiler_params=params(28),
        cost_estimate=cost(10 * pairs * HDIM, 12 * half * wide * 2, pairs),
        name=name,
    )(*common, tokens, own, *window, *parts)


def row_block(shape):
    return pl.BlockSpec(shape, lambda step: (step, 0))


def fold_kernel(even_ref, d1, swapped, side, out):
    odd = 1.0 - even_ref[0].astype(F32)
    total = d1[...].astype(F32) + swapped[...].astype(F32) + side[...].astype(F32) * odd
    out[...] = total.astype(BF16)


def fold(even, d1, swapped, side):
    block = row_block((d1.shape[0] // 2, d1.shape[1]))
    return pl.pallas_call(
        fold_kernel,
        grid=(2,),
        out_shape=jax.ShapeDtypeStruct(d1.shape, BF16),
        in_specs=[smem()] + [block] * 3,
        out_specs=block,
        compiler_params=params(),
        cost_estimate=cost(3 * d1.size, 8 * d1.size),
        name="fold",
    )(even, d1, swapped, side)


def close_kernel(even_ref, dq_own, dq_back, d0, back, side, out):
    even = even_ref[0].astype(F32)
    wide = dq_own.shape[1]
    pair = d0[...].astype(F32) + back[...].astype(F32) + side[...].astype(F32) * even
    out[0, :, :wide] = (dq_own[...] + dq_back[...].astype(F32)).astype(BF16)
    out[0, :, wide:] = pair.astype(BF16)


def close(even, dq_own, dq_back, d0, back, side):
    half, wide = dq_own.shape
    tok = half // XN
    pair = row_block((tok, 2 * wide))
    return pl.pallas_call(
        close_kernel,
        grid=(XN,),
        out_shape=jax.ShapeDtypeStruct((XN, tok, 3 * wide), BF16),
        in_specs=[smem(), row_block((tok, wide)), row_block((tok, wide)), pair, pair, pair],
        out_specs=pl.BlockSpec((1, tok, 3 * wide), lambda step: (step, 0, 0)),
        compiler_params=params(),
        cost_estimate=cost(6 * half * wide, 24 * half * wide),
        name="close",
    )(even, dq_own, dq_back, d0, back, side)


def unpack_kernel(parts, dq, dk, dv):
    wide = GROUP * HDIM
    for group in range(XN):
        dq[:, group * wide : (group + 1) * wide] = parts[group, :, :wide]
        for h in range(GROUP):
            at = wide + 2 * h * HDIM
            cols = slice((group * GROUP + h) * HDIM, (group * GROUP + h + 1) * HDIM)
            dk[:, cols] = parts[group, :, at : at + HDIM]
            dv[:, cols] = parts[group, :, at + HDIM : at + 2 * HDIM]


def unpack(parts):
    tok = parts.shape[1]
    return pl.pallas_call(
        unpack_kernel,
        out_shape=[jax.ShapeDtypeStruct((tok, HEADS * HDIM), BF16)] * 3,
        in_specs=[vmem()],
        out_specs=[vmem()] * 3,
        compiler_params=params(),
        cost_estimate=cost(0, 12 * tok * HEADS * HDIM),
        name="unpack",
    )(parts)


def over_x(value):
    groups = [[z * XN + x for x in range(XN)] for z in range(lax.axis_size("col") // XN)]
    return lax.all_to_all(value, "col", 0, 0, axis_index_groups=groups)


def across_z(value):
    count = lax.axis_size("col")
    return lax.ppermute(value, "col", [(c, (c + XN) % count) for c in range(count)])


def along_row(value, steps):
    count = lax.axis_size("row")
    first, last = max(0, -steps), min(count, count - steps)
    return lax.ppermute(value, "row", [(r, r + steps) for r in range(first, last)])


def in_chip(value):
    count = lax.axis_size("row")
    return lax.ppermute(value, "row", [(r, r ^ 1) for r in range(count)])


def own_grads(operands):
    common, own, window, parts, even = operands
    dq_own, d0, d1, d2, d3 = grads("grads_own", common, own, own, window, F32, parts)
    side, swapped = along_row(d3, -1), in_chip(d2)
    return dq_own, d0, along_row(fold(even, d1, swapped, side), -2), side


def no_grads(operands):
    own, window = operands[1:3]
    empty = jnp.zeros_like(window[1])
    return jnp.zeros((own.shape[0], GROUP * HDIM), F32), empty, empty, empty


def per_device(query, key, value, saved_out, grad_out, frame_ids):
    row, col = lax.axis_index("row"), lax.axis_index("col")
    place = jnp.stack([col % XN, col // XN]).astype(jnp.int32)
    is_even = row % 2 == 0
    even = is_even.astype(jnp.int32).reshape(1)
    tok = query.shape[0]
    half = XN * tok
    wide = 2 * GROUP * HDIM

    kv = jnp.stack([key, value])
    kv_far = along_row(kv, 2)
    own = over_x(pack_queries(query, saved_out, grad_out, frame_ids[:, None])).reshape(half, -1)
    far = across_z(own)
    near = over_x(pack_keys(kv, kv_far)).reshape(half, -1)
    w0, w1 = near[:, :wide], near[:, wide:]
    w3 = along_row(jnp.where(is_even, w0, w1), 1)
    w2 = in_chip(w1)
    held = jnp.stack(
        [
            row >= 0,
            row >= 2,
            jnp.where(is_even, row >= 1, row >= 3),
            jnp.where(is_even, row >= 3, row >= 1),
        ]
    )
    bias = jnp.where(held, 0.0, NEG).astype(F32)

    window = (near, w2, w3)
    own_near = stats("stats_own", bias, own, own, window)
    far_other = across_z(own_near)
    far_near = stats("stats_far", bias, far, own, window)
    own_other = across_z(far_near)

    common = (bias, place, far_near, far_other)
    dq_far, *parts = grads("grads_far", common, far, own, window, BF16)
    dq_far, own_other = lax.optimization_barrier((dq_far, own_other))
    dq_back = across_z(dq_far)
    common = (bias, place, own_near, own_other)
    dq_own, d0, back, side = lax.cond(
        row < lax.axis_size("row"), own_grads, no_grads, (common, own, window, parts, even)
    )
    return tuple(unpack(over_x(close(even, dq_own, dq_back, d0, back, side))))


def solution(mesh):
    placed = P(("row", "col"), None)
    return jax.shard_map(
        per_device,
        mesh=mesh,
        in_specs=(placed,) * 5 + (P(("row", "col")),),
        out_specs=(placed,) * 3,
        check_vma=False,
    )
```

```python
import functools
import math

import jax
import jax.numpy as jnp
from jax import lax
from jax.experimental import pallas as pl
from jax.experimental.pallas import tpu as pltpu
from jax.sharding import PartitionSpec as P

HEADS = 20
HDIM = 128
WBLK = 4
XN = 4
GROUP = HEADS // XN
NEG = -1e30
FACTOR = HDIM ** (-0.5)
SCALE2 = FACTOR * math.log2(math.e)
LOW_LANE = 32
FRAME_LANE = 64
BF16 = jnp.bfloat16
F32 = jnp.float32


def params(room=20):
    return pltpu.CompilerParams(vmem_limit_bytes=room * 1024 * 1024)


def cost(flops, moved, exps=0):
    return pl.CostEstimate(flops=flops, bytes_accessed=moved, transcendentals=exps)


def load_all(sources, held, sems):
    copies = [
        pltpu.make_async_copy(src, held.at[at], sems.at[at]) for at, src in enumerate(sources)
    ]
    for copy in copies:
        copy.start()
    for copy in copies:
        copy.wait()


def pack_queries_kernel(q_any, o_any, g_any, f_ref, out, held, sems):
    load_all((q_any, o_any, g_any), held, sems)
    tok = held.shape[1]
    wide = GROUP * HDIM
    lane = lax.broadcasted_iota(jnp.int32, (tok, HDIM), 1)
    here = lax.broadcasted_iota(jnp.int32, (tok, tok), 0)
    same = here == lax.broadcasted_iota(jnp.int32, (tok, tok), 1)
    frame = jnp.sum(jnp.where(same, f_ref[...].astype(F32), 0.0), axis=1, keepdims=True)
    meta = jnp.where(lane == FRAME_LANE, frame, 0.0)
    for head in range(HEADS):
        cols = slice(head * HDIM, (head + 1) * HDIM)
        product = held[2, :, cols].astype(F32) * held[1, :, cols].astype(F32)
        dot = jnp.sum(product, axis=1, keepdims=True)
        high = dot.astype(BF16).astype(F32)
        meta = jnp.where(lane == head, high, meta)
        meta = jnp.where(lane == LOW_LANE + head, dot - high, meta)
    meta = meta.astype(BF16)
    for group in range(XN):
        here = slice(group * wide, (group + 1) * wide)
        out[group, :, :wide] = held[0, :, here]
        out[group, :, wide : 2 * wide] = held[2, :, here]
        out[group, :, 2 * wide :] = meta


def pack_queries(query, saved_out, grad_out, frames):
    tok, width = query.shape
    shape = (XN, tok, 2 * GROUP * HDIM + HDIM)
    return pl.pallas_call(
        pack_queries_kernel,
        out_shape=jax.ShapeDtypeStruct(shape, BF16),
        in_specs=[pl.BlockSpec(memory_space=pl.ANY)] * 3 + [vmem()],
        out_specs=vmem(),
        scratch_shapes=[pltpu.VMEM((3, tok, width), BF16), pltpu.SemaphoreType.DMA((3,))],
        compiler_params=params(60),
        cost_estimate=cost(2 * tok * width, 14 * tok * width),
        name="pack_queries",
    )(query, saved_out, grad_out, frames)


def pack_keys_kernel(near, far, out):
    for head in range(HEADS):
        group, h = divmod(head, GROUP)
        cols = slice(head * HDIM, (head + 1) * HDIM)
        for block, ref in enumerate((near, far)):
            for at in range(2):
                first = (2 * (block * GROUP + h) + at) * HDIM
                out[group, :, first : first + HDIM] = ref[at, :, cols]


def pack_keys(near, far):
    _, tok, width = near.shape
    return pl.pallas_call(
        pack_keys_kernel,
        out_shape=jax.ShapeDtypeStruct((XN, tok, 4 * GROUP * HDIM), BF16),
        in_specs=[vmem()] * 2,
        out_specs=vmem(),
        compiler_params=params(),
        cost_estimate=cost(0, 16 * tok * width),
        name="pack_keys",
    )(near, far)


META = slice(2 * GROUP * HDIM, (2 * GROUP + 1) * HDIM)


def head_slice(at):
    return slice(at * HDIM, (at + 1) * HDIM)


def seen(rows, own_meta):
    k_frame = own_meta.astype(F32)[:, FRAME_LANE : FRAME_LANE + 1]
    return k_frame <= rows[FRAME_LANE : FRAME_LANE + 1, :]


def stats_kernel(bias_ref, tokens, own, near, w2, w3, out_ref):
    half = own.shape[0]
    mask = seen(tokens[:, META].astype(F32).T, own[:, META])
    out_ref[...] = jnp.zeros_like(out_ref)
    for head in range(GROUP):
        queries = tokens[:, head_slice(head)].T
        at = head_slice(2 * head)
        keys = [near[:, at], near[:, head_slice(2 * (GROUP + head))], w2[:, at], w3[:, at]]
        scores = jnp.dot(
            jnp.concatenate(keys, axis=0), queries, preferred_element_type=F32
        ) * SCALE2
        parts = [scores[role * half : (role + 1) * half] for role in range(4)]
        parts[0] = jnp.where(mask, parts[0], NEG)
        peaks = [
            jnp.max(part, axis=0, keepdims=True) + bias_ref[role]
            for role, part in enumerate(parts)
        ]
        peak = functools.reduce(jnp.maximum, peaks)
        total = jnp.zeros_like(peak)
        for role, part in enumerate(parts):
            total += jnp.sum(jnp.exp2(part - (peak - bias_ref[role])), axis=0, keepdims=True)
        out_ref[head : head + 1, :] = peak
        out_ref[8 + head : 9 + head, :] = total


def smem():
    return pl.BlockSpec(memory_space=pltpu.SMEM)


def vmem():
    return pl.BlockSpec(memory_space=pltpu.VMEM)


def stats(name, bias, tokens, own, window):
    half = own.shape[0]
    pairs = GROUP * half * 4 * half
    return pl.pallas_call(
        stats_kernel,
        out_shape=jax.ShapeDtypeStruct((16, half), F32),
        in_specs=[smem()] + [vmem()] * 5,
        out_specs=vmem(),
        compiler_params=params(),
        cost_estimate=cost(4 * pairs * HDIM, 5 * half * GROUP * HDIM * 2, pairs),
        name=name,
    )(bias, tokens, own, *window)


def log_total(one, other):
    one_peak, one_sum = one[:8, :], one[8:, :]
    other_peak, other_sum = other[:8, :], other[8:, :]
    peak = jnp.maximum(one_peak, other_peak)
    one_part = one_sum * jnp.exp2(one_peak - peak)
    return peak + jnp.log2(one_part + other_sum * jnp.exp2(other_peak - peak))


def grads_kernel(parts_in, bias_ref, place, one, other, tokens, own, near, w2, w3, *rest):
    if parts_in:
        parts, rest = rest[:WBLK], rest[WBLK:]
    dq_out, *outs = rest[: 1 + WBLK]
    rest = rest[1 + WBLK :]
    rows, dq_acc, sums, window, held, k_meta, load_sems, sems, *rest = rest
    half = rows.shape[1]

    moves = [
        (own.at[:, META], k_meta),
        (tokens, held),
        (near.at[:, : 2 * GROUP * HDIM], window.at[0]),
        (near.at[:, 2 * GROUP * HDIM :], window.at[1]),
        (w2, window.at[2]),
        (w3, window.at[3]),
    ]
    if parts_in:
        moves += [(part, rest[0].at[role]) for role, part in enumerate(parts)]
    loads = [
        pltpu.make_async_copy(src, dst, load_sems.at[i]) for i, (src, dst) in enumerate(moves)
    ]
    for load in loads:
        load.start()
    for load in loads:
        load.wait()

    rows[...] = held[:, META].astype(F32).T
    mask = seen(rows, k_meta[...])
    totals = log_total(one, other)
    for head in range(GROUP):
        q_cols = head_slice(head)
        queries, grads = held[:, q_cols], held[:, head_slice(GROUP + head)]
        first = place[0] * GROUP + head
        dot = rows[pl.ds(first, 1), :] + rows[pl.ds(LOW_LANE + first, 1), :]
        keys = window[:, :, head_slice(2 * head)].reshape(WBLK * half, HDIM)
        values = window[:, :, head_slice(2 * head + 1)].reshape(WBLK * half, HDIM)
        scores = jnp.dot(keys, queries.T, preferred_element_type=F32) * SCALE2
        pieces = []
        for role in range(WBLK):
            piece = scores[role * half : (role + 1) * half]
            if role == 0:
                piece = jnp.where(mask, piece, NEG)
            pieces.append(jnp.exp2(piece - (totals[head : head + 1] - bias_ref[role])))
        probs = jnp.concatenate(pieces, axis=0)
        dv = jnp.dot(probs.astype(BF16), grads, preferred_element_type=F32)
        dp = jnp.dot(values, grads.T, preferred_element_type=F32)
        ds = (probs * (dp - dot)).astype(BF16)
        dk = jnp.dot(ds, queries, preferred_element_type=F32) * FACTOR
        dq = jnp.dot(keys.T, ds, preferred_element_type=F32)
        for role in range(WBLK):
            of = slice(role * half, (role + 1) * half)
            for cols, value in ((2 * head, dk[of]), (2 * head + 1, dv[of])):
                if parts_in:
                    value += rest[0][role, :, head_slice(cols)].astype(F32)
                sums[role, :, head_slice(cols)] = value.astype(BF16)
        dq_acc[:, q_cols] = (dq * FACTOR).T.astype(dq_acc.dtype)
    stores = [pltpu.make_async_copy(dq_acc, dq_out, sems.at[WBLK])]
    for role in range(WBLK):
        stores.append(pltpu.make_async_copy(sums.at[role], outs[role], sems.at[role]))
    for store in stores:
        store.start()
    for store in stores:
        store.wait()


def grads(name, common, tokens, own, window, dq_kind, parts=()):
    half = own.shape[0]
    wide = GROUP * HDIM
    pairs = GROUP * half * WBLK * half
    hbm = pl.BlockSpec(memory_space=pl.ANY)
    blocks = pltpu.VMEM((WBLK, half, 2 * wide), BF16)
    scratch = [
        pltpu.VMEM((HDIM, half), F32),
        pltpu.VMEM((half, wide), dq_kind),
        blocks,
        blocks,
        pltpu.VMEM(tokens.shape, BF16),
        pltpu.VMEM((half, HDIM), BF16),
        pltpu.SemaphoreType.DMA((2 * WBLK + 2,)),
        pltpu.SemaphoreType.DMA((WBLK + 1,)),
    ]
    return pl.pallas_call(
        functools.partial(grads_kernel, bool(parts)),
        out_shape=[jax.ShapeDtypeStruct((half, wide), dq_kind)]
        + [jax.ShapeDtypeStruct((half, 2 * wide), BF16)] * WBLK,
        in_specs=[smem(), smem(), vmem(), vmem()] + [hbm] * (5 + len(parts)),
        out_specs=[hbm] * (1 + WBLK),
        scratch_shapes=scratch + [blocks] * bool(parts),
        compiler_params=params(28),
        cost_estimate=cost(10 * pairs * HDIM, 12 * half * wide * 2, pairs),
        name=name,
    )(*common, tokens, own, *window, *parts)


def row_block(shape):
    return pl.BlockSpec(shape, lambda step: (step, 0))


def fold_kernel(even_ref, d1, swapped, side, out):
    odd = 1.0 - even_ref[0].astype(F32)
    total = d1[...].astype(F32) + swapped[...].astype(F32) + side[...].astype(F32) * odd
    out[...] = total.astype(BF16)


def fold(even, d1, swapped, side):
    block = row_block((d1.shape[0] // 2, d1.shape[1]))
    return pl.pallas_call(
        fold_kernel,
        grid=(2,),
        out_shape=jax.ShapeDtypeStruct(d1.shape, BF16),
        in_specs=[smem()] + [block] * 3,
        out_specs=block,
        compiler_params=params(),
        cost_estimate=cost(3 * d1.size, 8 * d1.size),
        name="fold",
    )(even, d1, swapped, side)


def close_kernel(even_ref, dq_own, dq_back, d0, back, side, out, mine, theirs, pairs, sems):
    even = even_ref[0].astype(F32)
    moves = [(dq_own, mine), (dq_back, theirs)]
    moves += [(src, pairs.at[at]) for at, src in enumerate((d0, back, side))]
    loads = [pltpu.make_async_copy(src, dst, sems.at[i]) for i, (src, dst) in enumerate(moves)]
    for load in loads:
        load.start()
    for load in loads:
        load.wait()
    tok = out.shape[1]
    wide = mine.shape[1]
    for step in range(XN):
        rows = slice(step * tok, (step + 1) * tok)
        pair = pairs[0, rows, :].astype(F32) + pairs[1, rows, :].astype(F32)
        pair += pairs[2, rows, :].astype(F32) * even
        out[step, :, :wide] = (mine[rows, :] + theirs[rows, :].astype(F32)).astype(BF16)
        out[step, :, wide:] = pair.astype(BF16)


def close(even, dq_own, dq_back, d0, back, side):
    half, wide = dq_own.shape
    tok = half // XN
    return pl.pallas_call(
        close_kernel,
        out_shape=jax.ShapeDtypeStruct((XN, tok, 3 * wide), BF16),
        in_specs=[smem()] + [pl.BlockSpec(memory_space=pl.ANY)] * 5,
        out_specs=vmem(),
        scratch_shapes=[
            pltpu.VMEM((half, wide), F32),
            pltpu.VMEM((half, wide), BF16),
            pltpu.VMEM((3, half, 2 * wide), BF16),
            pltpu.SemaphoreType.DMA((5,)),
        ],
        compiler_params=params(),
        cost_estimate=cost(6 * half * wide, 24 * half * wide),
        name="close",
    )(even, dq_own, dq_back, d0, back, side)


def unpack_kernel(parts, dq, dk, dv):
    wide = GROUP * HDIM
    for group in range(XN):
        dq[:, group * wide : (group + 1) * wide] = parts[group, :, :wide]
        for h in range(GROUP):
            at = wide + 2 * h * HDIM
            cols = slice((group * GROUP + h) * HDIM, (group * GROUP + h + 1) * HDIM)
            dk[:, cols] = parts[group, :, at : at + HDIM]
            dv[:, cols] = parts[group, :, at + HDIM : at + 2 * HDIM]


def unpack(parts):
    tok = parts.shape[1]
    return pl.pallas_call(
        unpack_kernel,
        out_shape=[jax.ShapeDtypeStruct((tok, HEADS * HDIM), BF16)] * 3,
        in_specs=[vmem()],
        out_specs=[vmem()] * 3,
        compiler_params=params(),
        cost_estimate=cost(0, 12 * tok * HEADS * HDIM),
        name="unpack",
    )(parts)


def over_x(value):
    groups = [[z * XN + x for x in range(XN)] for z in range(lax.axis_size("col") // XN)]
    return lax.all_to_all(value, "col", 0, 0, axis_index_groups=groups)


def across_z(value):
    count = lax.axis_size("col")
    return lax.ppermute(value, "col", [(c, (c + XN) % count) for c in range(count)])


def along_row(value, steps):
    count = lax.axis_size("row")
    first, last = max(0, -steps), min(count, count - steps)
    return lax.ppermute(value, "row", [(r, r + steps) for r in range(first, last)])


def in_chip(value):
    count = lax.axis_size("row")
    return lax.ppermute(value, "row", [(r, r ^ 1) for r in range(count)])


def own_grads(operands):
    common, own, window, parts, even = operands
    dq_own, d0, d1, d2, d3 = grads("grads_own", common, own, own, window, F32, parts)
    side, swapped = along_row(d3, -1), in_chip(d2)
    return dq_own, d0, along_row(fold(even, d1, swapped, side), -2), side


def no_grads(operands):
    own, window = operands[1:3]
    empty = jnp.zeros_like(window[1])
    return jnp.zeros((own.shape[0], GROUP * HDIM), F32), empty, empty, empty


def per_device(query, key, value, saved_out, grad_out, frame_ids):
    row, col = lax.axis_index("row"), lax.axis_index("col")
    place = jnp.stack([col % XN, col // XN]).astype(jnp.int32)
    is_even = row % 2 == 0
    even = is_even.astype(jnp.int32).reshape(1)
    tok = query.shape[0]
    half = XN * tok
    wide = 2 * GROUP * HDIM

    kv = jnp.stack([key, value])
    kv_far = along_row(kv, 2)
    own = over_x(pack_queries(query, saved_out, grad_out, frame_ids[None, :])).reshape(half, -1)
    far = across_z(own)
    near = over_x(pack_keys(kv, kv_far)).reshape(half, -1)
    w0, w1 = near[:, :wide], near[:, wide:]
    w3 = along_row(jnp.where(is_even, w0, w1), 1)
    w2 = in_chip(w1)
    held = jnp.stack(
        [
            row >= 0,
            row >= 2,
            jnp.where(is_even, row >= 1, row >= 3),
            jnp.where(is_even, row >= 3, row >= 1),
        ]
    )
    bias = jnp.where(held, 0.0, NEG).astype(F32)

    window = (near, w2, w3)
    own_near = stats("stats_own", bias, own, own, window)
    far_other = across_z(own_near)
    far_near = stats("stats_far", bias, far, own, window)
    own_other = across_z(far_near)

    common = (bias, place, far_near, far_other)
    dq_far, *parts = grads("grads_far", common, far, own, window, BF16)
    dq_far, own_other = lax.optimization_barrier((dq_far, own_other))
    dq_back = across_z(dq_far)
    common = (bias, place, own_near, own_other)
    dq_own, d0, back, side = lax.cond(
        row < lax.axis_size("row"), own_grads, no_grads, (common, own, window, parts, even)
    )
    return tuple(unpack(over_x(close(even, dq_own, dq_back, d0, back, side))))


def solution(mesh):
    placed = P(("row", "col"), None)
    return jax.shard_map(
        per_device,
        mesh=mesh,
        in_specs=(placed,) * 5 + (P(("row", "col")),),
        out_specs=(placed,) * 3,
        check_vma=False,
    )
```

```python
import functools
import math

import jax
import jax.numpy as jnp
from jax import lax
from jax.experimental import pallas as pl
from jax.experimental.pallas import tpu as pltpu
from jax.sharding import PartitionSpec as P

HEADS = 20
HDIM = 128
WBLK = 4
XN = 4
GROUP = HEADS // XN
NEG = -1e30
FACTOR = HDIM ** (-0.5)
SCALE2 = FACTOR * math.log2(math.e)
LOW_LANE = 32
FRAME_LANE = 64
BF16 = jnp.bfloat16
F32 = jnp.float32


def params(room=20):
    return pltpu.CompilerParams(vmem_limit_bytes=room * 1024 * 1024)


def cost(flops, moved, exps=0):
    return pl.CostEstimate(flops=flops, bytes_accessed=moved, transcendentals=exps)


def load_all(sources, held, sems):
    copies = [
        pltpu.make_async_copy(src, held.at[at], sems.at[at]) for at, src in enumerate(sources)
    ]
    for copy in copies:
        copy.start()
    for copy in copies:
        copy.wait()


def pack_queries_kernel(q_any, o_any, g_any, f_ref, out, held, sems):
    load_all((q_any, o_any, g_any), held, sems)
    tok = held.shape[1]
    wide = GROUP * HDIM
    lane = lax.broadcasted_iota(jnp.int32, (tok, HDIM), 1)
    here = lax.broadcasted_iota(jnp.int32, (tok, tok), 0)
    same = here == lax.broadcasted_iota(jnp.int32, (tok, tok), 1)
    frame = jnp.sum(jnp.where(same, f_ref[...].astype(F32), 0.0), axis=1, keepdims=True)
    meta = jnp.where(lane == FRAME_LANE, frame, 0.0)
    for head in range(HEADS):
        cols = slice(head * HDIM, (head + 1) * HDIM)
        product = held[2, :, cols].astype(F32) * held[1, :, cols].astype(F32)
        dot = jnp.sum(product, axis=1, keepdims=True)
        high = dot.astype(BF16).astype(F32)
        meta = jnp.where(lane == head, high, meta)
        meta = jnp.where(lane == LOW_LANE + head, dot - high, meta)
    meta = meta.astype(BF16)
    for group in range(XN):
        here = slice(group * wide, (group + 1) * wide)
        out[group, :, :wide] = held[0, :, here]
        out[group, :, wide : 2 * wide] = held[2, :, here]
        out[group, :, 2 * wide :] = meta


def pack_queries(query, saved_out, grad_out, frames):
    tok, width = query.shape
    shape = (XN, tok, 2 * GROUP * HDIM + HDIM)
    return pl.pallas_call(
        pack_queries_kernel,
        out_shape=jax.ShapeDtypeStruct(shape, BF16),
        in_specs=[pl.BlockSpec(memory_space=pl.ANY)] * 3 + [vmem()],
        out_specs=vmem(),
        scratch_shapes=[pltpu.VMEM((3, tok, width), BF16), pltpu.SemaphoreType.DMA((3,))],
        compiler_params=params(60),
        cost_estimate=cost(2 * tok * width, 14 * tok * width),
        name="pack_queries",
    )(query, saved_out, grad_out, frames)


def pack_keys_kernel(near, far, out):
    for head in range(HEADS):
        group, h = divmod(head, GROUP)
        cols = slice(head * HDIM, (head + 1) * HDIM)
        for block, ref in enumerate((near, far)):
            for at in range(2):
                first = (2 * (block * GROUP + h) + at) * HDIM
                out[group, :, first : first + HDIM] = ref[at, :, cols]


def pack_keys(near, far):
    _, tok, width = near.shape
    return pl.pallas_call(
        pack_keys_kernel,
        out_shape=jax.ShapeDtypeStruct((XN, tok, 4 * GROUP * HDIM), BF16),
        in_specs=[vmem()] * 2,
        out_specs=vmem(),
        compiler_params=params(),
        cost_estimate=cost(0, 16 * tok * width),
        name="pack_keys",
    )(near, far)


META = slice(2 * GROUP * HDIM, (2 * GROUP + 1) * HDIM)


def head_slice(at):
    return slice(at * HDIM, (at + 1) * HDIM)


def seen(rows, own_meta):
    k_frame = own_meta.astype(F32)[:, FRAME_LANE : FRAME_LANE + 1]
    return k_frame <= rows[FRAME_LANE : FRAME_LANE + 1, :]


def stats_kernel(bias_ref, tokens, own, near, w2, w3, out_ref):
    half = own.shape[0]
    mask = seen(tokens[:, META].astype(F32).T, own[:, META])
    out_ref[...] = jnp.zeros_like(out_ref)
    for head in range(GROUP):
        queries = tokens[:, head_slice(head)].T
        at = head_slice(2 * head)
        keys = [near[:, at], near[:, head_slice(2 * (GROUP + head))], w2[:, at], w3[:, at]]
        scores = jnp.dot(
            jnp.concatenate(keys, axis=0), queries, preferred_element_type=F32
        ) * SCALE2
        parts = [scores[role * half : (role + 1) * half] for role in range(4)]
        parts[0] = jnp.where(mask, parts[0], NEG)
        peaks = [
            jnp.max(part, axis=0, keepdims=True) + bias_ref[role]
            for role, part in enumerate(parts)
        ]
        peak = functools.reduce(jnp.maximum, peaks)
        total = jnp.zeros_like(peak)
        for role, part in enumerate(parts):
            total += jnp.sum(jnp.exp2(part - (peak - bias_ref[role])), axis=0, keepdims=True)
        out_ref[head : head + 1, :] = peak
        out_ref[8 + head : 9 + head, :] = total


def smem():
    return pl.BlockSpec(memory_space=pltpu.SMEM)


def vmem():
    return pl.BlockSpec(memory_space=pltpu.VMEM)


def stats(name, bias, tokens, own, window):
    half = own.shape[0]
    pairs = GROUP * half * 4 * half
    return pl.pallas_call(
        stats_kernel,
        out_shape=jax.ShapeDtypeStruct((16, half), F32),
        in_specs=[smem()] + [vmem()] * 5,
        out_specs=vmem(),
        compiler_params=params(),
        cost_estimate=cost(4 * pairs * HDIM, 5 * half * GROUP * HDIM * 2, pairs),
        name=name,
    )(bias, tokens, own, *window)


def log_total(one, other):
    one_peak, one_sum = one[:8, :], one[8:, :]
    other_peak, other_sum = other[:8, :], other[8:, :]
    peak = jnp.maximum(one_peak, other_peak)
    one_part = one_sum * jnp.exp2(one_peak - peak)
    return peak + jnp.log2(one_part + other_sum * jnp.exp2(other_peak - peak))


def grads_kernel(roles, parts_in, dq_in, bias_ref, place, one, other, tokens, own, *rest):
    count = len(roles)
    sources, rest = rest[: 1 + (2 in roles) * 2], rest[1 + (2 in roles) * 2 :]
    if parts_in:
        parts, rest = rest[:count], rest[count:]
    if dq_in:
        dq_part, *rest = rest
    dq_out, *outs = rest[: 1 + count]
    rows, dq_acc, sums, window, held, k_meta, load_sems, sems, *rest = rest[1 + count :]
    half = rows.shape[1]
    near, *others = sources
    blocks = [near.at[:, : 2 * GROUP * HDIM], near.at[:, 2 * GROUP * HDIM :], *others]

    moves = [(own.at[:, META], k_meta), (tokens, held)]
    moves += [(blocks[role], window.at[at]) for at, role in enumerate(roles)]
    if parts_in:
        moves += [(part, rest[0].at[at]) for at, part in enumerate(parts)]
    if dq_in:
        moves.append((dq_part, rest[1]))
    loads = [
        pltpu.make_async_copy(src, dst, load_sems.at[i]) for i, (src, dst) in enumerate(moves)
    ]
    for load in loads:
        load.start()
    for load in loads:
        load.wait()

    rows[...] = held[:, META].astype(F32).T
    totals = log_total(one, other)
    for head in range(GROUP):
        q_cols = head_slice(head)
        queries, grads = held[:, q_cols], held[:, head_slice(GROUP + head)]
        first = place[0] * GROUP + head
        dot = rows[pl.ds(first, 1), :] + rows[pl.ds(LOW_LANE + first, 1), :]
        keys = window[:, :, head_slice(2 * head)].reshape(count * half, HDIM)
        values = window[:, :, head_slice(2 * head + 1)].reshape(count * half, HDIM)
        scores = jnp.dot(keys, queries.T, preferred_element_type=F32) * SCALE2
        pieces = []
        for at, role in enumerate(roles):
            piece = scores[at * half : (at + 1) * half]
            if role == 0:
                piece = jnp.where(seen(rows, k_meta[...]), piece, NEG)
            pieces.append(jnp.exp2(piece - (totals[head : head + 1] - bias_ref[role])))
        probs = jnp.concatenate(pieces, axis=0)
        dv = jnp.dot(probs.astype(BF16), grads, preferred_element_type=F32)
        dp = jnp.dot(values, grads.T, preferred_element_type=F32)
        ds = (probs * (dp - dot)).astype(BF16)
        dk = jnp.dot(ds, queries, preferred_element_type=F32) * FACTOR
        dq = jnp.dot(keys.T, ds, preferred_element_type=F32)
        for at in range(count):
            of = slice(at * half, (at + 1) * half)
            for cols, value in ((2 * head, dk[of]), (2 * head + 1, dv[of])):
                if parts_in:
                    value += rest[0][at, :, head_slice(cols)].astype(F32)
                sums[at, :, head_slice(cols)] = value.astype(BF16)
        turned = (dq * FACTOR).T
        if dq_in:
            turned += rest[1][:, q_cols]
        dq_acc[:, q_cols] = turned.astype(dq_acc.dtype)
    stores = [pltpu.make_async_copy(dq_acc, dq_out, sems.at[count])]
    for at in range(count):
        stores.append(pltpu.make_async_copy(sums.at[at], outs[at], sems.at[at]))
    for store in stores:
        store.start()
    for store in stores:
        store.wait()


def grads(name, common, tokens, own, roles, sources, dq_kind, parts=(), dq_part=None):
    half = own.shape[0]
    wide = GROUP * HDIM
    count = len(roles)
    pairs = GROUP * half * count * half
    hbm = pl.BlockSpec(memory_space=pl.ANY)
    blocks = pltpu.VMEM((count, half, 2 * wide), BF16)
    extra = list(parts) + ([] if dq_part is None else [dq_part])
    scratch = [
        pltpu.VMEM((HDIM, half), F32),
        pltpu.VMEM((half, wide), dq_kind),
        blocks,
        blocks,
        pltpu.VMEM(tokens.shape, BF16),
        pltpu.VMEM((half, HDIM), BF16),
        pltpu.SemaphoreType.DMA((2 * WBLK + 3,)),
        pltpu.SemaphoreType.DMA((WBLK + 1,)),
    ]
    if parts:
        scratch.append(blocks)
    if dq_part is not None:
        scratch.append(pltpu.VMEM((half, wide), F32))
    return pl.pallas_call(
        functools.partial(grads_kernel, roles, bool(parts), dq_part is not None),
        out_shape=[jax.ShapeDtypeStruct((half, wide), dq_kind)]
        + [jax.ShapeDtypeStruct((half, 2 * wide), BF16)] * count,
        in_specs=[smem(), smem(), vmem(), vmem()] + [hbm] * (2 + len(sources) + len(extra)),
        out_specs=[hbm] * (1 + count),
        scratch_shapes=scratch,
        compiler_params=params(28),
        cost_estimate=cost(10 * pairs * HDIM, 12 * half * wide * 2, pairs),
        name=name,
    )(*common, tokens, own, *sources, *extra)


def row_block(shape):
    return pl.BlockSpec(shape, lambda step: (step, 0))


def fold_kernel(even_ref, d1, swapped, side, out):
    odd = 1.0 - even_ref[0].astype(F32)
    total = d1[...].astype(F32) + swapped[...].astype(F32) + side[...].astype(F32) * odd
    out[...] = total.astype(BF16)


def fold(even, d1, swapped, side):
    block = row_block((d1.shape[0] // 2, d1.shape[1]))
    return pl.pallas_call(
        fold_kernel,
        grid=(2,),
        out_shape=jax.ShapeDtypeStruct(d1.shape, BF16),
        in_specs=[smem()] + [block] * 3,
        out_specs=block,
        compiler_params=params(),
        cost_estimate=cost(3 * d1.size, 8 * d1.size),
        name="fold",
    )(even, d1, swapped, side)


def close_kernel(even_ref, dq_own, dq_back, d0, back, side, out, mine, theirs, pairs, sems):
    even = even_ref[0].astype(F32)
    moves = [(dq_own, mine), (dq_back, theirs)]
    moves += [(src, pairs.at[at]) for at, src in enumerate((d0, back, side))]
    loads = [pltpu.make_async_copy(src, dst, sems.at[i]) for i, (src, dst) in enumerate(moves)]
    for load in loads:
        load.start()
    for load in loads:
        load.wait()
    tok = out.shape[1]
    wide = mine.shape[1]
    for step in range(XN):
        rows = slice(step * tok, (step + 1) * tok)
        pair = pairs[0, rows, :].astype(F32) + pairs[1, rows, :].astype(F32)
        pair += pairs[2, rows, :].astype(F32) * even
        out[step, :, :wide] = (mine[rows, :] + theirs[rows, :].astype(F32)).astype(BF16)
        out[step, :, wide:] = pair.astype(BF16)


def close(even, dq_own, dq_back, d0, back, side):
    half, wide = dq_own.shape
    tok = half // XN
    return pl.pallas_call(
        close_kernel,
        out_shape=jax.ShapeDtypeStruct((XN, tok, 3 * wide), BF16),
        in_specs=[smem()] + [pl.BlockSpec(memory_space=pl.ANY)] * 5,
        out_specs=vmem(),
        scratch_shapes=[
            pltpu.VMEM((half, wide), F32),
            pltpu.VMEM((half, wide), BF16),
            pltpu.VMEM((3, half, 2 * wide), BF16),
            pltpu.SemaphoreType.DMA((5,)),
        ],
        compiler_params=params(),
        cost_estimate=cost(6 * half * wide, 24 * half * wide),
        name="close",
    )(even, dq_own, dq_back, d0, back, side)


def unpack_kernel(parts, dq, dk, dv):
    wide = GROUP * HDIM
    for group in range(XN):
        dq[:, group * wide : (group + 1) * wide] = parts[group, :, :wide]
        for h in range(GROUP):
            at = wide + 2 * h * HDIM
            cols = slice((group * GROUP + h) * HDIM, (group * GROUP + h + 1) * HDIM)
            dk[:, cols] = parts[group, :, at : at + HDIM]
            dv[:, cols] = parts[group, :, at + HDIM : at + 2 * HDIM]


def unpack(parts):
    tok = parts.shape[1]
    return pl.pallas_call(
        unpack_kernel,
        out_shape=[jax.ShapeDtypeStruct((tok, HEADS * HDIM), BF16)] * 3,
        in_specs=[vmem()],
        out_specs=[vmem()] * 3,
        compiler_params=params(),
        cost_estimate=cost(0, 12 * tok * HEADS * HDIM),
        name="unpack",
    )(parts)


def over_x(value):
    groups = [[z * XN + x for x in range(XN)] for z in range(lax.axis_size("col") // XN)]
    return lax.all_to_all(value, "col", 0, 0, axis_index_groups=groups)


def across_z(value):
    count = lax.axis_size("col")
    return lax.ppermute(value, "col", [(c, (c + XN) % count) for c in range(count)])


def along_row(value, steps):
    count = lax.axis_size("row")
    first, last = max(0, -steps), min(count, count - steps)
    return lax.ppermute(value, "row", [(r, r + steps) for r in range(first, last)])


def in_chip(value):
    count = lax.axis_size("row")
    return lax.ppermute(value, "row", [(r, r ^ 1) for r in range(count)])


def own_grads(operands):
    common, own, window, parts, even = operands
    near = window[:1]
    dq_part, d2, d3 = grads("grads_own23", common, own, own, (2, 3), window, F32, parts[2:])
    side, swapped = along_row(d3, -1), in_chip(d2)
    dq_own, d0, d1 = grads(
        "grads_own01", common, own, own, (0, 1), near, F32, parts[:2], dq_part
    )
    return dq_own, d0, along_row(fold(even, d1, swapped, side), -2), side


def no_grads(operands):
    own, window = operands[1:3]
    empty = jnp.zeros_like(window[1])
    return jnp.zeros((own.shape[0], GROUP * HDIM), F32), empty, empty, empty


def per_device(query, key, value, saved_out, grad_out, frame_ids):
    row, col = lax.axis_index("row"), lax.axis_index("col")
    place = jnp.stack([col % XN, col // XN]).astype(jnp.int32)
    is_even = row % 2 == 0
    even = is_even.astype(jnp.int32).reshape(1)
    tok = query.shape[0]
    half = XN * tok
    wide = 2 * GROUP * HDIM

    kv = jnp.stack([key, value])
    kv_far = along_row(kv, 2)
    own = over_x(pack_queries(query, saved_out, grad_out, frame_ids[None, :])).reshape(half, -1)
    far = across_z(own)
    near = over_x(pack_keys(kv, kv_far)).reshape(half, -1)
    w0, w1 = near[:, :wide], near[:, wide:]
    w3 = along_row(jnp.where(is_even, w0, w1), 1)
    w2 = in_chip(w1)
    held = jnp.stack(
        [
            row >= 0,
            row >= 2,
            jnp.where(is_even, row >= 1, row >= 3),
            jnp.where(is_even, row >= 3, row >= 1),
        ]
    )
    bias = jnp.where(held, 0.0, NEG).astype(F32)

    window = (near, w2, w3)
    own_near = stats("stats_own", bias, own, own, window)
    far_other = across_z(own_near)
    far_near = stats("stats_far", bias, far, own, window)
    own_other = across_z(far_near)

    common = (bias, place, far_near, far_other)
    dq_far, *parts = grads("grads_far", common, far, own, (0, 1, 2, 3), window, BF16)
    dq_far, own_other = lax.optimization_barrier((dq_far, own_other))
    dq_back = across_z(dq_far)
    common = (bias, place, own_near, own_other)
    dq_own, d0, back, side = lax.cond(
        row < lax.axis_size("row"), own_grads, no_grads, (common, own, window, parts, even)
    )
    return tuple(unpack(over_x(close(even, dq_own, dq_back, d0, back, side))))


def solution(mesh):
    placed = P(("row", "col"), None)
    return jax.shard_map(
        per_device,
        mesh=mesh,
        in_specs=(placed,) * 5 + (P(("row", "col")),),
        out_specs=(placed,) * 3,
        check_vma=False,
    )
```

```python
import functools
import math

import jax
import jax.numpy as jnp
from jax import lax
from jax.experimental import pallas as pl
from jax.experimental.pallas import tpu as pltpu
from jax.sharding import PartitionSpec as P

HEADS = 20
HDIM = 128
WBLK = 4
XN = 4
GROUP = HEADS // XN
NEG = -1e30
FACTOR = HDIM ** (-0.5)
SCALE2 = FACTOR * math.log2(math.e)
LOW_LANE = 32
FRAME_LANE = 64
BF16 = jnp.bfloat16
F32 = jnp.float32


def params(room=20):
    return pltpu.CompilerParams(vmem_limit_bytes=room * 1024 * 1024)


def cost(flops, moved, exps=0):
    return pl.CostEstimate(flops=flops, bytes_accessed=moved, transcendentals=exps)


def load_all(sources, held, sems):
    copies = [
        pltpu.make_async_copy(src, held.at[at], sems.at[at]) for at, src in enumerate(sources)
    ]
    for copy in copies:
        copy.start()
    for copy in copies:
        copy.wait()


def pack_queries_kernel(q_any, o_any, g_any, f_ref, out, held, sems):
    load_all((q_any, o_any, g_any), held, sems)
    tok = held.shape[1]
    wide = GROUP * HDIM
    lane = lax.broadcasted_iota(jnp.int32, (tok, HDIM), 1)
    here = lax.broadcasted_iota(jnp.int32, (tok, tok), 0)
    same = here == lax.broadcasted_iota(jnp.int32, (tok, tok), 1)
    frame = jnp.sum(jnp.where(same, f_ref[...].astype(F32), 0.0), axis=1, keepdims=True)
    meta = jnp.where(lane == FRAME_LANE, frame, 0.0)
    for head in range(HEADS):
        cols = slice(head * HDIM, (head + 1) * HDIM)
        product = held[2, :, cols].astype(F32) * held[1, :, cols].astype(F32)
        dot = jnp.sum(product, axis=1, keepdims=True)
        high = dot.astype(BF16).astype(F32)
        meta = jnp.where(lane == head, high, meta)
        meta = jnp.where(lane == LOW_LANE + head, dot - high, meta)
    meta = meta.astype(BF16)
    for group in range(XN):
        here = slice(group * wide, (group + 1) * wide)
        out[group, :, :wide] = held[0, :, here]
        out[group, :, wide : 2 * wide] = held[2, :, here]
        out[group, :, 2 * wide :] = meta


def pack_queries(query, saved_out, grad_out, frames):
    tok, width = query.shape
    shape = (XN, tok, 2 * GROUP * HDIM + HDIM)
    return pl.pallas_call(
        pack_queries_kernel,
        out_shape=jax.ShapeDtypeStruct(shape, BF16),
        in_specs=[pl.BlockSpec(memory_space=pl.ANY)] * 3 + [vmem()],
        out_specs=vmem(),
        scratch_shapes=[pltpu.VMEM((3, tok, width), BF16), pltpu.SemaphoreType.DMA((3,))],
        compiler_params=params(60),
        cost_estimate=cost(2 * tok * width, 14 * tok * width),
        name="pack_queries",
    )(query, saved_out, grad_out, frames)


def pack_keys_kernel(near, far, *outs):
    wide = GROUP * HDIM
    for group in range(XN):
        here = slice(group * wide, (group + 1) * wide)
        for at, out in enumerate(outs):
            out[group, :, :wide] = near[at, :, here]
            out[group, :, wide:] = far[at, :, here]


def pack_keys(near, far):
    _, tok, width = near.shape
    return pl.pallas_call(
        pack_keys_kernel,
        out_shape=[jax.ShapeDtypeStruct((XN, tok, 2 * GROUP * HDIM), BF16)] * 2,
        in_specs=[vmem()] * 2,
        out_specs=[vmem()] * 2,
        compiler_params=params(),
        cost_estimate=cost(0, 16 * tok * width),
        name="pack_keys",
    )(near, far)


META = slice(2 * GROUP * HDIM, (2 * GROUP + 1) * HDIM)


def head_slice(at):
    return slice(at * HDIM, (at + 1) * HDIM)


def seen(rows, own_meta):
    k_frame = own_meta.astype(F32)[:, FRAME_LANE : FRAME_LANE + 1]
    return k_frame <= rows[FRAME_LANE : FRAME_LANE + 1, :]


def stats_kernel(bias_ref, tokens, own, near, w2, w3, out_ref):
    half = own.shape[0]
    mask = seen(tokens[:, META].astype(F32).T, own[:, META])
    out_ref[...] = jnp.zeros_like(out_ref)
    for head in range(GROUP):
        queries = tokens[:, head_slice(head)].T
        at = head_slice(head)
        keys = [near[:, at], near[:, head_slice(GROUP + head)], w2[:, at], w3[:, at]]
        scores = jnp.dot(
            jnp.concatenate(keys, axis=0), queries, preferred_element_type=F32
        ) * SCALE2
        parts = [scores[role * half : (role + 1) * half] for role in range(4)]
        parts[0] = jnp.where(mask, parts[0], NEG)
        peaks = [
            jnp.max(part, axis=0, keepdims=True) + bias_ref[role]
            for role, part in enumerate(parts)
        ]
        peak = functools.reduce(jnp.maximum, peaks)
        total = jnp.zeros_like(peak)
        for role, part in enumerate(parts):
            total += jnp.sum(jnp.exp2(part - (peak - bias_ref[role])), axis=0, keepdims=True)
        out_ref[head : head + 1, :] = peak
        out_ref[8 + head : 9 + head, :] = total


def smem():
    return pl.BlockSpec(memory_space=pltpu.SMEM)


def vmem():
    return pl.BlockSpec(memory_space=pltpu.VMEM)


def stats(name, bias, tokens, own, window):
    half = own.shape[0]
    pairs = GROUP * half * 4 * half
    return pl.pallas_call(
        stats_kernel,
        out_shape=jax.ShapeDtypeStruct((16, half), F32),
        in_specs=[smem()] + [vmem()] * 5,
        out_specs=vmem(),
        compiler_params=params(),
        cost_estimate=cost(4 * pairs * HDIM, 5 * half * GROUP * HDIM * 2, pairs),
        name=name,
    )(bias, tokens, own, *window)


def log_total(one, other):
    one_peak, one_sum = one[:8, :], one[8:, :]
    other_peak, other_sum = other[:8, :], other[8:, :]
    peak = jnp.maximum(one_peak, other_peak)
    one_part = one_sum * jnp.exp2(one_peak - peak)
    return peak + jnp.log2(one_part + other_sum * jnp.exp2(other_peak - peak))


def grads_kernel(roles, parts_in, dq_in, bias_ref, place, one, other, tokens, own, *rest):
    count = len(roles)
    given = 6 if 2 in roles else 2
    sources, rest = rest[:given], rest[given:]
    if parts_in:
        parts, rest = rest[:count], rest[count:]
    if dq_in:
        dq_part, *rest = rest
    dq_out, *outs = rest[: 1 + count]
    rows, dq_acc, sums, window, held, k_meta, load_sems, sems, *rest = rest[1 + count :]
    half = rows.shape[1]
    wide = GROUP * HDIM
    blocks = [[near.at[:, :wide] for near in sources[:2]], [near.at[:, wide:] for near in sources[:2]]]
    blocks += [sources[2:4], sources[4:6]]

    moves = [(own.at[:, META], k_meta), (tokens, held)]
    for at, role in enumerate(roles):
        moves.append((blocks[role][0], window.at[at, :, :wide]))
        moves.append((blocks[role][1], window.at[at, :, wide:]))
    if parts_in:
        moves += [(part, rest[0].at[at]) for at, part in enumerate(parts)]
    if dq_in:
        moves.append((dq_part, rest[1]))
    loads = [
        pltpu.make_async_copy(src, dst, load_sems.at[i]) for i, (src, dst) in enumerate(moves)
    ]
    for load in loads:
        load.start()
    for load in loads:
        load.wait()

    rows[...] = held[:, META].astype(F32).T
    totals = log_total(one, other)
    for head in range(GROUP):
        q_cols = head_slice(head)
        queries, grads = held[:, q_cols], held[:, head_slice(GROUP + head)]
        first = place[0] * GROUP + head
        dot = rows[pl.ds(first, 1), :] + rows[pl.ds(LOW_LANE + first, 1), :]
        keys = window[:, :, head_slice(head)].reshape(count * half, HDIM)
        values = window[:, :, head_slice(GROUP + head)].reshape(count * half, HDIM)
        scores = jnp.dot(keys, queries.T, preferred_element_type=F32) * SCALE2
        pieces = []
        for at, role in enumerate(roles):
            piece = scores[at * half : (at + 1) * half]
            if role == 0:
                piece = jnp.where(seen(rows, k_meta[...]), piece, NEG)
            pieces.append(jnp.exp2(piece - (totals[head : head + 1] - bias_ref[role])))
        probs = jnp.concatenate(pieces, axis=0)
        dv = jnp.dot(probs.astype(BF16), grads, preferred_element_type=F32)
        dp = jnp.dot(values, grads.T, preferred_element_type=F32)
        ds = (probs * (dp - dot)).astype(BF16)
        dk = jnp.dot(ds, queries, preferred_element_type=F32) * FACTOR
        dq = jnp.dot(keys.T, ds, preferred_element_type=F32)
        for at in range(count):
            of = slice(at * half, (at + 1) * half)
            for cols, value in ((2 * head, dk[of]), (2 * head + 1, dv[of])):
                if parts_in:
                    value += rest[0][at, :, head_slice(cols)].astype(F32)
                sums[at, :, head_slice(cols)] = value.astype(BF16)
        turned = (dq * FACTOR).T
        if dq_in:
            turned += rest[1][:, q_cols]
        dq_acc[:, q_cols] = turned.astype(dq_acc.dtype)
    stores = [pltpu.make_async_copy(dq_acc, dq_out, sems.at[count])]
    for at in range(count):
        stores.append(pltpu.make_async_copy(sums.at[at], outs[at], sems.at[at]))
    for store in stores:
        store.start()
    for store in stores:
        store.wait()


def grads(name, common, tokens, own, roles, sources, dq_kind, parts=(), dq_part=None):
    half = own.shape[0]
    wide = GROUP * HDIM
    count = len(roles)
    pairs = GROUP * half * count * half
    hbm = pl.BlockSpec(memory_space=pl.ANY)
    blocks = pltpu.VMEM((count, half, 2 * wide), BF16)
    extra = list(parts) + ([] if dq_part is None else [dq_part])
    scratch = [
        pltpu.VMEM((HDIM, half), F32),
        pltpu.VMEM((half, wide), dq_kind),
        blocks,
        blocks,
        pltpu.VMEM(tokens.shape, BF16),
        pltpu.VMEM((half, HDIM), BF16),
        pltpu.SemaphoreType.DMA((3 * WBLK + 3,)),
        pltpu.SemaphoreType.DMA((WBLK + 1,)),
    ]
    if parts:
        scratch.append(blocks)
    if dq_part is not None:
        scratch.append(pltpu.VMEM((half, wide), F32))
    return pl.pallas_call(
        functools.partial(grads_kernel, roles, bool(parts), dq_part is not None),
        out_shape=[jax.ShapeDtypeStruct((half, wide), dq_kind)]
        + [jax.ShapeDtypeStruct((half, 2 * wide), BF16)] * count,
        in_specs=[smem(), smem(), vmem(), vmem()] + [hbm] * (2 + len(sources) + len(extra)),
        out_specs=[hbm] * (1 + count),
        scratch_shapes=scratch,
        compiler_params=params(28),
        cost_estimate=cost(10 * pairs * HDIM, 12 * half * wide * 2, pairs),
        name=name,
    )(*common, tokens, own, *sources, *extra)


def row_block(shape):
    return pl.BlockSpec(shape, lambda step: (step, 0))


def fold_kernel(even_ref, d1, swapped, side, out):
    odd = 1.0 - even_ref[0].astype(F32)
    total = d1[...].astype(F32) + swapped[...].astype(F32) + side[...].astype(F32) * odd
    out[...] = total.astype(BF16)


def fold(even, d1, swapped, side):
    block = row_block((d1.shape[0] // 2, d1.shape[1]))
    return pl.pallas_call(
        fold_kernel,
        grid=(2,),
        out_shape=jax.ShapeDtypeStruct(d1.shape, BF16),
        in_specs=[smem()] + [block] * 3,
        out_specs=block,
        compiler_params=params(),
        cost_estimate=cost(3 * d1.size, 8 * d1.size),
        name="fold",
    )(even, d1, swapped, side)


def close_kernel(even_ref, dq_own, dq_back, d0, back, side, out, mine, theirs, pairs, sems):
    even = even_ref[0].astype(F32)
    moves = [(dq_own, mine), (dq_back, theirs)]
    moves += [(src, pairs.at[at]) for at, src in enumerate((d0, back, side))]
    loads = [pltpu.make_async_copy(src, dst, sems.at[i]) for i, (src, dst) in enumerate(moves)]
    for load in loads:
        load.start()
    for load in loads:
        load.wait()
    tok = out.shape[1]
    wide = mine.shape[1]
    for step in range(XN):
        rows = slice(step * tok, (step + 1) * tok)
        pair = pairs[0, rows, :].astype(F32) + pairs[1, rows, :].astype(F32)
        pair += pairs[2, rows, :].astype(F32) * even
        out[step, :, :wide] = (mine[rows, :] + theirs[rows, :].astype(F32)).astype(BF16)
        out[step, :, wide:] = pair.astype(BF16)


def close(even, dq_own, dq_back, d0, back, side):
    half, wide = dq_own.shape
    tok = half // XN
    return pl.pallas_call(
        close_kernel,
        out_shape=jax.ShapeDtypeStruct((XN, tok, 3 * wide), BF16),
        in_specs=[smem()] + [pl.BlockSpec(memory_space=pl.ANY)] * 5,
        out_specs=vmem(),
        scratch_shapes=[
            pltpu.VMEM((half, wide), F32),
            pltpu.VMEM((half, wide), BF16),
            pltpu.VMEM((3, half, 2 * wide), BF16),
            pltpu.SemaphoreType.DMA((5,)),
        ],
        compiler_params=params(),
        cost_estimate=cost(6 * half * wide, 24 * half * wide),
        name="close",
    )(even, dq_own, dq_back, d0, back, side)


def unpack_kernel(parts, dq, dk, dv):
    wide = GROUP * HDIM
    for group in range(XN):
        dq[:, group * wide : (group + 1) * wide] = parts[group, :, :wide]
        for h in range(GROUP):
            at = wide + 2 * h * HDIM
            cols = slice((group * GROUP + h) * HDIM, (group * GROUP + h + 1) * HDIM)
            dk[:, cols] = parts[group, :, at : at + HDIM]
            dv[:, cols] = parts[group, :, at + HDIM : at + 2 * HDIM]


def unpack(parts):
    tok = parts.shape[1]
    return pl.pallas_call(
        unpack_kernel,
        out_shape=[jax.ShapeDtypeStruct((tok, HEADS * HDIM), BF16)] * 3,
        in_specs=[vmem()],
        out_specs=[vmem()] * 3,
        compiler_params=params(),
        cost_estimate=cost(0, 12 * tok * HEADS * HDIM),
        name="unpack",
    )(parts)


def over_x(value):
    groups = [[z * XN + x for x in range(XN)] for z in range(lax.axis_size("col") // XN)]
    return lax.all_to_all(value, "col", 0, 0, axis_index_groups=groups)


def across_z(value):
    count = lax.axis_size("col")
    return lax.ppermute(value, "col", [(c, (c + XN) % count) for c in range(count)])


def along_row(value, steps):
    count = lax.axis_size("row")
    first, last = max(0, -steps), min(count, count - steps)
    return lax.ppermute(value, "row", [(r, r + steps) for r in range(first, last)])


def in_chip(value):
    count = lax.axis_size("row")
    return lax.ppermute(value, "row", [(r, r ^ 1) for r in range(count)])


def halo(near, is_even):
    wide = GROUP * HDIM
    own, second = near[:, :wide], near[:, wide:]
    third = along_row(jnp.where(is_even, own, second), 1)
    return in_chip(second), third


def own_grads(operands):
    common, own, window, parts, even = operands
    near = window[:2]
    dq_part, d2, d3 = grads("grads_own23", common, own, own, (2, 3), window, F32, parts[2:])
    side, swapped = along_row(d3, -1), in_chip(d2)
    dq_own, d0, d1 = grads(
        "grads_own01", common, own, own, (0, 1), near, F32, parts[:2], dq_part
    )
    return dq_own, d0, along_row(fold(even, d1, swapped, side), -2), side


def no_grads(operands):
    own = operands[1]
    empty = jnp.zeros((own.shape[0], 2 * GROUP * HDIM), BF16)
    return jnp.zeros((own.shape[0], GROUP * HDIM), F32), empty, empty, empty


def per_device(query, key, value, saved_out, grad_out, frame_ids):
    row, col = lax.axis_index("row"), lax.axis_index("col")
    place = jnp.stack([col % XN, col // XN]).astype(jnp.int32)
    is_even = row % 2 == 0
    even = is_even.astype(jnp.int32).reshape(1)
    tok = query.shape[0]
    half = XN * tok

    kv = jnp.stack([key, value])
    kv_far = along_row(kv, 2)
    own = over_x(pack_queries(query, saved_out, grad_out, frame_ids[None, :])).reshape(half, -1)
    far = across_z(own)
    keys, values = pack_keys(kv, kv_far)
    keys = over_x(keys)
    values, keys = lax.optimization_barrier((values, keys))
    keys = keys.reshape(half, -1)
    values = over_x(values).reshape(half, -1)
    k2, k3 = halo(keys, is_even)
    v2, v3 = halo(values, is_even)
    held = jnp.stack(
        [
            row >= 0,
            row >= 2,
            jnp.where(is_even, row >= 1, row >= 3),
            jnp.where(is_even, row >= 3, row >= 1),
        ]
    )
    bias = jnp.where(held, 0.0, NEG).astype(F32)

    own_near = stats("stats_own", bias, own, own, (keys, k2, k3))
    far_other = across_z(own_near)
    far_near = stats("stats_far", bias, far, own, (keys, k2, k3))
    own_other = across_z(far_near)

    window = (keys, values, k2, v2, k3, v3)
    common = (bias, place, far_near, far_other)
    dq_far, *parts = grads("grads_far", common, far, own, (0, 1, 2, 3), window, BF16)
    dq_far, own_other = lax.optimization_barrier((dq_far, own_other))
    dq_back = across_z(dq_far)
    common = (bias, place, own_near, own_other)
    dq_own, d0, back, side = lax.cond(
        row < lax.axis_size("row"), own_grads, no_grads, (common, own, window, parts, even)
    )
    return tuple(unpack(over_x(close(even, dq_own, dq_back, d0, back, side))))


def solution(mesh):
    placed = P(("row", "col"), None)
    return jax.shard_map(
        per_device,
        mesh=mesh,
        in_specs=(placed,) * 5 + (P(("row", "col")),),
        out_specs=(placed,) * 3,
        check_vma=False,
    )
```

```python
import functools
import math

import jax
import jax.numpy as jnp
from jax import lax
from jax.experimental import pallas as pl
from jax.experimental.pallas import tpu as pltpu
from jax.sharding import PartitionSpec as P

HEADS = 20
HDIM = 128
WBLK = 4
XN = 4
GROUP = HEADS // XN
NEG = -1e30
FACTOR = HDIM ** (-0.5)
SCALE2 = FACTOR * math.log2(math.e)
LOW_LANE = 32
FRAME_LANE = 64
BF16 = jnp.bfloat16
F32 = jnp.float32


def params(room=20):
    return pltpu.CompilerParams(vmem_limit_bytes=room * 1024 * 1024)


def cost(flops, moved, exps=0):
    return pl.CostEstimate(flops=flops, bytes_accessed=moved, transcendentals=exps)


def load_all(sources, held, sems):
    copies = [
        pltpu.make_async_copy(src, held.at[at], sems.at[at]) for at, src in enumerate(sources)
    ]
    for copy in copies:
        copy.start()
    for copy in copies:
        copy.wait()


def pack_queries_kernel(q_any, o_any, g_any, f_ref, out, held, sems):
    load_all((q_any, o_any, g_any), held, sems)
    tok = held.shape[1]
    wide = GROUP * HDIM
    lane = lax.broadcasted_iota(jnp.int32, (tok, HDIM), 1)
    here = lax.broadcasted_iota(jnp.int32, (tok, tok), 0)
    same = here == lax.broadcasted_iota(jnp.int32, (tok, tok), 1)
    frame = jnp.sum(jnp.where(same, f_ref[...].astype(F32), 0.0), axis=1, keepdims=True)
    meta = jnp.where(lane == FRAME_LANE, frame, 0.0)
    for head in range(HEADS):
        cols = slice(head * HDIM, (head + 1) * HDIM)
        product = held[2, :, cols].astype(F32) * held[1, :, cols].astype(F32)
        dot = jnp.sum(product, axis=1, keepdims=True)
        high = dot.astype(BF16).astype(F32)
        meta = jnp.where(lane == head, high, meta)
        meta = jnp.where(lane == LOW_LANE + head, dot - high, meta)
    meta = meta.astype(BF16)
    for group in range(XN):
        here = slice(group * wide, (group + 1) * wide)
        out[group, :, :wide] = held[0, :, here]
        out[group, :, wide : 2 * wide] = held[2, :, here]
        out[group, :, 2 * wide :] = meta


def pack_queries(query, saved_out, grad_out, frames):
    tok, width = query.shape
    shape = (XN, tok, 2 * GROUP * HDIM + HDIM)
    return pl.pallas_call(
        pack_queries_kernel,
        out_shape=jax.ShapeDtypeStruct(shape, BF16),
        in_specs=[pl.BlockSpec(memory_space=pl.ANY)] * 3 + [vmem()],
        out_specs=vmem(),
        scratch_shapes=[pltpu.VMEM((3, tok, width), BF16), pltpu.SemaphoreType.DMA((3,))],
        compiler_params=params(60),
        cost_estimate=cost(2 * tok * width, 14 * tok * width),
        name="pack_queries",
    )(query, saved_out, grad_out, frames)


def pack_keys_kernel(near, far, out):
    for head in range(HEADS):
        group, h = divmod(head, GROUP)
        cols = slice(head * HDIM, (head + 1) * HDIM)
        for block, ref in enumerate((near, far)):
            for at in range(2):
                first = (2 * (block * GROUP + h) + at) * HDIM
                out[group, :, first : first + HDIM] = ref[at, :, cols]


def pack_keys(near, far):
    _, tok, width = near.shape
    return pl.pallas_call(
        pack_keys_kernel,
        out_shape=jax.ShapeDtypeStruct((XN, tok, 4 * GROUP * HDIM), BF16),
        in_specs=[vmem()] * 2,
        out_specs=vmem(),
        compiler_params=params(),
        cost_estimate=cost(0, 16 * tok * width),
        name="pack_keys",
    )(near, far)


META = slice(2 * GROUP * HDIM, (2 * GROUP + 1) * HDIM)


def head_slice(at):
    return slice(at * HDIM, (at + 1) * HDIM)


def seen(rows, own_meta):
    k_frame = own_meta.astype(F32)[:, FRAME_LANE : FRAME_LANE + 1]
    return k_frame <= rows[FRAME_LANE : FRAME_LANE + 1, :]


def stats_kernel(bias_ref, tokens, own, near, w2, w3, out_ref):
    half = own.shape[0]
    mask = seen(tokens[:, META].astype(F32).T, own[:, META])
    out_ref[...] = jnp.zeros_like(out_ref)
    for head in range(GROUP):
        queries = tokens[:, head_slice(head)].T
        at = head_slice(2 * head)
        keys = [near[:, at], near[:, head_slice(2 * (GROUP + head))], w2[:, at], w3[:, at]]
        scores = jnp.dot(
            jnp.concatenate(keys, axis=0), queries, preferred_element_type=F32
        ) * SCALE2
        parts = [scores[role * half : (role + 1) * half] for role in range(4)]
        parts[0] = jnp.where(mask, parts[0], NEG)
        peaks = [
            jnp.max(part, axis=0, keepdims=True) + bias_ref[role]
            for role, part in enumerate(parts)
        ]
        peak = functools.reduce(jnp.maximum, peaks)
        total = jnp.zeros_like(peak)
        for role, part in enumerate(parts):
            total += jnp.sum(jnp.exp2(part - (peak - bias_ref[role])), axis=0, keepdims=True)
        out_ref[head : head + 1, :] = peak
        out_ref[8 + head : 9 + head, :] = total


def smem():
    return pl.BlockSpec(memory_space=pltpu.SMEM)


def vmem():
    return pl.BlockSpec(memory_space=pltpu.VMEM)


def stats(name, bias, tokens, own, window):
    half = own.shape[0]
    pairs = GROUP * half * 4 * half
    return pl.pallas_call(
        stats_kernel,
        out_shape=jax.ShapeDtypeStruct((16, half), F32),
        in_specs=[smem()] + [vmem()] * 5,
        out_specs=vmem(),
        compiler_params=params(),
        cost_estimate=cost(4 * pairs * HDIM, 5 * half * GROUP * HDIM * 2, pairs),
        name=name,
    )(bias, tokens, own, *window)


def log_total(one, other):
    one_peak, one_sum = one[:8, :], one[8:, :]
    other_peak, other_sum = other[:8, :], other[8:, :]
    peak = jnp.maximum(one_peak, other_peak)
    one_part = one_sum * jnp.exp2(one_peak - peak)
    return peak + jnp.log2(one_part + other_sum * jnp.exp2(other_peak - peak))


def grads_kernel(roles, parts_in, dq_in, bias_ref, place, one, other, tokens, own, *rest):
    count = len(roles)
    sources, rest = rest[: 1 + (2 in roles) * 2], rest[1 + (2 in roles) * 2 :]
    if parts_in:
        parts, rest = rest[:count], rest[count:]
    if dq_in:
        dq_part, *rest = rest
    dq_out, *outs = rest[: 1 + count]
    rows, dq_acc, sums, window, held, k_meta, load_sems, sems, *rest = rest[1 + count :]
    half = rows.shape[1]
    near, *others = sources
    blocks = [near.at[:, : 2 * GROUP * HDIM], near.at[:, 2 * GROUP * HDIM :], *others]

    moves = [(own.at[:, META], k_meta), (tokens, held)]
    moves += [(blocks[role], window.at[at]) for at, role in enumerate(roles)]
    if parts_in:
        moves += [(part, rest[0].at[at]) for at, part in enumerate(parts)]
    if dq_in:
        moves.append((dq_part, rest[1]))
    loads = [
        pltpu.make_async_copy(src, dst, load_sems.at[i]) for i, (src, dst) in enumerate(moves)
    ]
    for load in loads:
        load.start()
    for load in loads[:2]:
        load.wait()

    rows[...] = held[:, META].astype(F32).T
    totals = log_total(one, other)
    for load in loads[2:]:
        load.wait()

    split = 3

    def leave(part, cols):
        copies = [
            pltpu.make_async_copy(
                sums.at[at, :, cols], outs[at].at[:, cols], sems.at[part, at]
            )
            for at in range(count)
        ]
        for copy in copies:
            copy.start()
        return copies

    for head in range(GROUP):
        q_cols = head_slice(head)
        queries, grads = held[:, q_cols], held[:, head_slice(GROUP + head)]
        first = place[0] * GROUP + head
        dot = rows[pl.ds(first, 1), :] + rows[pl.ds(LOW_LANE + first, 1), :]
        keys = window[:, :, head_slice(2 * head)].reshape(count * half, HDIM)
        values = window[:, :, head_slice(2 * head + 1)].reshape(count * half, HDIM)
        scores = jnp.dot(keys, queries.T, preferred_element_type=F32) * SCALE2
        pieces = []
        for at, role in enumerate(roles):
            piece = scores[at * half : (at + 1) * half]
            if role == 0:
                piece = jnp.where(seen(rows, k_meta[...]), piece, NEG)
            pieces.append(jnp.exp2(piece - (totals[head : head + 1] - bias_ref[role])))
        probs = jnp.concatenate(pieces, axis=0)
        dv = jnp.dot(probs.astype(BF16), grads, preferred_element_type=F32)
        dp = jnp.dot(values, grads.T, preferred_element_type=F32)
        ds = (probs * (dp - dot)).astype(BF16)
        dk = jnp.dot(ds, queries, preferred_element_type=F32) * FACTOR
        dq = jnp.dot(keys.T, ds, preferred_element_type=F32)
        for at in range(count):
            of = slice(at * half, (at + 1) * half)
            for cols, value in ((2 * head, dk[of]), (2 * head + 1, dv[of])):
                if parts_in:
                    value += rest[0][at, :, head_slice(cols)].astype(F32)
                sums[at, :, head_slice(cols)] = value.astype(BF16)
        turned = (dq * FACTOR).T
        if dq_in:
            turned += rest[1][:, q_cols]
        dq_acc[:, q_cols] = turned.astype(dq_acc.dtype)
        if head == split - 1:
            stores = leave(0, slice(0, 2 * split * HDIM))
    stores += leave(1, slice(2 * split * HDIM, 2 * GROUP * HDIM))
    stores.append(pltpu.make_async_copy(dq_acc, dq_out, sems.at[0, count]))
    stores[-1].start()
    for store in stores:
        store.wait()


def grads(name, common, tokens, own, roles, sources, dq_kind, parts=(), dq_part=None):
    half = own.shape[0]
    wide = GROUP * HDIM
    count = len(roles)
    pairs = GROUP * half * count * half
    hbm = pl.BlockSpec(memory_space=pl.ANY)
    blocks = pltpu.VMEM((count, half, 2 * wide), BF16)
    extra = list(parts) + ([] if dq_part is None else [dq_part])
    scratch = [
        pltpu.VMEM((HDIM, half), F32),
        pltpu.VMEM((half, wide), dq_kind),
        blocks,
        blocks,
        pltpu.VMEM(tokens.shape, BF16),
        pltpu.VMEM((half, HDIM), BF16),
        pltpu.SemaphoreType.DMA((2 * WBLK + 3,)),
        pltpu.SemaphoreType.DMA((2, WBLK + 1)),
    ]
    if parts:
        scratch.append(blocks)
    if dq_part is not None:
        scratch.append(pltpu.VMEM((half, wide), F32))
    return pl.pallas_call(
        functools.partial(grads_kernel, roles, bool(parts), dq_part is not None),
        out_shape=[jax.ShapeDtypeStruct((half, wide), dq_kind)]
        + [jax.ShapeDtypeStruct((half, 2 * wide), BF16)] * count,
        in_specs=[smem(), smem(), vmem(), vmem()] + [hbm] * (2 + len(sources) + len(extra)),
        out_specs=[hbm] * (1 + count),
        scratch_shapes=scratch,
        compiler_params=params(28),
        cost_estimate=cost(10 * pairs * HDIM, 12 * half * wide * 2, pairs),
        name=name,
    )(*common, tokens, own, *sources, *extra)


def row_block(shape):
    return pl.BlockSpec(shape, lambda step: (step, 0))


def fold_kernel(even_ref, d1, swapped, side, out):
    odd = 1.0 - even_ref[0].astype(F32)
    total = d1[...].astype(F32) + swapped[...].astype(F32) + side[...].astype(F32) * odd
    out[...] = total.astype(BF16)


def fold(even, d1, swapped, side):
    block = row_block((d1.shape[0] // 2, d1.shape[1]))
    return pl.pallas_call(
        fold_kernel,
        grid=(2,),
        out_shape=jax.ShapeDtypeStruct(d1.shape, BF16),
        in_specs=[smem()] + [block] * 3,
        out_specs=block,
        compiler_params=params(),
        cost_estimate=cost(3 * d1.size, 8 * d1.size),
        name="fold",
    )(even, d1, swapped, side)


def close_kernel(even_ref, dq_own, dq_back, d0, back, side, out, mine, theirs, pairs, sems):
    even = even_ref[0].astype(F32)
    moves = [(dq_own, mine), (dq_back, theirs)]
    moves += [(src, pairs.at[at]) for at, src in enumerate((d0, back, side))]
    loads = [pltpu.make_async_copy(src, dst, sems.at[i]) for i, (src, dst) in enumerate(moves)]
    for load in loads:
        load.start()
    for load in loads:
        load.wait()
    tok = out.shape[1]
    wide = mine.shape[1]
    for step in range(XN):
        rows = slice(step * tok, (step + 1) * tok)
        pair = pairs[0, rows, :].astype(F32) + pairs[1, rows, :].astype(F32)
        pair += pairs[2, rows, :].astype(F32) * even
        out[step, :, :wide] = (mine[rows, :] + theirs[rows, :].astype(F32)).astype(BF16)
        out[step, :, wide:] = pair.astype(BF16)


def close(even, dq_own, dq_back, d0, back, side):
    half, wide = dq_own.shape
    tok = half // XN
    return pl.pallas_call(
        close_kernel,
        out_shape=jax.ShapeDtypeStruct((XN, tok, 3 * wide), BF16),
        in_specs=[smem()] + [pl.BlockSpec(memory_space=pl.ANY)] * 5,
        out_specs=vmem(),
        scratch_shapes=[
            pltpu.VMEM((half, wide), F32),
            pltpu.VMEM((half, wide), BF16),
            pltpu.VMEM((3, half, 2 * wide), BF16),
            pltpu.SemaphoreType.DMA((5,)),
        ],
        compiler_params=params(),
        cost_estimate=cost(6 * half * wide, 24 * half * wide),
        name="close",
    )(even, dq_own, dq_back, d0, back, side)


def unpack_kernel(parts, dq, dk, dv):
    wide = GROUP * HDIM
    for group in range(XN):
        dq[:, group * wide : (group + 1) * wide] = parts[group, :, :wide]
        for h in range(GROUP):
            at = wide + 2 * h * HDIM
            cols = slice((group * GROUP + h) * HDIM, (group * GROUP + h + 1) * HDIM)
            dk[:, cols] = parts[group, :, at : at + HDIM]
            dv[:, cols] = parts[group, :, at + HDIM : at + 2 * HDIM]


def unpack(parts):
    tok = parts.shape[1]
    return pl.pallas_call(
        unpack_kernel,
        out_shape=[jax.ShapeDtypeStruct((tok, HEADS * HDIM), BF16)] * 3,
        in_specs=[vmem()],
        out_specs=[vmem()] * 3,
        compiler_params=params(),
        cost_estimate=cost(0, 12 * tok * HEADS * HDIM),
        name="unpack",
    )(parts)


def over_x(value):
    groups = [[z * XN + x for x in range(XN)] for z in range(lax.axis_size("col") // XN)]
    return lax.all_to_all(value, "col", 0, 0, axis_index_groups=groups)


def across_z(value):
    count = lax.axis_size("col")
    return lax.ppermute(value, "col", [(c, (c + XN) % count) for c in range(count)])


def along_row(value, steps):
    count = lax.axis_size("row")
    first, last = max(0, -steps), min(count, count - steps)
    return lax.ppermute(value, "row", [(r, r + steps) for r in range(first, last)])


def in_chip(value):
    count = lax.axis_size("row")
    return lax.ppermute(value, "row", [(r, r ^ 1) for r in range(count)])


def own_grads(operands):
    common, own, window, parts, even = operands
    near = window[:1]
    dq_part, d2, d3 = grads("grads_own23", common, own, own, (2, 3), window, F32, parts[2:])
    side, swapped = along_row(d3, -1), in_chip(d2)
    dq_own, d0, d1 = grads(
        "grads_own01", common, own, own, (0, 1), near, F32, parts[:2], dq_part
    )
    return dq_own, d0, along_row(fold(even, d1, swapped, side), -2), side


def no_grads(operands):
    own, window = operands[1:3]
    empty = jnp.zeros_like(window[1])
    return jnp.zeros((own.shape[0], GROUP * HDIM), F32), empty, empty, empty


def per_device(query, key, value, saved_out, grad_out, frame_ids):
    row, col = lax.axis_index("row"), lax.axis_index("col")
    place = jnp.stack([col % XN, col // XN]).astype(jnp.int32)
    is_even = row % 2 == 0
    even = is_even.astype(jnp.int32).reshape(1)
    tok = query.shape[0]
    half = XN * tok
    wide = 2 * GROUP * HDIM

    kv = jnp.stack([key, value])
    kv_far = along_row(kv, 2)
    own = over_x(pack_queries(query, saved_out, grad_out, frame_ids[None, :])).reshape(half, -1)
    far = across_z(own)
    near = over_x(pack_keys(kv, kv_far)).reshape(half, -1)
    w0, w1 = near[:, :wide], near[:, wide:]
    w3 = along_row(jnp.where(is_even, w0, w1), 1)
    w2 = in_chip(w1)
    held = jnp.stack(
        [
            row >= 0,
            row >= 2,
            jnp.where(is_even, row >= 1, row >= 3),
            jnp.where(is_even, row >= 3, row >= 1),
        ]
    )
    bias = jnp.where(held, 0.0, NEG).astype(F32)

    window = (near, w2, w3)
    own_near = stats("stats_own", bias, own, own, window)
    far_other = across_z(own_near)
    far_near = stats("stats_far", bias, far, own, window)
    own_other = across_z(far_near)

    common = (bias, place, far_near, far_other)
    dq_far, *parts = grads("grads_far", common, far, own, (0, 1, 2, 3), window, BF16)
    dq_far, own_other = lax.optimization_barrier((dq_far, own_other))
    dq_back = across_z(dq_far)
    common = (bias, place, own_near, own_other)
    dq_own, d0, back, side = lax.cond(
        row < lax.axis_size("row"), own_grads, no_grads, (common, own, window, parts, even)
    )
    return tuple(unpack(over_x(close(even, dq_own, dq_back, d0, back, side))))


def solution(mesh):
    placed = P(("row", "col"), None)
    return jax.shard_map(
        per_device,
        mesh=mesh,
        in_specs=(placed,) * 5 + (P(("row", "col")),),
        out_specs=(placed,) * 3,
        check_vma=False,
    )
```
